128 devices in a mesh: owner: 32 (over z, x, core), rep: 4 (over y).
Axes of the slice: x: 4, y: 4, z: 4, core: 2. Of those that a mesh axis runs over, the one named last changes fastest.
Arguments:
- features: float32 [64, 16, 9, 2048], P('owner')
- frame_counts: int32 [64], replicated, may hold values from 1 to 16, as said below
- video_rows: int32 [64], replicated, may hold values from 0 to 63, as said below
- pair_list: int32 [2048, 2], P('rep'), may hold values from 0 to 63, as said below
- pair_cotangent: float32 [2048], P('rep'), may hold values from -6 to 6
- kernel_one: float32 [3, 3, 1, 32], replicated, may hold values from -2 to 2
- kernel_two: float32 [3, 3, 32, 64], replicated, may hold values from -0.375 to 0.375
- kernel_three: float32 [3, 3, 64, 128], replicated, may hold values from -0.25 to 0.25
- kernel_last: float32 [128], replicated, may hold values from -0.5 to 0.5
Outputs:
- pair_score: float32 [2048], P('rep')
- feature_grad: float32 [64, 16, 9, 2048], P('owner', 'rep')
- grad_one: float32 [3, 3, 1, 32], replicated
- grad_two: float32 [3, 3, 32, 64], replicated
- grad_three: float32 [3, 3, 64, 128], replicated
- grad_last: float32 [128], replicated
The draws below stay inside these ranges and needn't reach their ends.
Inputs may be any that keep to these rules, and one draw needn't show every extreme that they name: `pair_list`: entries are video ids. Pairs stand in blocks of 512, block k on rep index k; in a block, pairs w * 16 to (w + 1) * 16 - 1 go to worker w. The two videos of a pair differ. Video v lives on owner video_rows[v] // 2; among the 32 video ids of one worker's pairs, counted with repetition, no owner holds more than 1, and for every worker some owner holds exactly 1. `video_rows`: A permutation of the rows. `frame_counts`: some video has 16 frames.
All inputs are finite; a program needn't handle non-finite values.
Results may differ from the reference program's by a relative error of at most 0.0058.
Values may be sent and summed in bfloat16 or wider, within the bound.
A program may use at most 192 MiB of HBM per device.

```python
import math
import jax
import jax.numpy as jnp
from jax import lax

D = 2048
REGIONS = 9
C1 = 32
C2 = 64
C3 = 128
MAXLEN = 16
PAIR_DEV = 16
VID_DEV = 2
CAP = 1
VIDEOS = 64
PAIRS = 2048
N_OWNER = 32
N_REP = 4


def pair_tables(key):
    k_row, k_owner = jax.random.split(key, 2)
    video_rows = jax.random.permutation(k_row, VIDEOS).astype(jnp.int32)
    inverse = jnp.argsort(video_rows).astype(jnp.int32)
    workers = N_REP * N_OWNER

    def one_worker(worker_index):
        worker_key = jax.random.fold_in(k_owner, worker_index)
        rounds = [jax.random.permutation(jax.random.fold_in(worker_key, c), N_OWNER) for c in range(CAP)]
        owners = jnp.concatenate(rounds)[:2 * PAIR_DEV]
        owners = jax.random.permutation(jax.random.fold_in(worker_key, CAP + 1), owners).reshape(PAIR_DEV, 2)
        places = jax.random.randint(jax.random.fold_in(worker_key, CAP + 2), (PAIR_DEV, 2), 0, VID_DEV)
        offset = jax.random.randint(jax.random.fold_in(worker_key, CAP + 3), (PAIR_DEV,), 0, VID_DEV - 1)
        collide = (owners[:, 0] == owners[:, 1]) & (places[:, 0] == places[:, 1])
        second = jnp.where(collide, (places[:, 0] + 1 + offset) % VID_DEV, places[:, 1])
        row_ids = owners * VID_DEV + jnp.stack([places[:, 0], second], axis=1)
        return inverse[row_ids]
    per_worker = jax.vmap(one_worker)(jnp.arange(workers))
    return (video_rows, per_worker.reshape(PAIRS, 2).astype(jnp.int32))


def draw_video_rows(key, part):
    shared = pair_tables(key)
    return shared[0]


def draw_pair_list(key, part):
    shared = pair_tables(key)
    return shared[1]


def draw_frame_counts(key, part):
    key = jax.random.fold_in(key, 5)
    k_len, k_long = jax.random.split(key, 2)
    counts = jax.random.randint(k_len, (VIDEOS,), 1, MAXLEN + 1)
    longest = jax.random.randint(k_long, (), 0, VIDEOS)
    return jnp.where(jnp.arange(VIDEOS) == longest, MAXLEN, counts).astype(jnp.int32)


def draw_features(key, part):
    key = jax.random.fold_in(key, 3)
    k_concept, k_pick, k_noise, k_scale = jax.random.split(key, 4)
    concepts = jax.random.normal(k_concept, (16, D), jnp.float32)
    picks = jax.random.randint(k_pick, (VIDEOS, MAXLEN, REGIONS), 0, 16)
    base_vectors = concepts[picks]
    shape = (VIDEOS, MAXLEN, REGIONS, D)
    noise = 0.6 * jax.random.normal(k_noise, shape, jnp.float32)
    scales = jnp.exp(jax.random.uniform(k_scale, (VIDEOS, MAXLEN, REGIONS, 1), jnp.float32, 0.0, math.log(4.0)))
    return (base_vectors + noise) * scales


def steps_of(key, dims, pieces, least, largest):
    def one(axis_at, blocks):
        draws = jax.random.uniform(jax.random.fold_in(jax.random.fold_in(key, 6), axis_at), (blocks,), jnp.float32, least / len(pieces), largest / len(pieces))
        return jnp.repeat(jnp.exp(draws), dims[axis_at] // blocks).reshape((-1,) + (1,) * (len(dims) - axis_at - 1))

    loudness = one(*pieces[0])
    for cut in pieces[1:]:
        loudness = loudness * one(*cut)
    return loudness


def bell_draw(stream_key, shape, deviation, limit, cuts=(), kind=jnp.bfloat16):
    drawn = jax.random.normal(stream_key, shape, jnp.float32) * deviation
    if len(cuts) > 0:
        drawn = steps_of(stream_key, shape, cuts, -0.22, 0.18) * drawn
    return jnp.clip(drawn, min=-limit, max=limit).astype(kind)


def setup_inputs(seed: int = 0) -> dict:
    key_of = jax.random.split(jax.random.key(seed), 10)
    return {
        "features": draw_features(jax.random.fold_in(key_of[9], 71), 0),
        "frame_counts": draw_frame_counts(jax.random.fold_in(key_of[9], 71), 0),
        "video_rows": draw_video_rows(jax.random.fold_in(key_of[9], 71), 0),
        "pair_list": draw_pair_list(jax.random.fold_in(key_of[9], 71), 0),
        "pair_cotangent": bell_draw(key_of[4], (PAIRS,), 1.0, 6.0, ((0, 4),), jnp.float32),
        "kernel_one": bell_draw(key_of[5], (3, 3, 1, C1), 9 ** -0.5, 2.0, (), jnp.float32),
        "kernel_two": bell_draw(key_of[6], (3, 3, C1, C2), (9 * C1) ** -0.5, 0.375, (), jnp.float32),
        "kernel_three": bell_draw(key_of[7], (3, 3, C2, C3), (9 * C2) ** -0.5, 0.25, (), jnp.float32),
        "kernel_last": bell_draw(key_of[8], (C3,), C3 ** -0.5, 0.5, (), jnp.float32),
    }


region_temp = 0.1
frame_temp = 0.1
loss_scale = 131072.0
norm_eps = 1e-06

def normalize_rows(values):
    summed = lax.optimization_barrier(jnp.sum(values * values, axis=-1, keepdims=True)) + norm_eps
    return (values * lax.rsqrt(summed)).astype(jnp.bfloat16)

def pull_back(values, incoming):
    summed = lax.optimization_barrier(jnp.sum(values * values, axis=-1, keepdims=True)) + norm_eps
    inverse = lax.rsqrt(summed)
    along = lax.optimization_barrier(jnp.sum(values * incoming, axis=-1, keepdims=True))
    return incoming * inverse - values * along * inverse * inverse * inverse

def conv_layer(inputs, kernel):
    return lax.conv_general_dilated(inputs, kernel, (1, 1), 'SAME', dimension_numbers=('NHWC', 'HWIO', 'NHWC'), precision=lax.Precision.HIGHEST)

def avg_pool(inputs):
    pair_count, height, breadth, channels = inputs.shape
    return inputs.reshape(pair_count, height // 2, 2, breadth // 2, 2, channels).mean(axis=(2, 4))

def frame_similarity(scores, len_left, len_right, kernels):
    kernel_one, kernel_two, kernel_three, kernel_last = kernels
    pair_count = scores.shape[0]
    frames = scores.shape[1] // REGIONS
    grouped = scores.reshape(pair_count, frames, REGIONS, frames, REGIONS)
    region_best = region_temp * jnp.log(lax.optimization_barrier(jnp.sum(jnp.exp(grouped / region_temp), axis=4)))
    frame_map = lax.optimization_barrier(jnp.mean(region_best, axis=2))
    positions = jnp.arange(frames, dtype=jnp.int32)
    valid_left = positions[None, :] < len_left[:, None]
    valid_right = positions[None, :] < len_right[:, None]
    frame_map = jnp.where(valid_left[:, :, None] & valid_right[:, None, :], frame_map, 0.0)
    hidden = jax.nn.silu(conv_layer(frame_map[..., None], kernel_one))
    hidden = jax.nn.silu(conv_layer(avg_pool(hidden), kernel_two))
    hidden = jax.nn.silu(conv_layer(avg_pool(hidden), kernel_three))
    output = jnp.tanh(jnp.einsum('phwc,c->phw', hidden, kernel_last, precision=lax.Precision.HIGHEST))
    coarse = jnp.arange(frames // 4, dtype=jnp.int32) * 4
    rows_valid = coarse[None, :] < len_left[:, None]
    cols_valid = coarse[None, :] < len_right[:, None]
    weighted = jnp.where(rows_valid[:, :, None] & cols_valid[:, None, :], jnp.exp(output / frame_temp), 0.0)
    row_sums = lax.optimization_barrier(jnp.sum(weighted, axis=2)) + jnp.where(rows_valid, 0.0, 1.0)
    row_best = frame_temp * jnp.log(row_sums)
    kept = lax.optimization_barrier(jnp.sum(jnp.where(rows_valid, row_best, 0.0), axis=1))
    return kept / lax.optimization_barrier(jnp.sum(rows_valid.astype(jnp.float32), axis=1))

def pair_batch(left, right, len_left, len_right, cotangent, kernels):
    scores = jnp.einsum('pxd,pyd->pxy', left.astype(jnp.float32), right.astype(jnp.float32))

    def similarity(values, weights):
        return frame_similarity(values, len_left, len_right, weights)
    sims, pull = jax.vjp(similarity, scores, kernels)
    score_grad, kernel_grads = pull(cotangent * loss_scale)
    score_half = score_grad.astype(jnp.bfloat16).astype(jnp.float32)
    left_grad = jnp.einsum('pxy,pyd->pxd', score_half, right.astype(jnp.float32)).astype(jnp.bfloat16)
    right_grad = jnp.einsum('pxy,pxd->pyd', score_half, left.astype(jnp.float32)).astype(jnp.bfloat16)
    return (sims, left_grad, right_grad, kernel_grads)

def reference(features, frame_counts, video_rows, pair_list, pair_cotangent, kernel_one, kernel_two, kernel_three, kernel_last):
    prepared = normalize_rows(features).reshape(VIDEOS, MAXLEN * REGIONS, D)
    kernels = (kernel_one, kernel_two, kernel_three, kernel_last)
    batches = PAIRS // PAIR_DEV
    left_ids = pair_list[:, 0].reshape(batches, PAIR_DEV)
    right_ids = pair_list[:, 1].reshape(batches, PAIR_DEV)
    cotangents = pair_cotangent.reshape(batches, PAIR_DEV)

    def step(carry, inputs):
        grad_rows, grads = carry
        left_id, right_id, cotangent = inputs
        left_row = video_rows[left_id]
        right_row = video_rows[right_id]
        sims, left_grad, right_grad, kernel_grads = pair_batch(prepared[left_row], prepared[right_row], frame_counts[left_id], frame_counts[right_id], cotangent, kernels)
        grad_rows = grad_rows.at[left_row].add(left_grad.astype(jnp.float32))
        grad_rows = grad_rows.at[right_row].add(right_grad.astype(jnp.float32))
        grads = jax.tree.map(jnp.add, grads, kernel_grads)
        return ((grad_rows, grads), sims)
    start_grads = (jnp.zeros(kernel_one.shape, jnp.float32), jnp.zeros(kernel_two.shape, jnp.float32), jnp.zeros(kernel_three.shape, jnp.float32), jnp.zeros(kernel_last.shape, jnp.float32))
    start_rows = jnp.zeros((VIDEOS, MAXLEN * REGIONS, D), jnp.float32)
    (grad_rows, grads), sims = lax.scan(step, (start_rows, start_grads), (left_ids, right_ids, cotangents))
    feature_grad = pull_back(features, grad_rows.reshape(features.shape))
    return (sims.reshape(PAIRS), feature_grad, grads[0] / loss_scale, grads[1] / loss_scale, grads[2] / loss_scale, grads[3] / loss_scale)
```

```python
import functools

import jax
import jax.numpy as jnp
import numpy as np
from jax import lax
from jax.experimental import pallas as pl
from jax.experimental.pallas import tpu as pltpu
from jax.sharding import PartitionSpec as P

MESH = pl.DeviceIdType.MESH
VMEM_SPEC = pl.BlockSpec(memory_space=pltpu.VMEM)
ANY_SPEC = pl.BlockSpec(memory_space=pl.ANY)
F32 = jnp.float32
BF16 = jnp.bfloat16

REGIONS = 9
FRAMES = 16
WIDTH = 2048
VIDEOS = 64
SIDE = 4
OWN = 2
SEEN = 16
ROWS = OWN * REGIONS * FRAMES
LANES = OWN * SEEN * 16

region_temp = 0.1
loss_scale = 131072.0
norm_eps = 1e-06


def gather_kernel(x_ref, c_ref, pa_ref, pb_ref, call_ref, ssem, rsem, dssem, drsem, csem, crsem, lsem, hs, hr):
    owner = lax.axis_index("owner")
    rep = lax.axis_index("rep")
    z, x, core = owner // 8, (owner // 2) % 4, owner % 2
    chip = owner // 2
    other = owner + 1 - 2 * core

    def shifted(axis, d):
        if axis == 0:
            return z * 8 + ((x + d + 4) % 4) * 2 + core
        return ((z + d + 4) % 4) * 8 + x * 2 + core

    def chip_at(first, du, dv):
        dx, dz = (du, dv) if first == 0 else (dv, du)
        return ((z + dz + 4) % 4) * 4 + (x + dx + 4) % 4

    barrier = pltpu.get_barrier_semaphore()
    for axis in (0, 1):
        for d in (1, -1):
            pl.semaphore_signal(barrier, inc=1, device_id=(shifted(axis, d), rep), device_id_type=MESH)
    pl.semaphore_signal(barrier, inc=1, device_id=(other, rep), device_id_type=MESH)
    for d in (1, 2, 3):
        pl.semaphore_signal(barrier, inc=1, device_id=(owner, (rep + d) % 4), device_id_type=MESH)

    for p in range(OWN):
        values = x_ref[p]
        summed = jnp.sum(values * values, axis=-1, keepdims=True) + norm_eps
        pa_ref[p] = (values * lax.rsqrt(summed)).astype(BF16)

    pl.semaphore_wait(barrier, 8)

    def c_copy(d):
        return pltpu.make_async_remote_copy(
            src_ref=c_ref,
            dst_ref=call_ref.at[rep],
            send_sem=csem.at[d - 1],
            recv_sem=crsem.at[d - 1],
            device_id=(owner, (rep + d) % 4),
            device_id_type=MESH,
        )

    kc, kp = rep // 2, rep % 2
    local = pltpu.make_async_copy(pa_ref.at[kp], pb_ref.at[chip], lsem.at[0])
    halves = []
    for h in range(2):
        lanes = pl.ds(pl.multiple_of(((1 - core) if h == 0 else core) * 1024, 1024), 1024)
        halves.append(
            pltpu.make_async_remote_copy(
                src_ref=pa_ref.at[kp, :, :, lanes],
                dst_ref=pb_ref.at[chip, :, :, lanes],
                send_sem=hs.at[h],
                recv_sem=hr.at[h],
                device_id=(other, rep),
                device_id_type=MESH,
            )
        )

    @pl.when(core == kc)
    def _():
        halves[0].start()
        local.start()
        halves[1].start()
        local.wait()

    @pl.when(core != kc)
    def _():
        halves[0].wait_recv()

    for d in (1, 2, 3):
        c_copy(d).start()
    own_c = pltpu.make_async_copy(c_ref, call_ref.at[rep], lsem.at[1])
    own_c.start()

    def piece(block, m, half):
        if half is None:
            lanes = pl.ds(pl.multiple_of(core * 1024 + m * 512, 512), 512)
        else:
            lanes = pl.ds(pl.multiple_of(core * 1024 + m * 512 + half * 256, 256), 256)
        return pb_ref.at[block, :, :, lanes]

    def ring(m, index, first, du, along):
        base = (m * 5 + index) * 4
        axis = first if along == 0 else 1 - first

        def block(d):
            return chip_at(first, d, 0) if along == 0 else chip_at(first, du, d)

        def copy(slot, source, d, half):
            ref = piece(source, m, half)
            return pltpu.make_async_remote_copy(
                src_ref=ref,
                dst_ref=ref,
                send_sem=ssem.at[base + slot],
                recv_sem=rsem.at[base + slot],
                device_id=(shifted(axis, d), rep),
                device_id_type=MESH,
            )

        return dict(
            send_plus=copy(0, block(0), 1, None),
            send_minus=copy(1, block(0), -1, None),
            fwd_plus=copy(2, block(-1), 1, 0),
            fwd_minus=copy(3, block(1), -1, 1),
            from_minus=copy(0, block(-1), 1, None),
            from_plus=copy(1, block(1), -1, None),
            far_a=copy(2, block(2), 1, 0),
            far_b=copy(3, block(2), -1, 1),
            block=block,
        )

    crossings = []

    def cross(m, block):
        n = len(crossings)
        ref = piece(block, m, None)
        copy = pltpu.make_async_remote_copy(
            src_ref=ref,
            dst_ref=ref,
            send_sem=dssem.at[n],
            recv_sem=drsem.at[n],
            device_id=(other, rep),
            device_id_type=MESH,
        )
        copy.start()
        lanes = pl.ds(pl.multiple_of((1 - core) * 1024 + m * 512, 512), 512)
        theirs = pb_ref.at[block, :, :, lanes]
        arriving = pltpu.make_async_remote_copy(
            src_ref=theirs,
            dst_ref=theirs,
            send_sem=dssem.at[n],
            recv_sem=drsem.at[n],
            device_id=(other, rep),
            device_id_type=MESH,
        )
        crossings.append((copy, arriving))

    offsets = (0, -1, 1, 2)
    ring1 = [ring(m, 0, m, 0, 0) for m in range(2)]
    ring2 = [{du: ring(m, 1 + n, m, du, 1) for n, du in enumerate(offsets)} for m in range(2)]

    def begin(r):
        r["send_plus"].start()
        r["send_minus"].start()

    for m in range(2):
        begin(ring1[m])
    for m in range(2):
        begin(ring2[m][0])
    for d, arrive, forward in ((-1, "from_minus", "fwd_plus"), (1, "from_plus", "fwd_minus")):
        for m in range(2):
            ring1[m][arrive].wait_recv()
            ring1[m][forward].start()
            begin(ring2[m][d])
            cross(m, ring1[m]["block"](d))
    for m in range(2):
        ring1[m]["far_a"].wait_recv()
        ring1[m]["far_b"].wait_recv()
        begin(ring2[m][2])
        cross(m, ring1[m]["block"](2))
    for du in offsets:
        for d, arrive, forward in ((-1, "from_minus", "fwd_plus"), (1, "from_plus", "fwd_minus")):
            for m in range(2):
                r = ring2[m][du]
                r[arrive].wait_recv()
                r[forward].start()
                cross(m, r["block"](d))
    for du in offsets:
        for m in range(2):
            r = ring2[m][du]
            r["far_a"].wait_recv()
            r["far_b"].wait_recv()
            cross(m, r["block"](2))
    for copy, arriving in crossings:
        arriving.wait_recv()
    for copy, arriving in crossings:
        copy.wait_send()
    for m in range(2):
        for r in [ring1[m]] + [ring2[m][du] for du in offsets]:
            for name in ("send_plus", "send_minus", "fwd_plus", "fwd_minus"):
                r[name].wait_send()

    @pl.when(core == kc)
    def _():
        halves[0].wait_send()
        halves[1].wait_send()

    @pl.when(core != kc)
    def _():
        halves[1].wait_recv()

    own_c.wait()
    for d in (1, 2, 3):
        c_copy(d).wait_send()
        pltpu.make_async_remote_copy(
            src_ref=c_ref,
            dst_ref=call_ref.at[(rep + 4 - d) % 4],
            send_sem=csem.at[d - 1],
            recv_sem=crsem.at[d - 1],
            device_id=(owner, (rep + d) % 4),
            device_id_type=MESH,
        ).wait_recv()


def gather(x, c):
    return pl.pallas_call(
        gather_kernel,
        name="gather_videos",
        out_shape=(
            jax.ShapeDtypeStruct((OWN, REGIONS, FRAMES, WIDTH), BF16),
            jax.ShapeDtypeStruct((SEEN, REGIONS, FRAMES, WIDTH), BF16),
            jax.ShapeDtypeStruct((SIDE, VIDEOS, VIDEOS), F32),
        ),
        in_specs=[VMEM_SPEC, VMEM_SPEC],
        out_specs=(VMEM_SPEC, ANY_SPEC, VMEM_SPEC),
        scratch_shapes=[
            pltpu.SemaphoreType.DMA((40,)),
            pltpu.SemaphoreType.DMA((40,)),
            pltpu.SemaphoreType.DMA((30,)),
            pltpu.SemaphoreType.DMA((30,)),
            pltpu.SemaphoreType.DMA((3,)),
            pltpu.SemaphoreType.DMA((3,)),
            pltpu.SemaphoreType.DMA((2,)),
            pltpu.SemaphoreType.DMA((2,)),
            pltpu.SemaphoreType.DMA((2,)),
        ],
        compiler_params=pltpu.CompilerParams(
            collective_id=0, has_side_effects=True, vmem_limit_bytes=40 * 2**20
        ),
    )(x, c)


def split2(v):
    high = v.astype(BF16)
    return high, (v - high.astype(F32)).astype(BF16)


def dot(a, b, ca, cb):
    return lax.dot_general(a, b, (((ca,), (cb,)), ((), ())), preferred_element_type=F32)


def dot3(a, b, ca, cb):
    (ah, al), (bh, bl) = a, b
    return dot(ah, bh, ca, cb) + dot(ah, bl, ca, cb) + dot(al, bh, ca, cb)


def dot_exact(v, chosen):
    high = v.astype(BF16)
    rest = v - high.astype(F32)
    mid = rest.astype(BF16)
    low = (rest - mid.astype(F32)).astype(BF16)
    return dot(high, chosen, 1, 0) + dot(mid, chosen, 1, 0) + dot(low, chosen, 1, 0)


def lane_of(shape):
    return lax.broadcasted_iota(jnp.int32, shape, len(shape) - 1)


def moved(v, di, dj):
    if di == 0 and dj == 0:
        return v
    out = pltpu.roll(v, (-(di * 64 + dj)) % LANES, 1)
    lane = lane_of((1, LANES))
    i4, j4 = (lane // 64) % 4, lane % 4
    ok = (i4 + di >= 0) & (i4 + di < 4) & (j4 + dj >= 0) & (j4 + dj < 4)
    return jnp.where(ok, out, 0.0)


def block_shift(v, du, dv):
    return jnp.concatenate([moved(v[:, :LANES], du, dv), moved(v[:, LANES:], dv, du)], axis=1)


def quad_sum(v, stride):
    lane = lane_of((1, LANES))
    for step in (stride, 2 * stride):
        low = (lane // step) % 2 == 0
        v = v + jnp.where(low, pltpu.roll(v, LANES - step, 1), pltpu.roll(v, step, 1))
    return v


def silu_pair(v):
    s = 1.0 / (1.0 + jnp.exp(-v))
    return v * s, s * (1.0 + v * (1.0 - s))


def core_kernel(
    pa_ref, pb_ref, vecs_ref, va_ref, vb_ref, w1_ref, w2_ref, w3_ref, kl_ref, perm_ref, unperm_ref, rowperm_ref,
    rg_ref, ps_ref, g1_ref, g2_ref, g3_ref, gl_ref,
    e_ref, q1_ref, q2_ref, fm_ref, x0_ref,
):
    pa = pa_ref[...].reshape(ROWS, WIDTH)
    sum1 = jnp.zeros((ROWS, 256), F32)
    fm2 = jnp.zeros((32, 256), F32)
    for s in range(REGIONS):
        pbs = pb_ref[:, s].reshape(SEEN * FRAMES, WIDTH)
        e = jnp.exp(dot(pa, pbs, 1, 1) * (1.0 / region_temp))
        e_ref[s] = e
        sum1 = sum1 + e
        sum2 = jnp.sum(e.reshape(OWN, REGIONS, FRAMES, 256), axis=1).reshape(32, 256)
        q2_ref[s] = sum2
        fm2 = fm2 + jnp.log(sum2)
    q1_ref[...] = sum1
    fm1 = jnp.sum(jnp.log(sum1).reshape(OWN, REGIONS, FRAMES, 256), axis=1).reshape(32, 256)
    valid = va_ref[...] * vb_ref[...]
    scale = region_temp / REGIONS
    fm = jnp.concatenate([jnp.where(valid > 0.0, fm1 * scale, 0.0), jnp.where(valid > 0.0, fm2 * scale, 0.0)], axis=0)
    fm_ref[...] = dot_exact(fm, perm_ref[...])
    for g in range(2):
        for p in range(OWN):
            for i4 in range(4):
                base = g * 32 + p * 16 + i4 * 4
                at = g * LANES + p * 256 + i4 * 64
                for pj in range(4):
                    if g == 0:
                        for pi in range(4):
                            x0_ref[pi * 4 + pj : pi * 4 + pj + 1, at : at + 64] = fm_ref[
                                base + pi : base + pi + 1, pj * 64 : pj * 64 + 64
                            ]
                    else:
                        x0_ref[pj * 4 : pj * 4 + 4, at : at + 64] = fm_ref[base : base + 4, pj * 64 : pj * 64 + 64]

    shifts = [(du, dv) for du in (-1, 0, 1) for dv in (-1, 0, 1)]
    x0 = x0_ref[...]
    xcat = split2(jnp.concatenate([block_shift(x0, du, dv) for du, dv in shifts], axis=0))
    w1 = split2(w1_ref[...])
    h1, ds1 = silu_pair(dot3(w1, xcat, 0, 0))
    pooled1 = []
    for qi in range(2):
        for qj in range(2):
            parts = [
                h1[((2 * qi + a) * 4 + 2 * qj + b) * 32 : ((2 * qi + a) * 4 + 2 * qj + b) * 32 + 32]
                for a in range(2)
                for b in range(2)
            ]
            pooled1.append((parts[0] + parts[1] + parts[2] + parts[3]) * 0.25)
    ext2 = [(1, -1), (0, 0), (1, 0), (0, 1)]
    h1cat = split2(
        jnp.concatenate(
            [block_shift(pooled1[qi * 2 + qj], du, dv) for qi, du in ext2 for qj, dv in ext2], axis=0
        )
    )
    w2 = split2(w2_ref[...])
    h2, ds2 = silu_pair(dot3(w2, h1cat, 0, 0))
    pooled2 = (h2[0:64] + h2[64:128] + h2[128:192] + h2[192:256]) * 0.25
    h2cat = split2(jnp.concatenate([block_shift(pooled2, du, dv) for du, dv in shifts], axis=0))
    w3 = split2(w3_ref[...])
    h3, ds3 = silu_pair(dot3(w3, h2cat, 0, 0))
    kl = kl_ref[...]
    out = jnp.tanh(jnp.sum(h3 * kl, axis=0, keepdims=True))

    dz = []
    for g in range(2):
        o = out[:, g * LANES : (g + 1) * LANES]
        rows_ok = vecs_ref[2 + g : 3 + g, :] > 0.0
        cols_ok = vecs_ref[3 - g : 4 - g, :] > 0.0
        inv = vecs_ref[4 + g : 5 + g, :]
        weighted = jnp.where(rows_ok & cols_ok, jnp.exp(o * (1.0 / region_temp)), 0.0)
        row_sums = quad_sum(weighted, 1 if g == 0 else 64) + jnp.where(rows_ok, 0.0, 1.0)
        if g == 0:
            best = jnp.where(rows_ok, region_temp * jnp.log(row_sums), 0.0)
            ps_ref[...] = quad_sum(best, 64) * inv
        dout = vecs_ref[g : g + 1, :] * inv * weighted / row_sums
        dz.append(dout * (1.0 - o * o))
    dz = jnp.concatenate(dz, axis=1)

    def first(pair):
        return pair[0][:, :LANES], pair[1][:, :LANES]

    gl_ref[...] = jnp.sum(h3[:, :LANES] * dz[:, :LANES], axis=1, keepdims=True)
    dpre3 = split2(dz * kl * ds3)
    g3_ref[...] = dot3(first(h2cat), first(dpre3), 1, 1)
    dh2cat = dot3(w3, dpre3, 1, 0)
    dpool2 = jnp.zeros((64, 2 * LANES), F32)
    for n, (du, dv) in enumerate(shifts):
        dpool2 = dpool2 + block_shift(dh2cat[n * 64 : n * 64 + 64], -du, -dv)
    dpool2 = dpool2 * 0.25
    dpre2 = split2(jnp.concatenate([dpool2, dpool2, dpool2, dpool2], axis=0) * ds2)
    g2 = dot3(first(h1cat), first(dpre2), 1, 1)
    for ti in range(3):
        for tj in range(3):
            total = jnp.zeros((32, 64), F32)
            for pi in range(2):
                for pj in range(2):
                    row = ((pi + ti) * 4 + pj + tj) * 32
                    col = (pi * 2 + pj) * 64
                    total = total + g2[row : row + 32, col : col + 64]
            g2_ref[ti * 3 + tj] = total
    dh1cat = dot3(w2, dpre2, 1, 0)
    dpool1 = [jnp.zeros((32, 2 * LANES), F32) for _ in range(4)]
    n = 0
    for qi, du in ext2:
        for qj, dv in ext2:
            dpool1[qi * 2 + qj] = dpool1[qi * 2 + qj] + block_shift(dh1cat[n * 32 : n * 32 + 32], -du, -dv)
            n += 1
    dpool1 = [d * 0.25 for d in dpool1]
    dpre1 = split2(
        jnp.concatenate([dpool1[(pi // 2) * 2 + pj // 2] for pi in range(4) for pj in range(4)], axis=0) * ds1
    )
    g1_ref[...] = dot3(first(xcat), first(dpre1), 1, 1)
    dxcat = dot3(w1, dpre1, 1, 0)
    dx0 = jnp.zeros((16, 2 * LANES), F32)
    for n, (du, dv) in enumerate(shifts):
        dx0 = dx0 + block_shift(dxcat[n * 16 : n * 16 + 16], -du, -dv)
    x0_ref[...] = dx0
    for g in range(2):
        for p in range(OWN):
            for i4 in range(4):
                base = g * 32 + p * 16 + i4 * 4
                at = g * LANES + p * 256 + i4 * 64
                for pj in range(4):
                    if g == 0:
                        for pi in range(4):
                            fm_ref[base + pi : base + pi + 1, pj * 64 : pj * 64 + 64] = x0_ref[
                                pi * 4 + pj : pi * 4 + pj + 1, at : at + 64
                            ]
                    else:
                        fm_ref[base : base + 4, pj * 64 : pj * 64 + 64] = x0_ref[pj * 4 : pj * 4 + 4, at : at + 64]
    dfm = dot_exact(fm_ref[...], unperm_ref[...])
    dfm1 = jnp.where(valid > 0.0, dfm[:32], 0.0) * (1.0 / REGIONS)
    dfm2 = jnp.where(valid > 0.0, dfm[32:], 0.0) * (1.0 / REGIONS)

    sum1 = q1_ref[...].reshape(OWN, REGIONS, FRAMES, 256)
    q1 = dfm1.reshape(OWN, 1, FRAMES, 256) / sum1
    rowperm = rowperm_ref[...]
    for s in range(REGIONS):
        q2 = (dfm2 / q2_ref[s]).reshape(OWN, 1, FRAMES, 256)
        grad = (e_ref[s].reshape(OWN, REGIONS, FRAMES, 256) * (q1 + q2)).reshape(ROWS, 256).astype(BF16)
        grad = dot(rowperm, grad, 1, 0).astype(BF16)
        pbs = pb_ref[:, s].reshape(SEEN * FRAMES, WIDTH)
        product = dot(grad, pbs, 1, 0)
        if s == 0:
            rg_ref[...] = product
        else:
            rg_ref[...] += product


def perm_tables():
    perm = np.zeros((256, 256), np.float32)
    for b in range(16):
        for j in range(16):
            perm[b * 16 + j, (j % 4) * 64 + b * 4 + j // 4] = 1.0
    rowperm = np.zeros((320, ROWS), np.float32)
    for p in range(OWN):
        for r in range(REGIONS):
            for i in range(FRAMES):
                rowperm[(i // 4) * 80 + p * 36 + r * 4 + i % 4, p * 144 + r * 16 + i] = 1.0
    return perm, perm.T.copy(), rowperm


def core_step(pa, pb, vecs, va, vb, w1, w2, w3, kl):
    perm, unperm, rowperm = (jnp.asarray(t, BF16) for t in perm_tables())
    return pl.pallas_call(
        core_kernel,
        name="scores_and_network",
        out_shape=(
            jax.ShapeDtypeStruct((320, WIDTH), F32),
            jax.ShapeDtypeStruct((1, LANES), F32),
            jax.ShapeDtypeStruct((144, 512), F32),
            jax.ShapeDtypeStruct((9, 32, 64), F32),
            jax.ShapeDtypeStruct((576, 128), F32),
            jax.ShapeDtypeStruct((128, 1), F32),
        ),
        in_specs=[VMEM_SPEC] * 12,
        out_specs=(VMEM_SPEC,) * 6,
        scratch_shapes=[
            pltpu.VMEM((REGIONS, ROWS, 256), F32),
            pltpu.VMEM((ROWS, 256), F32),
            pltpu.VMEM((REGIONS, 32, 256), F32),
            pltpu.VMEM((64, 256), F32),
            pltpu.VMEM((16, 2 * LANES), F32),
        ],
        compiler_params=pltpu.CompilerParams(vmem_limit_bytes=58 * 2**20),
    )(pa, pb, vecs, va, vb, w1, w2, w3, kl, perm, unperm, rowperm)


def scatter_kernel(rg_ref, out_ref, send_ref, recv_ref, ssem, rsem):
    owner = lax.axis_index("owner")
    rep = lax.axis_index("rep")
    barrier = pltpu.get_barrier_semaphore()
    for d in (1, 2, 3):
        pl.semaphore_signal(barrier, inc=1, device_id=(owner, (rep + d) % 4), device_id_type=MESH)
    send_ref[...] = rg_ref[...].astype(BF16)
    pl.semaphore_wait(barrier, 3)

    def copy(d):
        return pltpu.make_async_remote_copy(
            src_ref=send_ref.at[(rep + d) % 4],
            dst_ref=recv_ref.at[d - 1],
            send_sem=ssem.at[d - 1],
            recv_sem=rsem.at[d - 1],
            device_id=(owner, (rep + d) % 4),
            device_id_type=MESH,
        )

    for d in (2, 1, 3):
        copy(d).start()
    total = rg_ref[rep]
    for d in (1, 3, 2):
        copy(d).wait_recv()
        total = total + recv_ref[d - 1].astype(F32)
    out_ref[...] = total
    for d in (1, 2, 3):
        copy(d).wait_send()


def scatter(rg):
    return pl.pallas_call(
        scatter_kernel,
        name="sum_over_rep",
        out_shape=jax.ShapeDtypeStruct((80, WIDTH), F32),
        in_specs=[VMEM_SPEC],
        out_specs=VMEM_SPEC,
        scratch_shapes=[
            pltpu.VMEM((SIDE, 80, WIDTH), BF16),
            pltpu.VMEM((3, 80, WIDTH), BF16),
            pltpu.SemaphoreType.DMA((3,)),
            pltpu.SemaphoreType.DMA((3,)),
        ],
        compiler_params=pltpu.CompilerParams(
            collective_id=1, has_side_effects=True, vmem_limit_bytes=24 * 2**20
        ),
    )(rg)


def weight_tables(kernel_one, kernel_two, kernel_three):
    one = kernel_one.reshape(3, 3, 32)
    cols = []
    for pi in range(4):
        for pj in range(4):
            cols.append(jnp.pad(one, ((pi + 3, 6 - pi), (pj + 3, 6 - pj), (0, 0))))
    w1 = jnp.concatenate(cols, axis=-1)
    w1 = w1.reshape(3, 4, 3, 4, 512).transpose(0, 2, 1, 3, 4).reshape(144, 512)
    cols = []
    for pi in range(2):
        for pj in range(2):
            cols.append(jnp.pad(kernel_two, ((pi, 1 - pi), (pj, 1 - pj), (0, 0), (0, 0))))
    w2 = jnp.concatenate(cols, axis=-1).reshape(512, 256)
    return w1, w2, kernel_three.reshape(576, 128)


def fold_one(g1):
    g1 = g1.reshape(3, 3, 4, 4, 512).transpose(0, 2, 1, 3, 4).reshape(12, 12, 16, 32)
    total = 0.0
    for pi in range(4):
        for pj in range(4):
            total = total + g1[pi + 3 : pi + 6, pj + 3 : pj + 6, pi * 4 + pj]
    return total.reshape(3, 3, 1, 32)


def local(
    features, frame_counts, video_rows, pair_list, pair_cotangent, kernel_one, kernel_two, kernel_three, kernel_last
):
    owner = lax.axis_index("owner")
    rep = lax.axis_index("rep")
    by_region = features.transpose(0, 2, 1, 3)
    ids = jnp.arange(VIDEOS, dtype=jnp.int32)
    hot = (video_rows[:, None] == ids[None, :]).astype(F32)
    exact = functools.partial(jnp.dot, precision=lax.Precision.HIGHEST)
    pick_a = (pair_list[:, 0][:, None] == ids[None, :]).astype(F32)
    pick_b = (pair_list[:, 1][:, None] == ids[None, :]).astype(F32)
    row_a = exact(pick_a, hot)
    row_b = exact(pick_b, hot)
    c_part = exact((row_a * pair_cotangent[:, None]).T, row_b)
    counts = exact(frame_counts.astype(F32)[None, :], hot)[0]

    pa, pb, c_all = gather(by_region, c_part)
    c = jnp.sum(c_all, axis=0) * loss_scale
    mine_a = 2 * owner + jnp.arange(OWN)
    c_ab = lax.dynamic_slice_in_dim(c, 2 * owner, OWN, 0).reshape(OWN, SEEN, SIDE)
    c_ab = lax.dynamic_slice_in_dim(c_ab, rep, 1, 2)[:, :, 0]
    c_ba = lax.dynamic_slice_in_dim(c, 2 * owner, OWN, 1).reshape(SEEN, SIDE, OWN)
    c_ba = lax.dynamic_slice_in_dim(c_ba, rep, 1, 1)[:, 0].T
    len_a = lax.dynamic_slice_in_dim(counts, 2 * owner, OWN, 0)
    len_b = lax.dynamic_slice_in_dim(counts.reshape(SEEN, SIDE), rep, 1, 1)[:, 0]
    coarse = jnp.arange(4, dtype=F32) * 4
    ok_a = (coarse[None, :] < len_a[:, None]).astype(F32)
    ok_b = (coarse[None, :] < len_b[:, None]).astype(F32)
    full = (OWN, 4, SEEN, 4)

    def lanes(v):
        return jnp.broadcast_to(v, full).reshape(LANES)

    vecs = jnp.stack(
        [
            lanes(c_ab[:, None, :, None]),
            lanes(c_ba[:, None, :, None]),
            lanes(ok_a[:, :, None, None]),
            lanes(ok_b[None, None]),
            lanes((1.0 / jnp.sum(ok_a, axis=1))[:, None, None, None]),
            lanes((1.0 / jnp.sum(ok_b, axis=1))[None, None, :, None]),
        ]
        + [jnp.zeros((LANES,), F32)] * 2
    )
    frames = jnp.arange(FRAMES, dtype=F32)
    va = (frames[None, :] < len_a[:, None]).astype(F32).reshape(32, 1)
    vb = (frames[None, :] < len_b[:, None]).astype(F32).reshape(1, 256)
    w1, w2, w3 = weight_tables(kernel_one, kernel_two, kernel_three)
    rg, ps, g1, g2, g3, gl = core_step(pa, pb, vecs, va, vb, w1, w2, w3, kernel_last.reshape(128, 1))

    share = scatter(rg.reshape(SIDE, 80, WIDTH))[:72].reshape(OWN, REGIONS, 4, WIDTH)
    own_slice = lax.dynamic_slice_in_dim(by_region, rep * 4, 4, 2)
    summed = jnp.sum(own_slice * own_slice, axis=-1, keepdims=True) + norm_eps
    inverse = lax.rsqrt(summed)
    along = jnp.sum(own_slice * share, axis=-1, keepdims=True)
    feature_grad = share * inverse - own_slice * along * inverse * inverse * inverse
    feature_grad = feature_grad.transpose(0, 2, 1, 3)

    grads = lax.psum(
        (fold_one(g1), g2.reshape(3, 3, 32, 64), g3.reshape(3, 3, 64, 128), gl.reshape(128)), ("owner", "rep")
    )
    mine = ps.reshape(full)[:, 0, :, 0]
    table = lax.all_gather(mine, ("owner", "rep"))
    table = table.reshape(32, SIDE, OWN, SEEN).transpose(0, 2, 3, 1).reshape(VIDEOS, VIDEOS)
    pair_score = jnp.sum(exact(row_a, table) * row_b, axis=1)
    return (
        pair_score,
        feature_grad,
        grads[0] / loss_scale,
        grads[1] / loss_scale,
        grads[2] / loss_scale,
        grads[3] / loss_scale,
    )


def solution(mesh):
    placed = (P("owner", None, None, None), P(), P(), P("rep", None), P("rep"), P(), P(), P(), P())
    return jax.shard_map(
        local,
        mesh=mesh,
        in_specs=placed,
        out_specs=(P("rep"), P("owner", "rep", None, None), P(), P(), P(), P()),
        check_vma=False,
    )
```

```python
import functools

import jax
import jax.numpy as jnp
import numpy as np
from jax import lax
from jax.experimental import pallas as pl
from jax.experimental.pallas import tpu as pltpu
from jax.sharding import PartitionSpec as P

MESH = pl.DeviceIdType.MESH
VMEM_SPEC = pl.BlockSpec(memory_space=pltpu.VMEM)
F32 = jnp.float32
BF16 = jnp.bfloat16

REGIONS = 9
FRAMES = 16
WIDTH = 2048
VIDEOS = 64
SIDE = 4
OWN = 2
SEEN = 16
ROWS = OWN * REGIONS * FRAMES
LANES = OWN * SEEN * 16

ROW_TWO = 576
ROW_ONE = 720
ROW_PS = 736
ROW_ALL = 768

region_temp = 0.1
loss_scale = 131072.0
norm_eps = 1e-06


def gather_kernel(x_ref, c_ref, pa_ref, pb_ref, call_ref, ssem, rsem, dssem, drsem, csem, crsem, lsem, hs, hr):
    owner = lax.axis_index("owner")
    rep = lax.axis_index("rep")
    z, x, core = owner // 8, (owner // 2) % 4, owner % 2
    chip = owner // 2
    other = owner + 1 - 2 * core

    def shifted(axis, d):
        if axis == 0:
            return z * 8 + ((x + d + 4) % 4) * 2 + core
        return ((z + d + 4) % 4) * 8 + x * 2 + core

    def chip_at(first, du, dv):
        dx, dz = (du, dv) if first == 0 else (dv, du)
        return ((z + dz + 4) % 4) * 4 + (x + dx + 4) % 4

    barrier = pltpu.get_barrier_semaphore()
    for axis in (0, 1):
        for d in (1, -1):
            pl.semaphore_signal(barrier, inc=1, device_id=(shifted(axis, d), rep), device_id_type=MESH)
    pl.semaphore_signal(barrier, inc=1, device_id=(other, rep), device_id_type=MESH)
    for d in (1, 2, 3):
        pl.semaphore_signal(barrier, inc=1, device_id=(owner, (rep + d) % 4), device_id_type=MESH)

    for p in range(OWN):
        values = x_ref[p]
        summed = jnp.sum(values * values, axis=-1, keepdims=True) + norm_eps
        pa_ref[p] = (values * lax.rsqrt(summed)).astype(BF16)

    pl.semaphore_wait(barrier, 8)

    def c_copy(d):
        return pltpu.make_async_remote_copy(
            src_ref=c_ref,
            dst_ref=call_ref.at[rep],
            send_sem=csem.at[d - 1],
            recv_sem=crsem.at[d - 1],
            device_id=(owner, (rep + d) % 4),
            device_id_type=MESH,
        )

    kc, kp = rep // 2, rep % 2
    local = pltpu.make_async_copy(pa_ref.at[kp], pb_ref.at[chip], lsem.at[0])
    halves = []
    for h in range(2):
        lanes = pl.ds(pl.multiple_of(((1 - core) if h == 0 else core) * 1024, 1024), 1024)
        halves.append(
            pltpu.make_async_remote_copy(
                src_ref=pa_ref.at[kp, :, :, lanes],
                dst_ref=pb_ref.at[chip, :, :, lanes],
                send_sem=hs.at[h],
                recv_sem=hr.at[h],
                device_id=(other, rep),
                device_id_type=MESH,
            )
        )

    @pl.when(core == kc)
    def _():
        halves[0].start()
        local.start()
        halves[1].start()
        local.wait()

    @pl.when(core != kc)
    def _():
        halves[0].wait_recv()

    for d in (1, 2, 3):
        c_copy(d).start()
    own_c = pltpu.make_async_copy(c_ref, call_ref.at[rep], lsem.at[1])
    own_c.start()

    def piece(block, m, half):
        if half is None:
            lanes = pl.ds(pl.multiple_of(core * 1024 + m * 512, 512), 512)
        else:
            lanes = pl.ds(pl.multiple_of(core * 1024 + m * 512 + half * 256, 256), 256)
        return pb_ref.at[block, :, :, lanes]

    def ring(m, index, first, du, along):
        base = (m * 5 + index) * 4
        axis = first if along == 0 else 1 - first

        def block(d):
            return chip_at(first, d, 0) if along == 0 else chip_at(first, du, d)

        def copy(slot, source, d, half):
            ref = piece(source, m, half)
            return pltpu.make_async_remote_copy(
                src_ref=ref,
                dst_ref=ref,
                send_sem=ssem.at[base + slot],
                recv_sem=rsem.at[base + slot],
                device_id=(shifted(axis, d), rep),
                device_id_type=MESH,
            )

        return dict(
            send_plus=copy(0, block(0), 1, None),
            send_minus=copy(1, block(0), -1, None),
            fwd_plus=copy(2, block(-1), 1, 0),
            fwd_minus=copy(3, block(1), -1, 1),
            from_minus=copy(0, block(-1), 1, None),
            from_plus=copy(1, block(1), -1, None),
            far_a=copy(2, block(2), 1, 0),
            far_b=copy(3, block(2), -1, 1),
            block=block,
        )

    crossings = []

    def cross(m, block):
        n = len(crossings)
        ref = piece(block, m, None)
        copy = pltpu.make_async_remote_copy(
            src_ref=ref,
            dst_ref=ref,
            send_sem=dssem.at[n],
            recv_sem=drsem.at[n],
            device_id=(other, rep),
            device_id_type=MESH,
        )
        copy.start()
        lanes = pl.ds(pl.multiple_of((1 - core) * 1024 + m * 512, 512), 512)
        theirs = pb_ref.at[block, :, :, lanes]
        arriving = pltpu.make_async_remote_copy(
            src_ref=theirs,
            dst_ref=theirs,
            send_sem=dssem.at[n],
            recv_sem=drsem.at[n],
            device_id=(other, rep),
            device_id_type=MESH,
        )
        crossings.append((copy, arriving))

    offsets = (0, -1, 1, 2)
    ring1 = [ring(m, 0, m, 0, 0) for m in range(2)]
    ring2 = [{du: ring(m, 1 + n, m, du, 1) for n, du in enumerate(offsets)} for m in range(2)]

    def begin(r):
        r["send_plus"].start()
        r["send_minus"].start()

    for m in range(2):
        begin(ring1[m])
    for m in range(2):
        begin(ring2[m][0])
    for d, arrive, forward in ((-1, "from_minus", "fwd_plus"), (1, "from_plus", "fwd_minus")):
        for m in range(2):
            ring1[m][arrive].wait_recv()
            ring1[m][forward].start()
            begin(ring2[m][d])
            cross(m, ring1[m]["block"](d))
    for m in range(2):
        ring1[m]["far_a"].wait_recv()
        ring1[m]["far_b"].wait_recv()
        begin(ring2[m][2])
        cross(m, ring1[m]["block"](2))
    for du in offsets:
        for d, arrive, forward in ((-1, "from_minus", "fwd_plus"), (1, "from_plus", "fwd_minus")):
            for m in range(2):
                r = ring2[m][du]
                r[arrive].wait_recv()
                r[forward].start()
                cross(m, r["block"](d))
    for du in offsets:
        for m in range(2):
            r = ring2[m][du]
            r["far_a"].wait_recv()
            r["far_b"].wait_recv()
            cross(m, r["block"](2))
    for copy, arriving in crossings:
        arriving.wait_recv()
    for copy, arriving in crossings:
        copy.wait_send()
    for m in range(2):
        for r in [ring1[m]] + [ring2[m][du] for du in offsets]:
            for name in ("send_plus", "send_minus", "fwd_plus", "fwd_minus"):
                r[name].wait_send()

    @pl.when(core == kc)
    def _():
        halves[0].wait_send()
        halves[1].wait_send()

    @pl.when(core != kc)
    def _():
        halves[1].wait_recv()

    own_c.wait()
    for d in (1, 2, 3):
        c_copy(d).wait_send()
        pltpu.make_async_remote_copy(
            src_ref=c_ref,
            dst_ref=call_ref.at[(rep + 4 - d) % 4],
            send_sem=csem.at[d - 1],
            recv_sem=crsem.at[d - 1],
            device_id=(owner, (rep + d) % 4),
            device_id_type=MESH,
        ).wait_recv()


def gather(x, c):
    return pl.pallas_call(
        gather_kernel,
        name="gather_videos",
        out_shape=(
            jax.ShapeDtypeStruct((OWN, REGIONS, FRAMES, WIDTH), BF16),
            jax.ShapeDtypeStruct((SEEN, REGIONS, FRAMES, WIDTH), BF16),
            jax.ShapeDtypeStruct((SIDE, VIDEOS, VIDEOS), F32),
        ),
        in_specs=[VMEM_SPEC, VMEM_SPEC],
        out_specs=(VMEM_SPEC, VMEM_SPEC, VMEM_SPEC),
        scratch_shapes=[
            pltpu.SemaphoreType.DMA((40,)),
            pltpu.SemaphoreType.DMA((40,)),
            pltpu.SemaphoreType.DMA((30,)),
            pltpu.SemaphoreType.DMA((30,)),
            pltpu.SemaphoreType.DMA((3,)),
            pltpu.SemaphoreType.DMA((3,)),
            pltpu.SemaphoreType.DMA((2,)),
            pltpu.SemaphoreType.DMA((2,)),
            pltpu.SemaphoreType.DMA((2,)),
        ],
        compiler_params=pltpu.CompilerParams(
            collective_id=0, has_side_effects=True, vmem_limit_bytes=40 * 2**20
        ),
    )(x, c)


def split2(v):
    high = v.astype(BF16)
    return high, (v - high.astype(F32)).astype(BF16)


def dot(a, b, ca, cb):
    return lax.dot_general(a, b, (((ca,), (cb,)), ((), ())), preferred_element_type=F32)


def dot3(a, b, ca, cb):
    (ah, al), (bh, bl) = a, b
    return dot(ah, bh, ca, cb) + dot(ah, bl, ca, cb) + dot(al, bh, ca, cb)


def dot_exact(v, chosen):
    high = v.astype(BF16)
    rest = v - high.astype(F32)
    mid = rest.astype(BF16)
    low = (rest - mid.astype(F32)).astype(BF16)
    return dot(high, chosen, 1, 0) + dot(mid, chosen, 1, 0) + dot(low, chosen, 1, 0)


def lane_of(shape):
    return lax.broadcasted_iota(jnp.int32, shape, len(shape) - 1)


def moved(v, di, dj):
    if di == 0 and dj == 0:
        return v
    out = pltpu.roll(v, (-(di * 64 + dj)) % LANES, 1)
    lane = lane_of((1, LANES))
    i4, j4 = (lane // 64) % 4, lane % 4
    ok = (i4 + di >= 0) & (i4 + di < 4) & (j4 + dj >= 0) & (j4 + dj < 4)
    return jnp.where(ok, out, 0.0)


def block_shift(v, du, dv):
    return jnp.concatenate([moved(v[:, :LANES], du, dv), moved(v[:, LANES:], dv, du)], axis=1)


def quad_sum(v, stride):
    lane = lane_of((1, LANES))
    for step in (stride, 2 * stride):
        low = (lane // step) % 2 == 0
        v = v + jnp.where(low, pltpu.roll(v, LANES - step, 1), pltpu.roll(v, step, 1))
    return v


def silu_pair(v):
    s = 1.0 / (1.0 + jnp.exp(-v))
    return v * s, s * (1.0 + v * (1.0 - s))


def core_kernel(
    pa_ref, pb_ref, vecs_ref, va_ref, vb_ref, w1_ref, w2_ref, w3_ref, kl_ref, perm_ref, unperm_ref, rowperm_ref,
    rg_ref, acc_ref,
    e_ref, q1_ref, q2_ref, fm_ref, x0_ref,
):
    pa = pa_ref[...].reshape(ROWS, WIDTH)
    sum1 = jnp.zeros((ROWS, 256), F32)
    fm2 = jnp.zeros((32, 256), F32)
    for s in range(REGIONS):
        pbs = pb_ref[:, s].reshape(SEEN * FRAMES, WIDTH)
        e = jnp.exp(dot(pa, pbs, 1, 1) * (1.0 / region_temp))
        e_ref[s] = e
        sum1 = sum1 + e
        sum2 = jnp.sum(e.reshape(OWN, REGIONS, FRAMES, 256), axis=1).reshape(32, 256)
        q2_ref[s] = sum2
        fm2 = fm2 + jnp.log(sum2)
    q1_ref[...] = sum1
    fm1 = jnp.sum(jnp.log(sum1).reshape(OWN, REGIONS, FRAMES, 256), axis=1).reshape(32, 256)
    valid = va_ref[...] * vb_ref[...]
    scale = region_temp / REGIONS
    fm = jnp.concatenate([jnp.where(valid > 0.0, fm1 * scale, 0.0), jnp.where(valid > 0.0, fm2 * scale, 0.0)], axis=0)
    fm_ref[...] = dot_exact(fm, perm_ref[...])
    for g in range(2):
        for p in range(OWN):
            for i4 in range(4):
                base = g * 32 + p * 16 + i4 * 4
                at = g * LANES + p * 256 + i4 * 64
                for pj in range(4):
                    if g == 0:
                        for pi in range(4):
                            x0_ref[pi * 4 + pj : pi * 4 + pj + 1, at : at + 64] = fm_ref[
                                base + pi : base + pi + 1, pj * 64 : pj * 64 + 64
                            ]
                    else:
                        x0_ref[pj * 4 : pj * 4 + 4, at : at + 64] = fm_ref[base : base + 4, pj * 64 : pj * 64 + 64]

    shifts = [(du, dv) for du in (-1, 0, 1) for dv in (-1, 0, 1)]
    x0 = x0_ref[...]
    xcat = split2(jnp.concatenate([block_shift(x0, du, dv) for du, dv in shifts], axis=0))
    w1 = split2(w1_ref[...])
    h1, ds1 = silu_pair(dot3(w1, xcat, 0, 0))
    pooled1 = []
    for qi in range(2):
        for qj in range(2):
            parts = [
                h1[((2 * qi + a) * 4 + 2 * qj + b) * 32 : ((2 * qi + a) * 4 + 2 * qj + b) * 32 + 32]
                for a in range(2)
                for b in range(2)
            ]
            pooled1.append((parts[0] + parts[1] + parts[2] + parts[3]) * 0.25)
    ext2 = [(1, -1), (0, 0), (1, 0), (0, 1)]
    h1cat = split2(
        jnp.concatenate(
            [block_shift(pooled1[qi * 2 + qj], du, dv) for qi, du in ext2 for qj, dv in ext2], axis=0
        )
    )
    w2 = split2(w2_ref[...])
    h2, ds2 = silu_pair(dot3(w2, h1cat, 0, 0))
    pooled2 = (h2[0:64] + h2[64:128] + h2[128:192] + h2[192:256]) * 0.25
    h2cat = split2(jnp.concatenate([block_shift(pooled2, du, dv) for du, dv in shifts], axis=0))
    w3 = split2(w3_ref[...])
    h3, ds3 = silu_pair(dot3(w3, h2cat, 0, 0))
    kl = kl_ref[...]
    out = jnp.tanh(jnp.sum(h3 * kl, axis=0, keepdims=True))

    dz = []
    for g in range(2):
        o = out[:, g * LANES : (g + 1) * LANES]
        rows_ok = vecs_ref[2 + g : 3 + g, :] > 0.0
        cols_ok = vecs_ref[3 - g : 4 - g, :] > 0.0
        inv = vecs_ref[4 + g : 5 + g, :]
        weighted = jnp.where(rows_ok & cols_ok, jnp.exp(o * (1.0 / region_temp)), 0.0)
        row_sums = quad_sum(weighted, 1 if g == 0 else 64) + jnp.where(rows_ok, 0.0, 1.0)
        if g == 0:
            best = jnp.where(rows_ok, region_temp * jnp.log(row_sums), 0.0)
            ps = quad_sum(best, 64) * inv
        dout = vecs_ref[g : g + 1, :] * inv * weighted / row_sums
        dz.append(dout * (1.0 - o * o))
    dz = jnp.concatenate(dz, axis=1)

    def first(pair):
        return pair[0][:, :LANES], pair[1][:, :LANES]

    owner = lax.axis_index("owner")
    rep = lax.axis_index("rep")
    lane = lane_of((1, 128))
    row = jnp.where(lane % 4 == rep, jnp.concatenate([ps[:, 0:64], ps[:, 256:320]], axis=1), 0.0)
    at = lax.broadcasted_iota(jnp.int32, (32, 128), 0)
    acc_ref[ROW_PS : ROW_PS + 32] = jnp.where(at == owner, row, 0.0)
    dz_first = jnp.broadcast_to(dz[:, :LANES], (8, LANES))
    gl = dot3(split2(dz_first), split2(h3[:, :LANES]), 1, 1)
    dpre3 = split2(dz * kl * ds3)
    acc_ref[0:576] = dot3(first(h2cat), first(dpre3), 1, 1) * (1.0 / loss_scale)
    dh2cat = dot3(w3, dpre3, 1, 0)
    dpool2 = jnp.zeros((64, 2 * LANES), F32)
    for n, (du, dv) in enumerate(shifts):
        dpool2 = dpool2 + block_shift(dh2cat[n * 64 : n * 64 + 64], -du, -dv)
    dpool2 = dpool2 * 0.25
    dpre2 = split2(jnp.concatenate([dpool2, dpool2, dpool2, dpool2], axis=0) * ds2)
    g2 = dot3(first(h1cat), first(dpre2), 1, 1)
    for ti in range(3):
        for tj in range(3):
            total = jnp.zeros((32, 64), F32)
            for pi in range(2):
                for pj in range(2):
                    row = ((pi + ti) * 4 + pj + tj) * 32
                    col = (pi * 2 + pj) * 64
                    total = total + g2[row : row + 32, col : col + 64]
            total = total * (1.0 / loss_scale)
            for half in range(2):
                n = (ti * 3 + tj) * 2 + half
                at = ROW_TWO + (n % 9) * 16
                acc_ref[at : at + 16, (n // 9) * 64 : (n // 9) * 64 + 64] = total[half * 16 : half * 16 + 16]
    dh1cat = dot3(w2, dpre2, 1, 0)
    dpool1 = [jnp.zeros((32, 2 * LANES), F32) for _ in range(4)]
    n = 0
    for qi, du in ext2:
        for qj, dv in ext2:
            dpool1[qi * 2 + qj] = dpool1[qi * 2 + qj] + block_shift(dh1cat[n * 32 : n * 32 + 32], -du, -dv)
            n += 1
    dpool1 = [d * 0.25 for d in dpool1]
    dpre1 = split2(
        jnp.concatenate([dpool1[(pi // 2) * 2 + pj // 2] for pi in range(4) for pj in range(4)], axis=0) * ds1
    )
    g1 = dot3(first(xcat), first(dpre1), 1, 1)
    plane = lane_of((1, 512)) // 32
    at = lax.broadcasted_iota(jnp.int32, (144, 512), 0)
    rows = []
    for ti in range(3):
        for tj in range(3):
            ei, ej = plane // 4 + ti + 3, plane % 4 + tj + 3
            wanted = ((ei // 4) * 3 + ej // 4) * 16 + (ei % 4) * 4 + ej % 4
            v = jnp.sum(jnp.where(at == wanted, g1, 0.0), axis=0, keepdims=True)
            v = v[:, 0:128] + v[:, 128:256] + v[:, 256:384] + v[:, 384:512]
            v = v + pltpu.roll(v, 64, 1)
            rows.append(v + pltpu.roll(v, 32, 1))
    rows.append(gl[0:1])
    rows.append(jnp.zeros((6, 128), F32))
    acc_ref[ROW_ONE : ROW_ONE + 16] = jnp.concatenate(rows, axis=0) * (1.0 / loss_scale)
    dxcat = dot3(w1, dpre1, 1, 0)
    dx0 = jnp.zeros((16, 2 * LANES), F32)
    for n, (du, dv) in enumerate(shifts):
        dx0 = dx0 + block_shift(dxcat[n * 16 : n * 16 + 16], -du, -dv)
    x0_ref[...] = dx0
    for g in range(2):
        for p in range(OWN):
            for i4 in range(4):
                base = g * 32 + p * 16 + i4 * 4
                at = g * LANES + p * 256 + i4 * 64
                for pj in range(4):
                    if g == 0:
                        for pi in range(4):
                            fm_ref[base + pi : base + pi + 1, pj * 64 : pj * 64 + 64] = x0_ref[
                                pi * 4 + pj : pi * 4 + pj + 1, at : at + 64
                            ]
                    else:
                        fm_ref[base : base + 4, pj * 64 : pj * 64 + 64] = x0_ref[pj * 4 : pj * 4 + 4, at : at + 64]
    dfm = dot_exact(fm_ref[...], unperm_ref[...])
    dfm1 = jnp.where(valid > 0.0, dfm[:32], 0.0) * (1.0 / REGIONS)
    dfm2 = jnp.where(valid > 0.0, dfm[32:], 0.0) * (1.0 / REGIONS)

    sum1 = q1_ref[...].reshape(OWN, REGIONS, FRAMES, 256)
    q1 = dfm1.reshape(OWN, 1, FRAMES, 256) / sum1
    rowperm = rowperm_ref[...]
    for s in range(REGIONS):
        q2 = (dfm2 / q2_ref[s]).reshape(OWN, 1, FRAMES, 256)
        grad = (e_ref[s].reshape(OWN, REGIONS, FRAMES, 256) * (q1 + q2)).reshape(ROWS, 256).astype(BF16)
        grad = dot(rowperm, grad, 1, 0).astype(BF16)
        pbs = pb_ref[:, s].reshape(SEEN * FRAMES, WIDTH)
        product = dot(grad, pbs, 1, 0)
        if s == 0:
            rg_ref[...] = product
        else:
            rg_ref[...] += product


def perm_tables():
    perm = np.zeros((256, 256), np.float32)
    for b in range(16):
        for j in range(16):
            perm[b * 16 + j, (j % 4) * 64 + b * 4 + j // 4] = 1.0
    rowperm = np.zeros((320, ROWS), np.float32)
    for p in range(OWN):
        for r in range(REGIONS):
            for i in range(FRAMES):
                rowperm[(i // 4) * 80 + p * 36 + r * 4 + i % 4, p * 144 + r * 16 + i] = 1.0
    return perm, perm.T.copy(), rowperm


def core_step(pa, pb, vecs, va, vb, w1, w2, w3, kl):
    perm, unperm, rowperm = (jnp.asarray(t, BF16) for t in perm_tables())
    return pl.pallas_call(
        core_kernel,
        name="scores_and_network",
        out_shape=(
            jax.ShapeDtypeStruct((320, WIDTH), F32),
            jax.ShapeDtypeStruct((ROW_ALL, 128), F32),
        ),
        in_specs=[VMEM_SPEC] * 12,
        out_specs=(VMEM_SPEC,) * 2,
        scratch_shapes=[
            pltpu.VMEM((REGIONS, ROWS, 256), F32),
            pltpu.VMEM((ROWS, 256), F32),
            pltpu.VMEM((REGIONS, 32, 256), F32),
            pltpu.VMEM((64, 256), F32),
            pltpu.VMEM((16, 2 * LANES), F32),
        ],
        compiler_params=pltpu.CompilerParams(vmem_limit_bytes=58 * 2**20),
    )(pa, pb, vecs, va, vb, w1, w2, w3, kl, perm, unperm, rowperm)


def sums_kernel(
    rg_ref, acc_ref, out_ref, all_ref, send_ref, recv_ref, part_a, part_b, rs, rr, sa, ra, sb, rb, sc, rc
):
    owner = lax.axis_index("owner")
    rep = lax.axis_index("rep")
    chip, core = owner // 2, owner % 2
    place = core * 4 + rep

    def in_plane(d):
        return (((chip + d) % 16) * 2 + core, rep)

    def in_column(d):
        to = (place + d) % 8
        return (chip * 2 + to // 4, to % 4)

    barrier = pltpu.get_barrier_semaphore()
    for d in range(1, 16):
        pl.semaphore_signal(barrier, inc=1, device_id=in_plane(d), device_id_type=MESH)
    for d in range(1, 8):
        pl.semaphore_signal(barrier, inc=1, device_id=in_column(d), device_id_type=MESH)
    send_ref[...] = rg_ref[...].astype(BF16)
    pl.semaphore_wait(barrier, 22)

    def rep_copy(d):
        return pltpu.make_async_remote_copy(
            src_ref=send_ref.at[(rep + d) % 4],
            dst_ref=recv_ref.at[d - 1],
            send_sem=rs.at[d - 1],
            recv_sem=rr.at[d - 1],
            device_id=(owner, (rep + d) % 4),
            device_id_type=MESH,
        )

    def scatter_copy(d):
        return pltpu.make_async_remote_copy(
            src_ref=acc_ref.at[(chip + d) % 16],
            dst_ref=part_a.at[d - 1],
            send_sem=sa.at[d - 1],
            recv_sem=ra.at[d - 1],
            device_id=in_plane(d),
            device_id_type=MESH,
        )

    def column_copy(d):
        return pltpu.make_async_remote_copy(
            src_ref=part_b.at[place],
            dst_ref=part_b.at[place],
            send_sem=sb.at[d - 1],
            recv_sem=rb.at[d - 1],
            device_id=in_column(d),
            device_id_type=MESH,
        )

    def gather_copy(d, at):
        return pltpu.make_async_remote_copy(
            src_ref=all_ref.at[at],
            dst_ref=all_ref.at[at],
            send_sem=sc.at[d - 1],
            recv_sem=rc.at[d - 1],
            device_id=in_plane(d),
            device_id_type=MESH,
        )

    for d in range(1, 16):
        scatter_copy(d).start()
    for d in (2, 1, 3):
        rep_copy(d).start()
    total = acc_ref[chip]
    for d in range(1, 16):
        scatter_copy(d).wait_recv()
        total = total + part_a[d - 1]
    part_b[place] = total
    for d in range(1, 8):
        column_copy(d).start()
    for d in range(1, 8):
        pltpu.make_async_remote_copy(
            src_ref=part_b.at[(place + 8 - d) % 8],
            dst_ref=part_b.at[(place + 8 - d) % 8],
            send_sem=sb.at[d - 1],
            recv_sem=rb.at[d - 1],
            device_id=in_column(d),
            device_id_type=MESH,
        ).wait_recv()
    total = part_b[0]
    for n in range(1, 8):
        total = total + part_b[n]
    all_ref[chip] = total
    for d in range(1, 16):
        gather_copy(d, chip).start()
    total = rg_ref[rep]
    for d in (1, 3, 2):
        rep_copy(d).wait_recv()
        total = total + recv_ref[d - 1].astype(F32)
    out_ref[...] = total
    for d in range(1, 16):
        gather_copy(d, (chip + 16 - d) % 16).wait_recv()
    for d in (1, 2, 3):
        rep_copy(d).wait_send()
    for d in range(1, 16):
        scatter_copy(d).wait_send()
        gather_copy(d, chip).wait_send()
    for d in range(1, 8):
        column_copy(d).wait_send()


def sums(rg, acc):
    tile = (ROW_ALL // 128, 8, 128)
    return pl.pallas_call(
        sums_kernel,
        name="sums_over_devices",
        out_shape=(
            jax.ShapeDtypeStruct((80, WIDTH), F32),
            jax.ShapeDtypeStruct((16,) + tile, F32),
        ),
        in_specs=[VMEM_SPEC] * 2,
        out_specs=(VMEM_SPEC,) * 2,
        scratch_shapes=[
            pltpu.VMEM((SIDE, 80, WIDTH), BF16),
            pltpu.VMEM((3, 80, WIDTH), BF16),
            pltpu.VMEM((15,) + tile, F32),
            pltpu.VMEM((8,) + tile, F32),
        ]
        + [pltpu.SemaphoreType.DMA((n,)) for n in (3, 3, 15, 15, 7, 7, 15, 15)],
        compiler_params=pltpu.CompilerParams(
            collective_id=1, has_side_effects=True, vmem_limit_bytes=24 * 2**20
        ),
    )(rg, acc.reshape((16,) + tile))


def weight_tables(kernel_one, kernel_two, kernel_three):
    one = kernel_one.reshape(3, 3, 32)
    cols = []
    for pi in range(4):
        for pj in range(4):
            cols.append(jnp.pad(one, ((pi + 3, 6 - pi), (pj + 3, 6 - pj), (0, 0))))
    w1 = jnp.concatenate(cols, axis=-1)
    w1 = w1.reshape(3, 4, 3, 4, 512).transpose(0, 2, 1, 3, 4).reshape(144, 512)
    cols = []
    for pi in range(2):
        for pj in range(2):
            cols.append(jnp.pad(kernel_two, ((pi, 1 - pi), (pj, 1 - pj), (0, 0), (0, 0))))
    w2 = jnp.concatenate(cols, axis=-1).reshape(512, 256)
    return w1, w2, kernel_three.reshape(576, 128)


def local(
    features, frame_counts, video_rows, pair_list, pair_cotangent, kernel_one, kernel_two, kernel_three, kernel_last
):
    owner = lax.axis_index("owner")
    rep = lax.axis_index("rep")
    by_region = features.transpose(0, 2, 1, 3)
    ids = jnp.arange(VIDEOS, dtype=jnp.int32)
    hot = (video_rows[:, None] == ids[None, :]).astype(F32)
    exact = functools.partial(jnp.dot, precision=lax.Precision.HIGHEST)
    pick_a = (pair_list[:, 0][:, None] == ids[None, :]).astype(F32)
    pick_b = (pair_list[:, 1][:, None] == ids[None, :]).astype(F32)
    row_a = exact(pick_a, hot)
    row_b = exact(pick_b, hot)
    c_part = exact((row_a * pair_cotangent[:, None]).T, row_b)
    counts = exact(frame_counts.astype(F32)[None, :], hot)[0]

    pa, pb, c_all = gather(by_region, c_part)
    c = jnp.sum(c_all, axis=0) * loss_scale
    c_ab = lax.dynamic_slice_in_dim(c, 2 * owner, OWN, 0).reshape(OWN, SEEN, SIDE)
    c_ab = lax.dynamic_slice_in_dim(c_ab, rep, 1, 2)[:, :, 0]
    c_ba = lax.dynamic_slice_in_dim(c, 2 * owner, OWN, 1).reshape(SEEN, SIDE, OWN)
    c_ba = lax.dynamic_slice_in_dim(c_ba, rep, 1, 1)[:, 0].T
    len_a = lax.dynamic_slice_in_dim(counts, 2 * owner, OWN, 0)
    len_b = lax.dynamic_slice_in_dim(counts.reshape(SEEN, SIDE), rep, 1, 1)[:, 0]
    coarse = jnp.arange(4, dtype=F32) * 4
    ok_a = (coarse[None, :] < len_a[:, None]).astype(F32)
    ok_b = (coarse[None, :] < len_b[:, None]).astype(F32)
    full = (OWN, 4, SEEN, 4)

    def lanes(v):
        return jnp.broadcast_to(v, full).reshape(LANES)

    vecs = jnp.stack(
        [
            lanes(c_ab[:, None, :, None]),
            lanes(c_ba[:, None, :, None]),
            lanes(ok_a[:, :, None, None]),
            lanes(ok_b[None, None]),
            lanes((1.0 / jnp.sum(ok_a, axis=1))[:, None, None, None]),
            lanes((1.0 / jnp.sum(ok_b, axis=1))[None, None, :, None]),
        ]
        + [jnp.zeros((LANES,), F32)] * 2
    )
    frames = jnp.arange(FRAMES, dtype=F32)
    va = (frames[None, :] < len_a[:, None]).astype(F32).reshape(32, 1)
    vb = (frames[None, :] < len_b[:, None]).astype(F32).reshape(1, 256)
    w1, w2, w3 = weight_tables(kernel_one, kernel_two, kernel_three)
    rg, acc = core_step(pa, pb, vecs, va, vb, w1, w2, w3, kernel_last.reshape(128, 1))

    share, acc = sums(rg.reshape(SIDE, 80, WIDTH), acc)
    share = share[:72].reshape(OWN, REGIONS, 4, WIDTH)
    acc = acc.reshape(ROW_ALL, 128)
    own_slice = lax.dynamic_slice_in_dim(by_region, rep * 4, 4, 2)
    summed = jnp.sum(own_slice * own_slice, axis=-1, keepdims=True) + norm_eps
    inverse = lax.rsqrt(summed)
    along = jnp.sum(own_slice * share, axis=-1, keepdims=True)
    feature_grad = share * inverse - own_slice * along * inverse * inverse * inverse
    feature_grad = feature_grad.transpose(0, 2, 1, 3)

    table = acc[ROW_PS:ROW_ALL].reshape(VIDEOS, VIDEOS)
    pair_score = jnp.sum(exact(row_a, table) * row_b, axis=1)
    two = acc[ROW_TWO:ROW_ONE]
    return (
        pair_score,
        feature_grad,
        acc[ROW_ONE : ROW_ONE + 9, :32].reshape(3, 3, 1, 32),
        jnp.concatenate([two[:, :64], two[:, 64:]], axis=0).reshape(3, 3, 32, 64),
        acc[:ROW_TWO].reshape(3, 3, 64, 128),
        acc[ROW_ONE + 9],
    )


def solution(mesh):
    placed = (P("owner", None, None, None), P(), P(), P("rep", None), P("rep"), P(), P(), P(), P())
    return jax.shard_map(
        local,
        mesh=mesh,
        in_specs=placed,
        out_specs=(P("rep"), P("owner", "rep", None, None), P(), P(), P(), P()),
        check_vma=False,
    )
```

```python
import jax
import jax.numpy as jnp
from jax import lax
from jax.experimental import pallas as pl
from jax.experimental.pallas import tpu as pltpu
from jax.sharding import PartitionSpec as P

MESH = pl.DeviceIdType.MESH
VMEM_SPEC = pl.BlockSpec(memory_space=pltpu.VMEM)
F32 = jnp.float32
BF16 = jnp.bfloat16

REGIONS = 9
FRAMES = 16
WIDTH = 2048
VIDEOS = 64
SIDE = 4
OWN = 2
SEEN = 16
ROWS = OWN * REGIONS * FRAMES
LANES = OWN * SEEN * 16

ROW_TWO = 576
ROW_ONE = 720
ROW_PS = 736
ROW_ALL = 768

region_temp = 0.1
loss_scale = 131072.0
norm_eps = 1e-06
C3 = 128


CHUNKS = 4
CHUNK = WIDTH // CHUNKS


def split2(v):
    high = v.astype(BF16)
    return high, (v - high.astype(F32)).astype(BF16)


def dot(a, b, ca, cb):
    return lax.dot_general(a, b, (((ca,), (cb,)), ((), ())), preferred_element_type=F32)


def dot3(a, b, ca, cb):
    (ah, al), (bh, bl) = a, b
    return dot(ah, bh, ca, cb) + dot(ah, bl, ca, cb) + dot(al, bh, ca, cb)


def dot_exact(v, chosen, cb=0):
    high = v.astype(BF16)
    rest = v - high.astype(F32)
    mid = rest.astype(BF16)
    low = (rest - mid.astype(F32)).astype(BF16)
    return dot(high, chosen, 1, cb) + dot(mid, chosen, 1, cb) + dot(low, chosen, 1, cb)


def lane_of(shape):
    return lax.broadcasted_iota(jnp.int32, shape, len(shape) - 1)


def moved(v, di, dj):
    if di == 0 and dj == 0:
        return v
    out = pltpu.roll(v, (-(di * 64 + dj)) % LANES, 1)
    lane = lane_of((1, LANES))
    i4, j4 = (lane // 64) % 4, lane % 4
    ok = (i4 + di >= 0) & (i4 + di < 4) & (j4 + dj >= 0) & (j4 + dj < 4)
    return jnp.where(ok, out, 0.0)


def block_shift(v, du, dv):
    return jnp.concatenate([moved(v[:, :LANES], du, dv), moved(v[:, LANES:], dv, du)], axis=1)


def quad_sum(v, stride):
    lane = lane_of((1, LANES))
    for step in (stride, 2 * stride):
        low = (lane // step) % 2 == 0
        v = v + jnp.where(low, pltpu.roll(v, LANES - step, 1), pltpu.roll(v, step, 1))
    return v


def silu_pair(v):
    s = 1.0 / (1.0 + jnp.exp(-v))
    return v * s, s * (1.0 + v * (1.0 - s))


def iota(shape, axis):
    return lax.broadcasted_iota(jnp.int32, shape, axis)


def ones_where(condition):
    return jnp.where(condition, 1.0, 0.0).astype(BF16)


def tap_rows(ti, tj):
    plane = lane_of((1, 512)) // 32
    ei, ej = plane // 4 + ti + 3, plane % 4 + tj + 3
    return ((ei // 4) * 3 + ej // 4) * 16 + (ei % 4) * 4 + ej % 4


SHIFTS = [(du, dv) for du in (-1, 0, 1) for dv in (-1, 0, 1)]
EXT2 = [(1, -1), (0, 0), (1, 0), (0, 1)]


def whole_kernel(
    x_ref, counts_ref, vrows_ref, pairs_ref, cot_ref, k1_ref, k2_ref, k3_ref, kl_ref,
    fg_ref, ps_ref, g1_ref, g2_ref, g3_ref, gl_ref,
    pa_ref, pb_ref, call_ref, hots_ref, w1_ref, w2_ref, own_ref,
    e_ref, q1_ref, q2_ref, fm_ref, x0_ref, grad_ref, acc_ref, rg_ref, send_ref, recv_ref, part_a, part_b, all_ref,
    ssem, rsem, dssem, drsem, csem, crsem, lsem, hs, hr, rs, rr, sa, ra, sb, rb, sc, rc,
):
    owner = lax.axis_index("owner")
    rep = lax.axis_index("rep")
    z, x, core = owner // 8, (owner // 2) % 4, owner % 2
    chip = owner // 2
    place = core * 4 + rep
    other = owner + 1 - 2 * core

    def in_plane(d):
        return (((chip + d) % 16) * 2 + core, rep)

    def in_column(d):
        to = (place + d) % 8
        return (chip * 2 + to // 4, to % 4)

    def shifted(axis, d):
        if axis == 0:
            return z * 8 + ((x + d + 4) % 4) * 2 + core
        return ((z + d + 4) % 4) * 8 + x * 2 + core

    def chip_at(first, du, dv):
        dx, dz = (du, dv) if first == 0 else (dv, du)
        return ((z + dz + 4) % 4) * 4 + (x + dx + 4) % 4

    barrier = pltpu.get_barrier_semaphore()
    for d in range(1, 16):
        pl.semaphore_signal(barrier, inc=1, device_id=in_plane(d), device_id_type=MESH)
    for d in range(1, 8):
        pl.semaphore_signal(barrier, inc=1, device_id=in_column(d), device_id_type=MESH)

    for p in range(OWN):
        values = x_ref[p]
        summed = jnp.sum(values * values, axis=-1, keepdims=True) + norm_eps
        pa_ref[p] = (values * lax.rsqrt(summed)).astype(BF16)

    pl.semaphore_wait(barrier, 22)

    kc, kp = rep // 2, rep % 2
    local = pltpu.make_async_copy(pa_ref.at[kp], pb_ref.at[chip], lsem.at[0])
    halves = []
    for h in range(2):
        lanes = pl.ds(pl.multiple_of(((1 - core) if h == 0 else core) * 1024, 1024), 1024)
        halves.append(
            pltpu.make_async_remote_copy(
                src_ref=pa_ref.at[kp, :, :, lanes],
                dst_ref=pb_ref.at[chip, :, :, lanes],
                send_sem=hs.at[h],
                recv_sem=hr.at[h],
                device_id=(other, rep),
                device_id_type=MESH,
            )
        )

    @pl.when(core == kc)
    def _():
        halves[0].start()
        local.start()
        halves[1].start()
        local.wait()

    @pl.when(core != kc)
    def _():
        halves[0].wait_recv()

    def piece(block, m, half):
        if half is None:
            lanes = pl.ds(pl.multiple_of(core * 1024 + m * 512, 512), 512)
        else:
            lanes = pl.ds(pl.multiple_of(core * 1024 + m * 512 + half * 256, 256), 256)
        return pb_ref.at[block, :, :, lanes]

    def ring(m, index, first, du, along):
        base = (m * 5 + index) * 4
        axis = first if along == 0 else 1 - first

        def block(d):
            return chip_at(first, d, 0) if along == 0 else chip_at(first, du, d)

        def copy(slot, source, d, half):
            ref = piece(source, m, half)
            return pltpu.make_async_remote_copy(
                src_ref=ref,
                dst_ref=ref,
                send_sem=ssem.at[base + slot],
                recv_sem=rsem.at[base + slot],
                device_id=(shifted(axis, d), rep),
                device_id_type=MESH,
            )

        return dict(
            send_plus=copy(0, block(0), 1, None),
            send_minus=copy(1, block(0), -1, None),
            fwd_plus=copy(2, block(-1), 1, 0),
            fwd_minus=copy(3, block(1), -1, 1),
            from_minus=copy(0, block(-1), 1, None),
            from_plus=copy(1, block(1), -1, None),
            far_a=copy(2, block(2), 1, 0),
            far_b=copy(3, block(2), -1, 1),
            block=block,
        )

    crossings = []

    def cross(m, block):
        n = len(crossings)
        ref = piece(block, m, None)
        copy = pltpu.make_async_remote_copy(
            src_ref=ref,
            dst_ref=ref,
            send_sem=dssem.at[n],
            recv_sem=drsem.at[n],
            device_id=(other, rep),
            device_id_type=MESH,
        )
        copy.start()
        lanes = pl.ds(pl.multiple_of((1 - core) * 1024 + m * 512, 512), 512)
        theirs = pb_ref.at[block, :, :, lanes]
        arriving = pltpu.make_async_remote_copy(
            src_ref=theirs,
            dst_ref=theirs,
            send_sem=dssem.at[n],
            recv_sem=drsem.at[n],
            device_id=(other, rep),
            device_id_type=MESH,
        )
        crossings.append((copy, arriving))

    def c_copy(d, at):
        return pltpu.make_async_remote_copy(
            src_ref=call_ref.at[at],
            dst_ref=call_ref.at[at],
            send_sem=csem.at[d - 1],
            recv_sem=crsem.at[d - 1],
            device_id=(owner, (rep + d) % 4),
            device_id_type=MESH,
        )

    def make_pairs():
        by_row = ones_where(iota((VIDEOS, VIDEOS), 0) == vrows_ref[...])
        videos = iota((VIDEOS, 512), 0)
        row_a = dot(by_row, ones_where(videos == pairs_ref[0:1, :]), 1, 0)
        row_b = dot(by_row, ones_where(videos == pairs_ref[1:2, :]), 1, 0)
        hots_ref[0] = row_a.astype(BF16)
        hots_ref[1] = row_b.astype(BF16)
        call_ref[rep] = dot_exact(row_a * cot_ref[...], row_b.astype(BF16), 1)
        for d in (1, 2, 3):
            c_copy(d, rep).start()

    def make_weights():
        tiled = dot_exact(k1_ref[...], ones_where(iota((32, 512), 1) % 32 == iota((32, 512), 0)))
        at = iota((144, 512), 0)
        w1 = jnp.zeros((144, 512), F32)
        for ti in range(3):
            for tj in range(3):
                w1 = jnp.where(at == tap_rows(ti, tj), tiled[ti * 3 + tj : ti * 3 + tj + 1], w1)
        w1_ref[...] = w1
        w2_ref[...] = jnp.zeros((512, 256), F32)
        for ti in range(3):
            for tj in range(3):
                for pi in range(2):
                    for pj in range(2):
                        row = ((pi + ti) * 4 + pj + tj) * 32
                        col = (pi * 2 + pj) * 64
                        w2_ref[row : row + 32, col : col + 64] = k2_ref[ti * 3 + tj]

    def frame_rows(shape):
        n = lane_of(shape)
        return ((n % 16) // 4) * 80 + (n // 144) * 36 + ((n % 144) // 16) * 4 + n % 4

    def make_own():
        chosen = ones_where(frame_rows((1, ROWS)) - rep * 80 == iota((80, ROWS), 0))
        for n in range(4):
            v = x_ref[:, :, :, n * 512 : n * 512 + 512].reshape(ROWS, 512)
            high = v.astype(BF16)
            rest = v - high.astype(F32)
            mid = rest.astype(BF16)
            low = (rest - mid.astype(F32)).astype(BF16)
            own_ref[:, n * 512 : n * 512 + 512] = (
                dot(chosen, high, 1, 0) + dot(chosen, mid, 1, 0) + dot(chosen, low, 1, 0)
            )

    offsets = (0, -1, 1, 2)
    ring1 = [ring(m, 0, m, 0, 0) for m in range(2)]
    ring2 = [{du: ring(m, 1 + n, m, du, 1) for n, du in enumerate(offsets)} for m in range(2)]

    def begin(r):
        r["send_plus"].start()
        r["send_minus"].start()

    for m in range(2):
        begin(ring1[m])
    for m in range(2):
        begin(ring2[m][0])
    for d, arrive, forward in ((-1, "from_minus", "fwd_plus"), (1, "from_plus", "fwd_minus")):
        for m in range(2):
            ring1[m][arrive].wait_recv()
            ring1[m][forward].start()
            begin(ring2[m][d])
            cross(m, ring1[m]["block"](d))
    for m in range(2):
        ring1[m]["far_a"].wait_recv()
        ring1[m]["far_b"].wait_recv()
        begin(ring2[m][2])
        cross(m, ring1[m]["block"](2))
    beside = {0: make_pairs, -1: make_weights, 1: make_own}
    for du in offsets:
        for d, arrive, forward in ((-1, "from_minus", "fwd_plus"), (1, "from_plus", "fwd_minus")):
            for m in range(2):
                r = ring2[m][du]
                r[arrive].wait_recv()
                r[forward].start()
                cross(m, r["block"](d))
        if du in beside:
            beside[du]()
    for du in offsets:
        for m in range(2):
            r = ring2[m][du]
            r["far_a"].wait_recv()
            r["far_b"].wait_recv()
            cross(m, r["block"](2))

    for d in (1, 2, 3):
        c_copy(d, (rep + 4 - d) % 4).wait_recv()
    cots = (call_ref[0] + call_ref[1] + call_ref[2] + call_ref[3]) * loss_scale
    by_row = ones_where(iota((VIDEOS, VIDEOS), 0) == vrows_ref[...])
    lengths = dot(jnp.broadcast_to(counts_ref[...], (8, VIDEOS)).astype(F32).astype(BF16), by_row, 1, 1)
    lengths_half = lengths.astype(BF16)
    at = iota((VIDEOS, LANES), 0)
    lane = iota((1, LANES), 1)
    len_a = dot(lengths_half, ones_where(at == 2 * owner + lane // 256), 1, 0)[0:1]
    pick_b = ones_where(at == 4 * ((lane % 64) // 4) + rep)
    len_b = dot(lengths_half, pick_b, 1, 0)[0:1]
    ok_a = ((lane // 64) % 4 * 4).astype(F32) < len_a
    ok_b = (lane % 4 * 4).astype(F32) < len_b
    inv_a = 1.0 / quad_sum(jnp.where(ok_a, 1.0, 0.0), 64)
    inv_b = 1.0 / quad_sum(jnp.where(ok_b, 1.0, 0.0), 1)
    mine = iota((8, VIDEOS), 1) == 2 * owner + iota((8, VIDEOS), 0) % 2
    mine = ones_where(mine)
    high = cots.astype(BF16)
    rest = cots - high.astype(F32)
    mid = rest.astype(BF16)
    low = (rest - mid.astype(F32)).astype(BF16)
    cot = []
    for cb in (0, 1):
        c_rows = dot(mine, high, 1, cb) + dot(mine, mid, 1, cb) + dot(mine, low, 1, cb)
        spread = dot_exact(c_rows, pick_b)
        cot.append(jnp.where(lane < 256, spread[0:1], spread[1:2]))
    frames_b = iota((1, 256), 1)
    len_vb = dot(lengths_half, ones_where(iota((VIDEOS, 256), 0) == 4 * (frames_b // 16) + rep), 1, 0)[0:1]
    valid_b = (frames_b % 16).astype(F32) < len_vb
    rows_32 = iota((32, VIDEOS), 0)
    len_va = jnp.sum(
        jnp.where(iota((32, VIDEOS), 1) == 2 * owner + rows_32 // 16, jnp.broadcast_to(lengths[0:1], (32, VIDEOS)), 0.0),
        axis=1,
        keepdims=True,
    )
    valid = ((iota((32, 256), 0) % 16).astype(F32) < len_va) & valid_b

    for copy, arriving in crossings:
        arriving.wait_recv()

    @pl.when(core != kc)
    def _():
        halves[1].wait_recv()

    pa = pa_ref[...].reshape(ROWS, WIDTH)
    sum1 = jnp.zeros((ROWS, 256), F32)
    fm2 = jnp.zeros((32, 256), F32)
    for s in range(REGIONS):
        pbs = pb_ref[:, s].reshape(SEEN * FRAMES, WIDTH)
        e = jnp.exp(dot(pa, pbs, 1, 1) * (1.0 / region_temp))
        e_ref[s] = e
        sum1 = sum1 + e
        sum2 = jnp.sum(e.reshape(OWN, REGIONS, FRAMES, 256), axis=1).reshape(32, 256)
        q2_ref[s] = sum2
        fm2 = fm2 + jnp.log(sum2)
    q1_ref[...] = sum1
    fm1 = jnp.sum(jnp.log(sum1).reshape(OWN, REGIONS, FRAMES, 256), axis=1).reshape(32, 256)
    scale = region_temp / REGIONS
    fm = jnp.concatenate([jnp.where(valid, fm1 * scale, 0.0), jnp.where(valid, fm2 * scale, 0.0)], axis=0)
    spot = iota((256, 256), 0)
    perm = ones_where((spot % 4) * 64 + (spot // 16) * 4 + (spot % 16) // 4 == iota((256, 256), 1))
    fm_ref[...] = dot_exact(fm, perm)
    for g in range(2):
        for p in range(OWN):
            for i4 in range(4):
                base = g * 32 + p * 16 + i4 * 4
                at = g * LANES + p * 256 + i4 * 64
                for pj in range(4):
                    if g == 0:
                        for pi in range(4):
                            x0_ref[pi * 4 + pj : pi * 4 + pj + 1, at : at + 64] = fm_ref[
                                base + pi : base + pi + 1, pj * 64 : pj * 64 + 64
                            ]
                    else:
                        x0_ref[pj * 4 : pj * 4 + 4, at : at + 64] = fm_ref[base : base + 4, pj * 64 : pj * 64 + 64]

    x0 = x0_ref[...]
    xcat = split2(jnp.concatenate([block_shift(x0, du, dv) for du, dv in SHIFTS], axis=0))
    w1 = split2(w1_ref[...])
    h1, ds1 = silu_pair(dot3(w1, xcat, 0, 0))
    pooled1 = []
    for qi in range(2):
        for qj in range(2):
            parts = [
                h1[((2 * qi + a) * 4 + 2 * qj + b) * 32 : ((2 * qi + a) * 4 + 2 * qj + b) * 32 + 32]
                for a in range(2)
                for b in range(2)
            ]
            pooled1.append((parts[0] + parts[1] + parts[2] + parts[3]) * 0.25)
    h1cat = split2(
        jnp.concatenate(
            [block_shift(pooled1[qi * 2 + qj], du, dv) for qi, du in EXT2 for qj, dv in EXT2], axis=0
        )
    )
    w2 = split2(w2_ref[...])
    h2, ds2 = silu_pair(dot3(w2, h1cat, 0, 0))
    pooled2 = (h2[0:64] + h2[64:128] + h2[128:192] + h2[192:256]) * 0.25
    h2cat = split2(jnp.concatenate([block_shift(pooled2, du, dv) for du, dv in SHIFTS], axis=0))
    w3 = split2(k3_ref[...])
    h3, ds3 = silu_pair(dot3(w3, h2cat, 0, 0))
    kl = jnp.sum(jnp.where(iota((C3, C3), 0) == iota((C3, C3), 1), kl_ref[...], 0.0), axis=1, keepdims=True)
    out = jnp.tanh(jnp.sum(h3 * kl, axis=0, keepdims=True))

    dz = []
    for g in range(2):
        o = out[:, g * LANES : (g + 1) * LANES]
        rows_ok, inv = ((ok_a, inv_a), (ok_b, inv_b))[g]
        weighted = jnp.where(ok_a & ok_b, jnp.exp(o * (1.0 / region_temp)), 0.0)
        row_sums = quad_sum(weighted, 1 if g == 0 else 64) + jnp.where(rows_ok, 0.0, 1.0)
        if g == 0:
            best = jnp.where(rows_ok, region_temp * jnp.log(row_sums), 0.0)
            ps = quad_sum(best, 64) * inv
        dout = cot[g] * inv * weighted / row_sums
        dz.append(dout * (1.0 - o * o))
    dz = jnp.concatenate(dz, axis=1)

    def scatter_copy(d):
        return pltpu.make_async_remote_copy(
            src_ref=acc_ref.at[pl.ds(pl.multiple_of(((chip + d) % 16) * 48, 48), 48)],
            dst_ref=part_a.at[d - 1],
            send_sem=sa.at[d - 1],
            recv_sem=ra.at[d - 1],
            device_id=in_plane(d),
            device_id_type=MESH,
        )

    def column_copy(d):
        return pltpu.make_async_remote_copy(
            src_ref=part_b.at[place],
            dst_ref=part_b.at[place],
            send_sem=sb.at[d - 1],
            recv_sem=rb.at[d - 1],
            device_id=in_column(d),
            device_id_type=MESH,
        )

    def gather_copy(d, at):
        return pltpu.make_async_remote_copy(
            src_ref=all_ref.at[pl.ds(pl.multiple_of(at * 48, 48), 48)],
            dst_ref=all_ref.at[pl.ds(pl.multiple_of(at * 48, 48), 48)],
            send_sem=sc.at[d - 1],
            recv_sem=rc.at[d - 1],
            device_id=in_plane(d),
            device_id_type=MESH,
        )

    def first(pair):
        return pair[0][:, :LANES], pair[1][:, :LANES]

    lane = lane_of((1, 128))
    row = jnp.where(lane % 4 == rep, jnp.concatenate([ps[:, 0:64], ps[:, 256:320]], axis=1), 0.0)
    at = lax.broadcasted_iota(jnp.int32, (32, 128), 0)
    acc_ref[ROW_PS : ROW_PS + 32] = jnp.where(at == owner, row, 0.0)
    dz_first = jnp.broadcast_to(dz[:, :LANES], (8, LANES))
    gl = dot3(split2(dz_first), split2(h3[:, :LANES]), 1, 1)
    dpre3 = split2(dz * kl * ds3)
    acc_ref[0:576] = dot3(first(h2cat), first(dpre3), 1, 1) * (1.0 / loss_scale)
    dh2cat = dot3(w3, dpre3, 1, 0)
    dpool2 = jnp.zeros((64, 2 * LANES), F32)
    for n, (du, dv) in enumerate(SHIFTS):
        dpool2 = dpool2 + block_shift(dh2cat[n * 64 : n * 64 + 64], -du, -dv)
    dpool2 = dpool2 * 0.25
    dpre2 = split2(jnp.concatenate([dpool2, dpool2, dpool2, dpool2], axis=0) * ds2)
    g2 = dot3(first(h1cat), first(dpre2), 1, 1)
    for ti in range(3):
        for tj in range(3):
            total = jnp.zeros((32, 64), F32)
            for pi in range(2):
                for pj in range(2):
                    row = ((pi + ti) * 4 + pj + tj) * 32
                    col = (pi * 2 + pj) * 64
                    total = total + g2[row : row + 32, col : col + 64]
            total = total * (1.0 / loss_scale)
            for half in range(2):
                n = (ti * 3 + tj) * 2 + half
                at = ROW_TWO + (n % 9) * 16
                acc_ref[at : at + 16, (n // 9) * 64 : (n // 9) * 64 + 64] = total[half * 16 : half * 16 + 16]
    dh1cat = dot3(w2, dpre2, 1, 0)
    dpool1 = [jnp.zeros((32, 2 * LANES), F32) for _ in range(4)]
    n = 0
    for qi, du in EXT2:
        for qj, dv in EXT2:
            dpool1[qi * 2 + qj] = dpool1[qi * 2 + qj] + block_shift(dh1cat[n * 32 : n * 32 + 32], -du, -dv)
            n += 1
    dpool1 = [d * 0.25 for d in dpool1]
    dpre1 = split2(
        jnp.concatenate([dpool1[(pi // 2) * 2 + pj // 2] for pi in range(4) for pj in range(4)], axis=0) * ds1
    )
    g1 = dot3(first(xcat), first(dpre1), 1, 1)
    at = iota((144, 512), 0)
    rows = []
    for ti in range(3):
        for tj in range(3):
            v = jnp.sum(jnp.where(at == tap_rows(ti, tj), g1, 0.0), axis=0, keepdims=True)
            v = v[:, 0:128] + v[:, 128:256] + v[:, 256:384] + v[:, 384:512]
            v = v + pltpu.roll(v, 64, 1)
            rows.append(v + pltpu.roll(v, 32, 1))
    rows.append(gl[0:1])
    rows.append(jnp.zeros((6, 128), F32))
    acc_ref[ROW_ONE : ROW_ONE + 16] = jnp.concatenate(rows, axis=0) * (1.0 / loss_scale)
    for d in range(1, 16):
        scatter_copy(d).start()
    dxcat = dot3(w1, dpre1, 1, 0)
    dx0 = jnp.zeros((16, 2 * LANES), F32)
    for n, (du, dv) in enumerate(SHIFTS):
        dx0 = dx0 + block_shift(dxcat[n * 16 : n * 16 + 16], -du, -dv)
    x0_ref[...] = dx0
    for g in range(2):
        for p in range(OWN):
            for i4 in range(4):
                base = g * 32 + p * 16 + i4 * 4
                at = g * LANES + p * 256 + i4 * 64
                for pj in range(4):
                    if g == 0:
                        for pi in range(4):
                            fm_ref[base + pi : base + pi + 1, pj * 64 : pj * 64 + 64] = x0_ref[
                                pi * 4 + pj : pi * 4 + pj + 1, at : at + 64
                            ]
                    else:
                        fm_ref[base : base + 4, pj * 64 : pj * 64 + 64] = x0_ref[pj * 4 : pj * 4 + 4, at : at + 64]
    dfm = dot_exact(fm_ref[...], perm, 1)
    dfm1 = jnp.where(valid, dfm[:32], 0.0) * (1.0 / REGIONS)
    dfm2 = jnp.where(valid, dfm[32:], 0.0) * (1.0 / REGIONS)

    sum1 = q1_ref[...].reshape(OWN, REGIONS, FRAMES, 256)
    q1 = dfm1.reshape(OWN, 1, FRAMES, 256) / sum1
    rowperm = ones_where(frame_rows((1, ROWS)) == iota((320, ROWS), 0))
    for s in range(REGIONS):
        q2 = (dfm2 / q2_ref[s]).reshape(OWN, 1, FRAMES, 256)
        grad = (e_ref[s].reshape(OWN, REGIONS, FRAMES, 256) * (q1 + q2)).reshape(ROWS, 256).astype(BF16)
        grad_ref[s] = dot(rowperm, grad, 1, 0).astype(BF16)

    def rep_copy(d, n):
        return pltpu.make_async_remote_copy(
            src_ref=send_ref.at[(rep + d) % 4, :, pl.ds(n * CHUNK, CHUNK)],
            dst_ref=recv_ref.at[d - 1, :, pl.ds(n * CHUNK, CHUNK)],
            send_sem=rs.at[n * 3 + d - 1],
            recv_sem=rr.at[n * 3 + d - 1],
            device_id=(owner, (rep + d) % 4),
            device_id_type=MESH,
        )

    for n in range(CHUNKS):
        cols = slice(n * CHUNK, (n + 1) * CHUNK)
        product = jnp.zeros((320, CHUNK), F32)
        for s in range(REGIONS):
            pbs = pb_ref[:, s, :, cols].reshape(SEEN * FRAMES, CHUNK)
            product = product + dot(grad_ref[s], pbs, 1, 0)
        product = product.reshape(SIDE, 80, CHUNK)
        rg_ref[:, :, cols] = product
        send_ref[:, :, cols] = product.astype(BF16)
        for d in (2, 1, 3):
            rep_copy(d, n).start()
        if n == 0:
            total = acc_ref[pl.ds(pl.multiple_of(chip * 48, 48), 48)]
            for d in range(1, 16):
                scatter_copy(d).wait_recv()
                total = total + part_a[d - 1]
            part_b[place] = total
            for d in range(1, 8):
                column_copy(d).start()
        if n == 2:
            for d in range(1, 8):
                pltpu.make_async_remote_copy(
                    src_ref=part_b.at[(place + 8 - d) % 8],
                    dst_ref=part_b.at[(place + 8 - d) % 8],
                    send_sem=sb.at[d - 1],
                    recv_sem=rb.at[d - 1],
                    device_id=in_column(d),
                    device_id_type=MESH,
                ).wait_recv()
            total = part_b[0]
            for q in range(1, 8):
                total = total + part_b[q]
            all_ref[pl.ds(pl.multiple_of(chip * 48, 48), 48)] = total
            for d in range(1, 16):
                gather_copy(d, chip).start()

    squares = jnp.zeros((80, 1), F32)
    along = jnp.zeros((80, 1), F32)
    for n in range(CHUNKS):
        cols = slice(n * CHUNK, (n + 1) * CHUNK)
        total = rg_ref[rep, :, cols]
        for d in (1, 3, 2):
            rep_copy(d, n).wait_recv()
            total = total + recv_ref[d - 1, :, cols].astype(F32)
        rg_ref[0, :, cols] = total
        own = own_ref[:, cols]
        squares = squares + jnp.sum(own * own, axis=1, keepdims=True)
        along = along + jnp.sum(own * total, axis=1, keepdims=True)
    inverse = lax.rsqrt(squares + norm_eps)
    back = along * inverse * inverse * inverse
    for n in range(CHUNKS):
        cols = slice(n * CHUNK, (n + 1) * CHUNK)
        result = rg_ref[0, :, cols] * inverse - own_ref[:, cols] * back
        for q in range(18):
            fg_ref[q, :, cols] = result[q * 4 : q * 4 + 4]
    for d in range(1, 16):
        gather_copy(d, (chip + 16 - d) % 16).wait_recv()
    g3_ref[...] = all_ref[0:ROW_TWO]
    for n in range(18):
        at = ROW_TWO + (n % 9) * 16
        g2_ref[n // 2, (n % 2) * 16 : (n % 2) * 16 + 16, :] = all_ref[at : at + 16, (n // 9) * 64 : (n // 9) * 64 + 64]
    g1_ref[...] = all_ref[ROW_ONE : ROW_ONE + 9, 0:32]
    gl_ref[...] = all_ref[ROW_ONE + 9 : ROW_ONE + 10]
    table = all_ref[ROW_PS:ROW_ALL]
    found = jnp.zeros((1, 512), F32)
    for p in range(OWN):
        left = dot(ones_where(iota((32, VIDEOS), 1) == 2 * iota((32, VIDEOS), 0) + p), hots_ref[0], 1, 0)
        value = dot_exact(table[:, p * 64 : p * 64 + 64], hots_ref[1])
        found = found + jnp.sum(left * value, axis=0, keepdims=True)
    ps_ref[...] = found

    for copy, arriving in crossings:
        copy.wait_send()
    for m in range(2):
        for r in [ring1[m]] + [ring2[m][du] for du in offsets]:
            for name in ("send_plus", "send_minus", "fwd_plus", "fwd_minus"):
                r[name].wait_send()

    @pl.when(core == kc)
    def _():
        halves[0].wait_send()
        halves[1].wait_send()

    for d in (1, 2, 3):
        c_copy(d, rep).wait_send()
        for n in range(CHUNKS):
            rep_copy(d, n).wait_send()
    for d in range(1, 16):
        scatter_copy(d).wait_send()
        gather_copy(d, chip).wait_send()
    for d in range(1, 8):
        column_copy(d).wait_send()


def whole(*args):
    return pl.pallas_call(
        whole_kernel,
        name="training_step",
        out_shape=(
            jax.ShapeDtypeStruct((OWN * REGIONS, 4, WIDTH), F32),
            jax.ShapeDtypeStruct((1, 512), F32),
            jax.ShapeDtypeStruct((9, 32), F32),
            jax.ShapeDtypeStruct((9, 32, 64), F32),
            jax.ShapeDtypeStruct((576, C3), F32),
            jax.ShapeDtypeStruct((1, C3), F32),
        ),
        in_specs=[VMEM_SPEC] * 9,
        out_specs=(VMEM_SPEC,) * 6,
        scratch_shapes=[
            pltpu.VMEM((OWN, REGIONS, FRAMES, WIDTH), BF16),
            pltpu.VMEM((SEEN, REGIONS, FRAMES, WIDTH), BF16),
            pltpu.VMEM((SIDE, VIDEOS, VIDEOS), F32),
            pltpu.VMEM((2, VIDEOS, 512), BF16),
            pltpu.VMEM((144, 512), F32),
            pltpu.VMEM((512, 256), F32),
            pltpu.VMEM((80, WIDTH), F32),
            pltpu.VMEM((REGIONS, ROWS, 256), F32),
            pltpu.VMEM((ROWS, 256), F32),
            pltpu.VMEM((REGIONS, 32, 256), F32),
            pltpu.VMEM((64, 256), F32),
            pltpu.VMEM((16, 2 * LANES), F32),
            pltpu.VMEM((REGIONS, 320, 256), BF16),
            pltpu.VMEM((ROW_ALL, 128), F32),
            pltpu.VMEM((SIDE, 80, WIDTH), F32),
            pltpu.VMEM((SIDE, 80, WIDTH), BF16),
            pltpu.VMEM((3, 80, WIDTH), BF16),
            pltpu.VMEM((15, 48, 128), F32),
            pltpu.VMEM((8, 48, 128), F32),
            pltpu.VMEM((ROW_ALL, 128), F32),
        ]
        + [
            pltpu.SemaphoreType.DMA((n,))
            for n in (40, 40, 30, 30, 3, 3, 1, 2, 2, 3 * CHUNKS, 3 * CHUNKS, 15, 15, 7, 7, 15, 15)
        ],
        compiler_params=pltpu.CompilerParams(
            collective_id=0, has_side_effects=True, vmem_limit_bytes=58 * 2**20
        ),
    )(*args)


def local(
    features, frame_counts, video_rows, pair_list, pair_cotangent, kernel_one, kernel_two, kernel_three, kernel_last
):
    fg, ps, g1, g2, g3, gl = whole(
        features.transpose(0, 2, 1, 3),
        frame_counts.reshape(1, VIDEOS),
        video_rows.reshape(1, VIDEOS),
        pair_list.T,
        pair_cotangent.reshape(1, 512),
        kernel_one.reshape(9, 32),
        kernel_two.reshape(9, 32, 64),
        kernel_three.reshape(576, C3),
        kernel_last.reshape(1, C3),
    )
    return (
        ps.reshape(512),
        fg.reshape(OWN, REGIONS, 4, WIDTH).transpose(0, 2, 1, 3),
        g1.reshape(3, 3, 1, 32),
        g2.reshape(3, 3, 32, 64),
        g3.reshape(3, 3, 64, C3),
        gl.reshape(C3),
    )


def solution(mesh):
    placed = (P("owner", None, None, None), P(), P(), P("rep", None), P("rep"), P(), P(), P(), P())
    return jax.shard_map(
        local,
        mesh=mesh,
        in_specs=placed,
        out_specs=(P("rep"), P("owner", "rep", None, None), P(), P(), P(), P()),
        check_vma=False,
    )
```

```python
import jax
import jax.numpy as jnp
from jax import lax
from jax.experimental import pallas as pl
from jax.experimental.pallas import tpu as pltpu
from jax.sharding import PartitionSpec as P

MESH = pl.DeviceIdType.MESH
VMEM_SPEC = pl.BlockSpec(memory_space=pltpu.VMEM)
ANY_SPEC = pl.BlockSpec(memory_space=pl.ANY)
F32 = jnp.float32
BF16 = jnp.bfloat16

REGIONS = 9
FRAMES = 16
WIDTH = 2048
VIDEOS = 64
SIDE = 4
OWN = 2
SEEN = 16
ROWS = OWN * REGIONS * FRAMES
LANES = OWN * SEEN * 16

ROW_TWO = 576
ROW_ONE = 720
ROW_PS = 736
ROW_ALL = 768

region_temp = 0.1
loss_scale = 131072.0
norm_eps = 1e-06
C3 = 128


CHUNKS = 4
CHUNK = WIDTH // CHUNKS


def split2(v):
    high = v.astype(BF16)
    return high, (v - high.astype(F32)).astype(BF16)


def dot(a, b, ca, cb):
    return lax.dot_general(a, b, (((ca,), (cb,)), ((), ())), preferred_element_type=F32)


def dot3(a, b, ca, cb):
    (ah, al), (bh, bl) = a, b
    return dot(ah, bh, ca, cb) + dot(ah, bl, ca, cb) + dot(al, bh, ca, cb)


def dot_exact(v, chosen, cb=0):
    high = v.astype(BF16)
    rest = v - high.astype(F32)
    mid = rest.astype(BF16)
    low = (rest - mid.astype(F32)).astype(BF16)
    return dot(high, chosen, 1, cb) + dot(mid, chosen, 1, cb) + dot(low, chosen, 1, cb)


def lane_of(shape):
    return lax.broadcasted_iota(jnp.int32, shape, len(shape) - 1)


def moved(v, di, dj):
    if di == 0 and dj == 0:
        return v
    out = pltpu.roll(v, (-(di * 64 + dj)) % LANES, 1)
    lane = lane_of((1, LANES))
    i4, j4 = (lane // 64) % 4, lane % 4
    ok = (i4 + di >= 0) & (i4 + di < 4) & (j4 + dj >= 0) & (j4 + dj < 4)
    return jnp.where(ok, out, 0.0)


def block_shift(v, du, dv):
    return jnp.concatenate([moved(v[:, :LANES], du, dv), moved(v[:, LANES:], dv, du)], axis=1)


def quad_sum(v, stride):
    lane = lane_of((1, LANES))
    for step in (stride, 2 * stride):
        low = (lane // step) % 2 == 0
        v = v + jnp.where(low, pltpu.roll(v, LANES - step, 1), pltpu.roll(v, step, 1))
    return v


def silu_pair(v):
    s = 1.0 / (1.0 + jnp.exp(-v))
    return v * s, s * (1.0 + v * (1.0 - s))


def iota(shape, axis):
    return lax.broadcasted_iota(jnp.int32, shape, axis)


def ones_where(condition):
    return jnp.where(condition, 1.0, 0.0).astype(BF16)


def tap_rows(ti, tj):
    plane = lane_of((1, 512)) // 32
    ei, ej = plane // 4 + ti + 3, plane % 4 + tj + 3
    return ((ei // 4) * 3 + ej // 4) * 16 + (ei % 4) * 4 + ej % 4


SHIFTS = [(du, dv) for du in (-1, 0, 1) for dv in (-1, 0, 1)]
EXT2 = [(1, -1), (0, 0), (1, 0), (0, 1)]


def whole_kernel(
    x_hbm, counts_ref, vrows_ref, pairs_ref, cot_ref, k1_ref, k2_hbm, k3_hbm, kl_ref,
    fg_ref, ps_ref, all_ref,
    x_ref, k2_ref, k3_ref, pa_ref, pb_ref, call_ref, hots_ref, w1_ref, w2_ref, own_ref,
    e_ref, q1_ref, q2_ref, fm_ref, x0_ref, grad_ref, acc_ref, rg_ref, send_ref, recv_ref, part_a, part_b,
    ssem, rsem, dssem, drsem, csem, crsem, lsem, insem, hs, hr, rs, rr, sa, ra, sb, rb, sc, rc,
):
    owner = lax.axis_index("owner")
    rep = lax.axis_index("rep")
    z, x, core = owner // 8, (owner // 2) % 4, owner % 2
    chip = owner // 2
    place = core * 4 + rep
    other = owner + 1 - 2 * core

    def in_plane(d):
        return (((chip + d) % 16) * 2 + core, rep)

    def in_column(d):
        to = (place + d) % 8
        return (chip * 2 + to // 4, to % 4)

    def shifted(axis, d):
        if axis == 0:
            return z * 8 + ((x + d + 4) % 4) * 2 + core
        return ((z + d + 4) % 4) * 8 + x * 2 + core

    def chip_at(first, du, dv):
        dx, dz = (du, dv) if first == 0 else (dv, du)
        return ((z + dz + 4) % 4) * 4 + (x + dx + 4) % 4

    loads = [pltpu.make_async_copy(x_hbm.at[p], x_ref.at[p], insem.at[p]) for p in range(OWN)]
    loads.append(pltpu.make_async_copy(k2_hbm, k2_ref, insem.at[2]))
    loads.append(pltpu.make_async_copy(k3_hbm, k3_ref, insem.at[3]))
    for load in loads:
        load.start()
    barrier = pltpu.get_barrier_semaphore()
    for d in range(1, 16):
        pl.semaphore_signal(barrier, inc=1, device_id=in_plane(d), device_id_type=MESH)
    for d in range(1, 8):
        pl.semaphore_signal(barrier, inc=1, device_id=in_column(d), device_id_type=MESH)

    for p in range(OWN):
        loads[p].wait()
        values = x_ref[p]
        summed = jnp.sum(values * values, axis=-1, keepdims=True) + norm_eps
        pa_ref[p] = (values * lax.rsqrt(summed)).astype(BF16)

    pl.semaphore_wait(barrier, 22)

    kc, kp = rep // 2, rep % 2
    local = pltpu.make_async_copy(pa_ref.at[kp], pb_ref.at[chip], lsem.at[0])

    def own_lanes(to, m):
        return pl.ds(pl.multiple_of(to * 1024 + m * 512, 512), 512)

    def to_other(n, lanes):
        return pltpu.make_async_remote_copy(
            src_ref=pa_ref.at[kp, :, :, lanes],
            dst_ref=pb_ref.at[chip, :, :, lanes],
            send_sem=hs.at[n],
            recv_sem=hr.at[n],
            device_id=(other, rep),
            device_id_type=MESH,
        )

    sent = [to_other(0, own_lanes(1 - core, 0)), to_other(1, own_lanes(1 - core, 1))]
    sent.append(to_other(2, pl.ds(pl.multiple_of(core * 1024, 1024), 1024)))
    got = [to_other(0, own_lanes(core, 0)), to_other(1, own_lanes(core, 1))]
    got.append(to_other(2, pl.ds(pl.multiple_of((1 - core) * 1024, 1024), 1024)))

    def piece(block, m, half):
        if half is None:
            lanes = pl.ds(pl.multiple_of(core * 1024 + m * 512, 512), 512)
        else:
            lanes = pl.ds(pl.multiple_of(core * 1024 + m * 512 + half * 256, 256), 256)
        return pb_ref.at[block, :, :, lanes]

    def ring(m, index, first, du, along):
        base = (m * 5 + index) * 4
        axis = first if along == 0 else 1 - first

        def block(d):
            return chip_at(first, d, 0) if along == 0 else chip_at(first, du, d)

        def copy(slot, source, d, half, prepared=False):
            ref = piece(source, m, half)
            return pltpu.make_async_remote_copy(
                src_ref=pa_ref.at[kp, :, :, own_lanes(core, m)] if prepared else ref,
                dst_ref=ref,
                send_sem=ssem.at[base + slot],
                recv_sem=rsem.at[base + slot],
                device_id=(shifted(axis, d), rep),
                device_id_type=MESH,
            )

        return dict(
            first_plus=copy(0, block(0), 1, None, True),
            first_minus=copy(1, block(0), -1, None, True),
            send_plus=copy(0, block(0), 1, None),
            send_minus=copy(1, block(0), -1, None),
            fwd_plus=copy(2, block(-1), 1, 0),
            fwd_minus=copy(3, block(1), -1, 1),
            from_minus=copy(0, block(-1), 1, None),
            from_plus=copy(1, block(1), -1, None),
            far_a=copy(2, block(2), 1, 0),
            far_b=copy(3, block(2), -1, 1),
            block=block,
        )

    crossings = []

    def cross(m, block):
        n = len(crossings)
        ref = piece(block, m, None)
        copy = pltpu.make_async_remote_copy(
            src_ref=ref,
            dst_ref=ref,
            send_sem=dssem.at[n],
            recv_sem=drsem.at[n],
            device_id=(other, rep),
            device_id_type=MESH,
        )
        copy.start()
        lanes = pl.ds(pl.multiple_of((1 - core) * 1024 + m * 512, 512), 512)
        theirs = pb_ref.at[block, :, :, lanes]
        arriving = pltpu.make_async_remote_copy(
            src_ref=theirs,
            dst_ref=theirs,
            send_sem=dssem.at[n],
            recv_sem=drsem.at[n],
            device_id=(other, rep),
            device_id_type=MESH,
        )
        crossings.append((copy, arriving))

    def c_copy(d, at):
        return pltpu.make_async_remote_copy(
            src_ref=call_ref.at[at],
            dst_ref=call_ref.at[at],
            send_sem=csem.at[d - 1],
            recv_sem=crsem.at[d - 1],
            device_id=(owner, (rep + d) % 4),
            device_id_type=MESH,
        )

    def make_pairs():
        by_row = ones_where(iota((VIDEOS, VIDEOS), 0) == vrows_ref[...])
        videos = iota((VIDEOS, 512), 0)
        row_a = dot(by_row, ones_where(videos == pairs_ref[0:1, :]), 1, 0)
        row_b = dot(by_row, ones_where(videos == pairs_ref[1:2, :]), 1, 0)
        hots_ref[0] = row_a.astype(BF16)
        hots_ref[1] = row_b.astype(BF16)
        call_ref[rep] = dot_exact(row_a * cot_ref[...], row_b.astype(BF16), 1)
        for d in (1, 2, 3):
            c_copy(d, rep).start()

    def make_weights():
        loads[2].wait()
        loads[3].wait()
        k1 = jnp.concatenate([k1_ref[n // 3, n % 3] for n in range(9)], axis=0)
        tiled = dot_exact(k1, ones_where(iota((32, 512), 1) % 32 == iota((32, 512), 0)))
        at = iota((144, 512), 0)
        w1 = jnp.zeros((144, 512), F32)
        for ti in range(3):
            for tj in range(3):
                w1 = jnp.where(at == tap_rows(ti, tj), tiled[ti * 3 + tj : ti * 3 + tj + 1], w1)
        w1_ref[...] = w1
        w2_ref[...] = jnp.zeros((512, 256), F32)
        for ti in range(3):
            for tj in range(3):
                for pi in range(2):
                    for pj in range(2):
                        row = ((pi + ti) * 4 + pj + tj) * 32
                        col = (pi * 2 + pj) * 64
                        w2_ref[row : row + 32, col : col + 64] = k2_ref[ti * 3 + tj]

    def frame_rows(shape):
        n = lane_of(shape)
        return ((n % 16) // 4) * 80 + (n // 144) * 36 + ((n % 144) // 16) * 4 + n % 4

    def make_own():
        chosen = ones_where(frame_rows((1, ROWS)) - rep * 80 == iota((80, ROWS), 0))
        for n in range(4):
            v = x_ref[:, :, :, n * 512 : n * 512 + 512].reshape(ROWS, 512)
            high = v.astype(BF16)
            rest = v - high.astype(F32)
            mid = rest.astype(BF16)
            low = (rest - mid.astype(F32)).astype(BF16)
            own_ref[:, n * 512 : n * 512 + 512] = (
                dot(chosen, high, 1, 0) + dot(chosen, mid, 1, 0) + dot(chosen, low, 1, 0)
            )

    offsets = (0, -1, 1, 2)
    ring1 = [ring(m, 0, m, 0, 0) for m in range(2)]
    ring2 = [{du: ring(m, 1 + n, m, du, 1) for n, du in enumerate(offsets)} for m in range(2)]

    def begin(r):
        r["send_plus"].start()
        r["send_minus"].start()

    @pl.when(core == kc)
    def _():
        sent[0].start()
        sent[1].start()
        for r in (ring1[0], ring1[1], ring2[0][0], ring2[1][0]):
            r["first_plus"].start()
            r["first_minus"].start()
        local.start()
        sent[2].start()

    @pl.when(core != kc)
    def _():
        for m in range(2):
            got[m].wait_recv()
            begin(ring1[m])
            begin(ring2[m][0])

    for d, arrive, forward in ((-1, "from_minus", "fwd_plus"), (1, "from_plus", "fwd_minus")):
        for m in range(2):
            ring1[m][arrive].wait_recv()
            ring1[m][forward].start()
            begin(ring2[m][d])
            cross(m, ring1[m]["block"](d))
    for m in range(2):
        ring1[m]["far_a"].wait_recv()
        ring1[m]["far_b"].wait_recv()
        begin(ring2[m][2])
        cross(m, ring1[m]["block"](2))
    beside = {0: make_pairs, -1: make_weights, 1: make_own}
    for du in offsets:
        for d, arrive, forward in ((-1, "from_minus", "fwd_plus"), (1, "from_plus", "fwd_minus")):
            for m in range(2):
                r = ring2[m][du]
                r[arrive].wait_recv()
                r[forward].start()
                cross(m, r["block"](d))
        if du in beside:
            beside[du]()
    for du in offsets:
        for m in range(2):
            r = ring2[m][du]
            r["far_a"].wait_recv()
            r["far_b"].wait_recv()
            cross(m, r["block"](2))

    for d in (1, 2, 3):
        c_copy(d, (rep + 4 - d) % 4).wait_recv()
    cots = (call_ref[0] + call_ref[1] + call_ref[2] + call_ref[3]) * loss_scale
    by_row = ones_where(iota((VIDEOS, VIDEOS), 0) == vrows_ref[...])
    lengths = dot(jnp.broadcast_to(counts_ref[...], (8, VIDEOS)).astype(F32).astype(BF16), by_row, 1, 1)
    lengths_half = lengths.astype(BF16)
    at = iota((VIDEOS, LANES), 0)
    lane = iota((1, LANES), 1)
    len_a = dot(lengths_half, ones_where(at == 2 * owner + lane // 256), 1, 0)[0:1]
    pick_b = ones_where(at == 4 * ((lane % 64) // 4) + rep)
    len_b = dot(lengths_half, pick_b, 1, 0)[0:1]
    ok_a = ((lane // 64) % 4 * 4).astype(F32) < len_a
    ok_b = (lane % 4 * 4).astype(F32) < len_b
    inv_a = 1.0 / quad_sum(jnp.where(ok_a, 1.0, 0.0), 64)
    inv_b = 1.0 / quad_sum(jnp.where(ok_b, 1.0, 0.0), 1)
    mine = iota((8, VIDEOS), 1) == 2 * owner + iota((8, VIDEOS), 0) % 2
    mine = ones_where(mine)
    high = cots.astype(BF16)
    rest = cots - high.astype(F32)
    mid = rest.astype(BF16)
    low = (rest - mid.astype(F32)).astype(BF16)
    cot = []
    for cb in (0, 1):
        c_rows = dot(mine, high, 1, cb) + dot(mine, mid, 1, cb) + dot(mine, low, 1, cb)
        spread = dot_exact(c_rows, pick_b)
        cot.append(jnp.where(lane < 256, spread[0:1], spread[1:2]))
    frames_b = iota((1, 256), 1)
    len_vb = dot(lengths_half, ones_where(iota((VIDEOS, 256), 0) == 4 * (frames_b // 16) + rep), 1, 0)[0:1]
    valid_b = (frames_b % 16).astype(F32) < len_vb
    rows_32 = iota((32, VIDEOS), 0)
    len_va = jnp.sum(
        jnp.where(iota((32, VIDEOS), 1) == 2 * owner + rows_32 // 16, jnp.broadcast_to(lengths[0:1], (32, VIDEOS)), 0.0),
        axis=1,
        keepdims=True,
    )
    valid = ((iota((32, 256), 0) % 16).astype(F32) < len_va) & valid_b

    for copy, arriving in crossings:
        arriving.wait_recv()

    @pl.when(core == kc)
    def _():
        local.wait()

    @pl.when(core != kc)
    def _():
        got[2].wait_recv()

    pa = pa_ref[...].reshape(ROWS, WIDTH)
    sum1 = jnp.zeros((ROWS, 256), F32)
    fm2 = jnp.zeros((32, 256), F32)
    for s in range(REGIONS):
        pbs = pb_ref[:, s].reshape(SEEN * FRAMES, WIDTH)
        e = jnp.exp(dot(pa, pbs, 1, 1) * (1.0 / region_temp))
        e_ref[s] = e
        sum1 = sum1 + e
        sum2 = jnp.sum(e.reshape(OWN, REGIONS, FRAMES, 256), axis=1).reshape(32, 256)
        q2_ref[s] = sum2
        fm2 = fm2 + jnp.log(sum2)
    q1_ref[...] = sum1
    fm1 = jnp.sum(jnp.log(sum1).reshape(OWN, REGIONS, FRAMES, 256), axis=1).reshape(32, 256)
    scale = region_temp / REGIONS
    fm = jnp.concatenate([jnp.where(valid, fm1 * scale, 0.0), jnp.where(valid, fm2 * scale, 0.0)], axis=0)
    spot = iota((256, 256), 0)
    perm = ones_where((spot % 4) * 64 + (spot // 16) * 4 + (spot % 16) // 4 == iota((256, 256), 1))
    fm_ref[...] = dot_exact(fm, perm)
    for g in range(2):
        for p in range(OWN):
            for i4 in range(4):
                base = g * 32 + p * 16 + i4 * 4
                at = g * LANES + p * 256 + i4 * 64
                for pj in range(4):
                    if g == 0:
                        for pi in range(4):
                            x0_ref[pi * 4 + pj : pi * 4 + pj + 1, at : at + 64] = fm_ref[
                                base + pi : base + pi + 1, pj * 64 : pj * 64 + 64
                            ]
                    else:
                        x0_ref[pj * 4 : pj * 4 + 4, at : at + 64] = fm_ref[base : base + 4, pj * 64 : pj * 64 + 64]

    x0 = x0_ref[...]
    xcat = split2(jnp.concatenate([block_shift(x0, du, dv) for du, dv in SHIFTS], axis=0))
    w1 = split2(w1_ref[...])
    h1, ds1 = silu_pair(dot3(w1, xcat, 0, 0))
    pooled1 = []
    for qi in range(2):
        for qj in range(2):
            parts = [
                h1[((2 * qi + a) * 4 + 2 * qj + b) * 32 : ((2 * qi + a) * 4 + 2 * qj + b) * 32 + 32]
                for a in range(2)
                for b in range(2)
            ]
            pooled1.append((parts[0] + parts[1] + parts[2] + parts[3]) * 0.25)
    h1cat = split2(
        jnp.concatenate(
            [block_shift(pooled1[qi * 2 + qj], du, dv) for qi, du in EXT2 for qj, dv in EXT2], axis=0
        )
    )
    w2 = split2(w2_ref[...])
    h2, ds2 = silu_pair(dot3(w2, h1cat, 0, 0))
    pooled2 = (h2[0:64] + h2[64:128] + h2[128:192] + h2[192:256]) * 0.25
    h2cat = split2(jnp.concatenate([block_shift(pooled2, du, dv) for du, dv in SHIFTS], axis=0))
    w3 = split2(k3_ref[...])
    h3, ds3 = silu_pair(dot3(w3, h2cat, 0, 0))
    kl = jnp.sum(jnp.where(iota((C3, C3), 0) == iota((C3, C3), 1), kl_ref[...], 0.0), axis=1, keepdims=True)
    out = jnp.tanh(jnp.sum(h3 * kl, axis=0, keepdims=True))

    dz = []
    for g in range(2):
        o = out[:, g * LANES : (g + 1) * LANES]
        rows_ok, inv = ((ok_a, inv_a), (ok_b, inv_b))[g]
        weighted = jnp.where(ok_a & ok_b, jnp.exp(o * (1.0 / region_temp)), 0.0)
        row_sums = quad_sum(weighted, 1 if g == 0 else 64) + jnp.where(rows_ok, 0.0, 1.0)
        if g == 0:
            best = jnp.where(rows_ok, region_temp * jnp.log(row_sums), 0.0)
            ps = quad_sum(best, 64) * inv
        dout = cot[g] * inv * weighted / row_sums
        dz.append(dout * (1.0 - o * o))
    dz = jnp.concatenate(dz, axis=1)

    def scatter_copy(d):
        return pltpu.make_async_remote_copy(
            src_ref=acc_ref.at[pl.ds(pl.multiple_of(((chip + d) % 16) * 48, 48), 48)],
            dst_ref=part_a.at[d - 1],
            send_sem=sa.at[d - 1],
            recv_sem=ra.at[d - 1],
            device_id=in_plane(d),
            device_id_type=MESH,
        )

    def column_copy(d):
        return pltpu.make_async_remote_copy(
            src_ref=part_b.at[place],
            dst_ref=part_b.at[place],
            send_sem=sb.at[d - 1],
            recv_sem=rb.at[d - 1],
            device_id=in_column(d),
            device_id_type=MESH,
        )

    def gather_copy(d, at):
        return pltpu.make_async_remote_copy(
            src_ref=all_ref.at[pl.ds(pl.multiple_of(at * 48, 48), 48)],
            dst_ref=all_ref.at[pl.ds(pl.multiple_of(at * 48, 48), 48)],
            send_sem=sc.at[d - 1],
            recv_sem=rc.at[d - 1],
            device_id=in_plane(d),
            device_id_type=MESH,
        )

    def first(pair):
        return pair[0][:, :LANES], pair[1][:, :LANES]

    lane = lane_of((1, 128))
    row = jnp.where(lane % 4 == rep, jnp.concatenate([ps[:, 0:64], ps[:, 256:320]], axis=1), 0.0)
    at = lax.broadcasted_iota(jnp.int32, (32, 128), 0)
    acc_ref[ROW_PS : ROW_PS + 32] = jnp.where(at == owner, row, 0.0)
    dz_first = jnp.broadcast_to(dz[:, :LANES], (8, LANES))
    gl = dot3(split2(dz_first), split2(h3[:, :LANES]), 1, 1)
    dpre3 = split2(dz * kl * ds3)
    acc_ref[0:576] = dot3(first(h2cat), first(dpre3), 1, 1) * (1.0 / loss_scale)
    dh2cat = dot3(w3, dpre3, 1, 0)
    dpool2 = jnp.zeros((64, 2 * LANES), F32)
    for n, (du, dv) in enumerate(SHIFTS):
        dpool2 = dpool2 + block_shift(dh2cat[n * 64 : n * 64 + 64], -du, -dv)
    dpool2 = dpool2 * 0.25
    dpre2 = split2(jnp.concatenate([dpool2, dpool2, dpool2, dpool2], axis=0) * ds2)
    g2 = dot3(first(h1cat), first(dpre2), 1, 1)
    for ti in range(3):
        for tj in range(3):
            total = jnp.zeros((32, 64), F32)
            for pi in range(2):
                for pj in range(2):
                    row = ((pi + ti) * 4 + pj + tj) * 32
                    col = (pi * 2 + pj) * 64
                    total = total + g2[row : row + 32, col : col + 64]
            total = total * (1.0 / loss_scale)
            for half in range(2):
                n = (ti * 3 + tj) * 2 + half
                at = ROW_TWO + (n % 9) * 16
                acc_ref[at : at + 16, (n // 9) * 64 : (n // 9) * 64 + 64] = total[half * 16 : half * 16 + 16]
    dh1cat = dot3(w2, dpre2, 1, 0)
    dpool1 = [jnp.zeros((32, 2 * LANES), F32) for _ in range(4)]
    n = 0
    for qi, du in EXT2:
        for qj, dv in EXT2:
            dpool1[qi * 2 + qj] = dpool1[qi * 2 + qj] + block_shift(dh1cat[n * 32 : n * 32 + 32], -du, -dv)
            n += 1
    dpool1 = [d * 0.25 for d in dpool1]
    dpre1 = split2(
        jnp.concatenate([dpool1[(pi // 2) * 2 + pj // 2] for pi in range(4) for pj in range(4)], axis=0) * ds1
    )
    g1 = dot3(first(xcat), first(dpre1), 1, 1)
    at = iota((144, 512), 0)
    rows = []
    for ti in range(3):
        for tj in range(3):
            v = jnp.sum(jnp.where(at == tap_rows(ti, tj), g1, 0.0), axis=0, keepdims=True)
            v = v[:, 0:128] + v[:, 128:256] + v[:, 256:384] + v[:, 384:512]
            v = v + pltpu.roll(v, 64, 1)
            rows.append(v + pltpu.roll(v, 32, 1))
    rows.append(gl[0:1])
    rows.append(jnp.zeros((6, 128), F32))
    acc_ref[ROW_ONE : ROW_ONE + 16] = jnp.concatenate(rows, axis=0) * (1.0 / loss_scale)
    for d in range(1, 16):
        scatter_copy(d).start()
    dxcat = dot3(w1, dpre1, 1, 0)
    dx0 = jnp.zeros((16, 2 * LANES), F32)
    for n, (du, dv) in enumerate(SHIFTS):
        dx0 = dx0 + block_shift(dxcat[n * 16 : n * 16 + 16], -du, -dv)
    x0_ref[...] = dx0
    for g in range(2):
        for p in range(OWN):
            for i4 in range(4):
                base = g * 32 + p * 16 + i4 * 4
                at = g * LANES + p * 256 + i4 * 64
                for pj in range(4):
                    if g == 0:
                        for pi in range(4):
                            fm_ref[base + pi : base + pi + 1, pj * 64 : pj * 64 + 64] = x0_ref[
                                pi * 4 + pj : pi * 4 + pj + 1, at : at + 64
                            ]
                    else:
                        fm_ref[base : base + 4, pj * 64 : pj * 64 + 64] = x0_ref[pj * 4 : pj * 4 + 4, at : at + 64]
    dfm = dot_exact(fm_ref[...], perm, 1)
    dfm1 = jnp.where(valid, dfm[:32], 0.0) * (1.0 / REGIONS)
    dfm2 = jnp.where(valid, dfm[32:], 0.0) * (1.0 / REGIONS)

    sum1 = q1_ref[...].reshape(OWN, REGIONS, FRAMES, 256)
    q1 = dfm1.reshape(OWN, 1, FRAMES, 256) / sum1
    rowperm = ones_where(frame_rows((1, ROWS)) == iota((320, ROWS), 0))
    for s in range(REGIONS):
        q2 = (dfm2 / q2_ref[s]).reshape(OWN, 1, FRAMES, 256)
        grad = (e_ref[s].reshape(OWN, REGIONS, FRAMES, 256) * (q1 + q2)).reshape(ROWS, 256).astype(BF16)
        grad_ref[s] = dot(rowperm, grad, 1, 0).astype(BF16)

    def way(n):
        return 1 if n < 2 else -1

    def rep_copy(kind, n):
        d = -way(n) if kind == 2 else way(n)
        of = (rep + 2) % 4 if kind == 0 else (rep + d + 4) % 4
        return pltpu.make_async_remote_copy(
            src_ref=send_ref.at[of, :, pl.ds(n * CHUNK, CHUNK)],
            dst_ref=recv_ref.at[kind, :, pl.ds(n * CHUNK, CHUNK)],
            send_sem=rs.at[n * 3 + kind],
            recv_sem=rr.at[n * 3 + kind],
            device_id=(owner, (rep + d + 4) % 4),
            device_id_type=MESH,
        )

    order = (0, 2, 1, 3)
    total = acc_ref[pl.ds(pl.multiple_of(chip * 48, 48), 48)]
    for d in range(1, 16):
        scatter_copy(d).wait_recv()
        total = total + part_a[d - 1]
    part_b[place] = total
    for d in range(1, 8):
        column_copy(d).start()
    for n in order:
        cols = slice(n * CHUNK, (n + 1) * CHUNK)
        product = jnp.zeros((320, CHUNK), F32)
        for s in range(REGIONS):
            pbs = pb_ref[:, s, :, cols].reshape(SEEN * FRAMES, CHUNK)
            product = product + dot(grad_ref[s], pbs, 1, 0)
        product = product.reshape(SIDE, 80, CHUNK)
        rg_ref[:, :, cols] = product
        send_ref[:, :, cols] = product.astype(BF16)
        rep_copy(0, n).start()
        rep_copy(2, n).start()
    for n in order:
        cols = slice(n * CHUNK, (n + 1) * CHUNK)
        of = (rep + way(n) + 4) % 4
        rep_copy(0, n).wait_recv()
        send_ref[of, :, cols] = (rg_ref[of, :, cols] + recv_ref[0, :, cols].astype(F32)).astype(BF16)
        rep_copy(1, n).start()
    for d in range(1, 8):
        pltpu.make_async_remote_copy(
            src_ref=part_b.at[(place + 8 - d) % 8],
            dst_ref=part_b.at[(place + 8 - d) % 8],
            send_sem=sb.at[d - 1],
            recv_sem=rb.at[d - 1],
            device_id=in_column(d),
            device_id_type=MESH,
        ).wait_recv()
    total = part_b[0]
    for q in range(1, 8):
        total = total + part_b[q]
    all_ref[pl.ds(pl.multiple_of(chip * 48, 48), 48)] = total
    for d in range(1, 16):
        gather_copy(d, chip).start()

    for d in range(1, 16):
        gather_copy(d, (chip + 16 - d) % 16).wait_recv()
    table = all_ref[ROW_PS:ROW_ALL]
    found = jnp.zeros((1, 512), F32)
    for p in range(OWN):
        left = dot(ones_where(iota((32, VIDEOS), 1) == 2 * iota((32, VIDEOS), 0) + p), hots_ref[0], 1, 0)
        value = dot_exact(table[:, p * 64 : p * 64 + 64], hots_ref[1])
        found = found + jnp.sum(left * value, axis=0, keepdims=True)
    ps_ref[...] = found
    own = own_ref[...]
    inverse = lax.rsqrt(jnp.sum(own * own, axis=1, keepdims=True) + norm_eps)
    along = jnp.zeros((80, 1), F32)
    for n in order:
        cols = slice(n * CHUNK, (n + 1) * CHUNK)
        rep_copy(2, n).wait_recv()
        rep_copy(1, n).wait_recv()
        total = rg_ref[rep, :, cols] + recv_ref[2, :, cols].astype(F32) + recv_ref[1, :, cols].astype(F32)
        rg_ref[rep, :, cols] = total
        along = along + jnp.sum(own_ref[:, cols] * total, axis=1, keepdims=True)
    back = along * inverse * inverse * inverse
    for n in range(CHUNKS):
        cols = slice(n * CHUNK, (n + 1) * CHUNK)
        result = rg_ref[rep, :, cols] * inverse - own_ref[:, cols] * back
        for q in range(18):
            fg_ref[q, :, cols] = result[q * 4 : q * 4 + 4]

    for copy, arriving in crossings:
        copy.wait_send()
    for m in range(2):
        for r in [ring1[m]] + [ring2[m][du] for du in offsets]:
            for name in ("send_plus", "send_minus", "fwd_plus", "fwd_minus"):
                r[name].wait_send()

    @pl.when(core == kc)
    def _():
        for copy in sent:
            copy.wait_send()

    for d in (1, 2, 3):
        c_copy(d, rep).wait_send()
        for n in range(CHUNKS):
            rep_copy(d - 1, n).wait_send()
    for d in range(1, 16):
        scatter_copy(d).wait_send()
        gather_copy(d, chip).wait_send()
    for d in range(1, 8):
        column_copy(d).wait_send()


def whole(*args):
    return pl.pallas_call(
        whole_kernel,
        name="training_step",
        out_shape=(
            jax.ShapeDtypeStruct((OWN * REGIONS, 4, WIDTH), F32),
            jax.ShapeDtypeStruct((1, 512), F32),
            jax.ShapeDtypeStruct((ROW_ALL, 128), F32),
        ),
        in_specs=[ANY_SPEC] + [VMEM_SPEC] * 5 + [ANY_SPEC] * 2 + [VMEM_SPEC],
        out_specs=(VMEM_SPEC,) * 3,
        scratch_shapes=[
            pltpu.VMEM((OWN, REGIONS, FRAMES, WIDTH), F32),
            pltpu.VMEM((9, 32, 64), F32),
            pltpu.VMEM((576, C3), F32),
            pltpu.VMEM((OWN, REGIONS, FRAMES, WIDTH), BF16),
            pltpu.VMEM((SEEN, REGIONS, FRAMES, WIDTH), BF16),
            pltpu.VMEM((SIDE, VIDEOS, VIDEOS), F32),
            pltpu.VMEM((2, VIDEOS, 512), BF16),
            pltpu.VMEM((144, 512), F32),
            pltpu.VMEM((512, 256), F32),
            pltpu.VMEM((80, WIDTH), F32),
            pltpu.VMEM((REGIONS, ROWS, 256), F32),
            pltpu.VMEM((ROWS, 256), F32),
            pltpu.VMEM((REGIONS, 32, 256), F32),
            pltpu.VMEM((64, 256), F32),
            pltpu.VMEM((16, 2 * LANES), F32),
            pltpu.VMEM((REGIONS, 320, 256), BF16),
            pltpu.VMEM((ROW_ALL, 128), F32),
            pltpu.VMEM((SIDE, 80, WIDTH), F32),
            pltpu.VMEM((SIDE, 80, WIDTH), BF16),
            pltpu.VMEM((3, 80, WIDTH), BF16),
            pltpu.VMEM((15, 48, 128), F32),
            pltpu.VMEM((8, 48, 128), F32),
        ]
        + [
            pltpu.SemaphoreType.DMA((n,))
            for n in (40, 40, 30, 30, 3, 3, 1, 4, 3, 3, 3 * CHUNKS, 3 * CHUNKS, 15, 15, 7, 7, 15, 15)
        ],
        compiler_params=pltpu.CompilerParams(
            collective_id=0, has_side_effects=True, vmem_limit_bytes=58 * 2**20
        ),
    )(*args)


def outputs_kernel(fg_in, ps_in, all_in, ps_ref, fg_ref, g1_ref, g2_ref, g3_ref, gl_ref, sem):
    copies = [
        pltpu.make_async_copy(fg_in, fg_ref, sem.at[0]),
        pltpu.make_async_copy(ps_in, ps_ref, sem.at[1]),
        pltpu.make_async_copy(all_in.at[0:ROW_TWO], g3_ref, sem.at[2]),
    ]
    for copy in copies:
        copy.start()
    small = all_in
    for n in range(18):
        at = ROW_TWO + (n % 9) * 16
        g2_ref[n // 2, (n % 2) * 16 : (n % 2) * 16 + 16, :] = small[at : at + 16, (n // 9) * 64 : (n // 9) * 64 + 64]
    for n in range(9):
        g1_ref[n // 3, n % 3] = small[ROW_ONE + n : ROW_ONE + n + 1, 0:32]
    gl_ref[...] = small[ROW_ONE + 9 : ROW_ONE + 10]
    for copy in copies:
        copy.wait()


def outputs(fg, ps, summed):
    return pl.pallas_call(
        outputs_kernel,
        name="outputs",
        out_shape=(
            jax.ShapeDtypeStruct((1, 512), F32),
            jax.ShapeDtypeStruct((OWN * REGIONS, 4, WIDTH), F32),
            jax.ShapeDtypeStruct((3, 3, 1, 32), F32),
            jax.ShapeDtypeStruct((9, 32, 64), F32),
            jax.ShapeDtypeStruct((576, C3), F32),
            jax.ShapeDtypeStruct((1, C3), F32),
        ),
        in_specs=[ANY_SPEC, ANY_SPEC, VMEM_SPEC],
        out_specs=(ANY_SPEC, ANY_SPEC, VMEM_SPEC, VMEM_SPEC, ANY_SPEC, VMEM_SPEC),
        scratch_shapes=[pltpu.SemaphoreType.DMA((3,))],
    )(fg, ps, summed)


def local(
    features, frame_counts, video_rows, pair_list, pair_cotangent, kernel_one, kernel_two, kernel_three, kernel_last
):
    fg, ps, summed = whole(
        features.transpose(0, 2, 1, 3),
        frame_counts.reshape(1, VIDEOS),
        video_rows.reshape(1, VIDEOS),
        pair_list.T,
        pair_cotangent.reshape(1, 512),
        kernel_one,
        kernel_two.reshape(9, 32, 64),
        kernel_three.reshape(576, C3),
        kernel_last.reshape(1, C3),
    )
    ps, fg, g1, g2, g3, gl = outputs(fg, ps, summed)
    return (
        ps.reshape(512),
        fg.reshape(OWN, REGIONS, 4, WIDTH).transpose(0, 2, 1, 3),
        g1,
        g2.reshape(3, 3, 32, 64),
        g3.reshape(3, 3, 64, C3),
        gl.reshape(C3),
    )


def solution(mesh):
    placed = (P("owner", None, None, None), P(), P(), P("rep", None), P("rep"), P(), P(), P(), P())
    return jax.shard_map(
        local,
        mesh=mesh,
        in_specs=placed,
        out_specs=(P("rep"), P("owner", "rep", None, None), P(), P(), P(), P()),
        check_vma=False,
    )
```

```python
import jax
import jax.numpy as jnp
from jax import lax
from jax.experimental import pallas as pl
from jax.experimental.pallas import tpu as pltpu
from jax.sharding import PartitionSpec as P

MESH = pl.DeviceIdType.MESH
VMEM_SPEC = pl.BlockSpec(memory_space=pltpu.VMEM)
ANY_SPEC = pl.BlockSpec(memory_space=pl.ANY)
F32 = jnp.float32
BF16 = jnp.bfloat16

REGIONS = 9
FRAMES = 16
WIDTH = 2048
VIDEOS = 64
SIDE = 4
OWN = 2
SEEN = 16
ROWS = OWN * REGIONS * FRAMES
LANES = OWN * SEEN * 16

ROW_TWO = 576
ROW_ONE = 720
ROW_PS = 736
ROW_ALL = 768

region_temp = 0.1
loss_scale = 131072.0
norm_eps = 1e-06
C3 = 128


CHUNKS = 4
CHUNK = WIDTH // CHUNKS


def split2(v):
    high = v.astype(BF16)
    return high, (v - high.astype(F32)).astype(BF16)


def dot(a, b, ca, cb):
    return lax.dot_general(a, b, (((ca,), (cb,)), ((), ())), preferred_element_type=F32)


def dot3(a, b, ca, cb):
    (ah, al), (bh, bl) = a, b
    return dot(ah, bh, ca, cb) + dot(ah, bl, ca, cb) + dot(al, bh, ca, cb)


def dot2(a, b, ca, cb):
    return dot(a[0], b, ca, cb) + dot(a[1], b, ca, cb)


def dot_exact(v, chosen, cb=0):
    high = v.astype(BF16)
    rest = v - high.astype(F32)
    mid = rest.astype(BF16)
    low = (rest - mid.astype(F32)).astype(BF16)
    return dot(high, chosen, 1, cb) + dot(mid, chosen, 1, cb) + dot(low, chosen, 1, cb)


def lane_of(shape):
    return lax.broadcasted_iota(jnp.int32, shape, len(shape) - 1)


def moved(v, di, dj):
    if di == 0 and dj == 0:
        return v
    out = pltpu.roll(v, (-(di * 64 + dj)) % LANES, 1)
    lane = lane_of((1, LANES))
    i4, j4 = (lane // 64) % 4, lane % 4
    ok = (i4 + di >= 0) & (i4 + di < 4) & (j4 + dj >= 0) & (j4 + dj < 4)
    return jnp.where(ok, out, 0.0)


def block_shift(v, du, dv):
    return jnp.concatenate([moved(v[:, :LANES], du, dv), moved(v[:, LANES:], dv, du)], axis=1)


def quad_sum(v, stride):
    lane = lane_of((1, LANES))
    for step in (stride, 2 * stride):
        low = (lane // step) % 2 == 0
        v = v + jnp.where(low, pltpu.roll(v, LANES - step, 1), pltpu.roll(v, step, 1))
    return v


def silu_pair(v):
    s = 1.0 / (1.0 + jnp.exp(-v))
    return v * s, s * (1.0 + v * (1.0 - s))


def iota(shape, axis):
    return lax.broadcasted_iota(jnp.int32, shape, axis)


def ones_where(condition):
    return jnp.where(condition, 1.0, 0.0).astype(BF16)


def tap_rows(ti, tj):
    plane = lane_of((1, 512)) // 32
    ei, ej = plane // 4 + ti + 3, plane % 4 + tj + 3
    return ((ei // 4) * 3 + ej // 4) * 16 + (ei % 4) * 4 + ej % 4


SHIFTS = [(du, dv) for du in (-1, 0, 1) for dv in (-1, 0, 1)]
EXT2 = [(1, -1), (0, 0), (1, 0), (0, 1)]


def whole_kernel(
    x_hbm, counts_ref, vrows_ref, pairs_ref, cot_ref, k1_ref, k2_hbm, k3_hbm, kl_ref,
    fg_ref, ps_ref, all_ref,
    x_ref, k2_ref, k3_ref, pa_ref, pb_ref, call_ref, hots_ref, w1_ref, w2_ref, own_ref,
    e_ref, q1_ref, q2_ref, fm_ref, x0_ref, grad_ref, acc_ref, rg_ref, send_ref, recv_ref, part_a, part_b,
    ssem, rsem, dssem, drsem, csem, crsem, lsem, insem, hs, hr, rs, rr, sa, ra, sb, rb, sc, rc,
):
    owner = lax.axis_index("owner")
    rep = lax.axis_index("rep")
    z, x, core = owner // 8, (owner // 2) % 4, owner % 2
    chip = owner // 2
    place = core * 4 + rep
    other = owner + 1 - 2 * core

    def in_plane(d):
        return (((chip + d) % 16) * 2 + core, rep)

    def in_column(d):
        to = (place + d) % 8
        return (chip * 2 + to // 4, to % 4)

    def shifted(axis, d):
        if axis == 0:
            return z * 8 + ((x + d + 4) % 4) * 2 + core
        return ((z + d + 4) % 4) * 8 + x * 2 + core

    def chip_at(first, du, dv):
        dx, dz = (du, dv) if first == 0 else (dv, du)
        return ((z + dz + 4) % 4) * 4 + (x + dx + 4) % 4

    loads = [pltpu.make_async_copy(x_hbm.at[p], x_ref.at[p], insem.at[p]) for p in range(OWN)]
    loads.append(pltpu.make_async_copy(k2_hbm, k2_ref, insem.at[2]))
    loads.append(pltpu.make_async_copy(k3_hbm, k3_ref, insem.at[3]))
    for load in loads:
        load.start()
    barrier = pltpu.get_barrier_semaphore()
    for d in range(1, 16):
        pl.semaphore_signal(barrier, inc=1, device_id=in_plane(d), device_id_type=MESH)
    for d in range(1, 8):
        pl.semaphore_signal(barrier, inc=1, device_id=in_column(d), device_id_type=MESH)

    for p in range(OWN):
        loads[p].wait()
        values = x_ref[p]
        summed = jnp.sum(values * values, axis=-1, keepdims=True) + norm_eps
        pa_ref[p] = (values * lax.rsqrt(summed)).astype(BF16)

    pl.semaphore_wait(barrier, 22)

    kc, kp = rep // 2, rep % 2
    local = pltpu.make_async_copy(pa_ref.at[kp], pb_ref.at[chip], lsem.at[0])

    def own_lanes(to, m):
        return pl.ds(pl.multiple_of(to * 1024 + m * 512, 512), 512)

    def to_other(n, lanes):
        return pltpu.make_async_remote_copy(
            src_ref=pa_ref.at[kp, :, :, lanes],
            dst_ref=pb_ref.at[chip, :, :, lanes],
            send_sem=hs.at[n],
            recv_sem=hr.at[n],
            device_id=(other, rep),
            device_id_type=MESH,
        )

    sent = [to_other(0, own_lanes(1 - core, 0)), to_other(1, own_lanes(1 - core, 1))]
    sent.append(to_other(2, pl.ds(pl.multiple_of(core * 1024, 1024), 1024)))
    got = [to_other(0, own_lanes(core, 0)), to_other(1, own_lanes(core, 1))]
    got.append(to_other(2, pl.ds(pl.multiple_of((1 - core) * 1024, 1024), 1024)))

    def piece(block, m, half):
        if half is None:
            lanes = pl.ds(pl.multiple_of(core * 1024 + m * 512, 512), 512)
        else:
            lanes = pl.ds(pl.multiple_of(core * 1024 + m * 512 + half * 256, 256), 256)
        return pb_ref.at[block, :, :, lanes]

    def ring(m, index, first, du, along):
        base = (m * 5 + index) * 4
        axis = first if along == 0 else 1 - first

        def block(d):
            return chip_at(first, d, 0) if along == 0 else chip_at(first, du, d)

        def copy(slot, source, d, half, prepared=False):
            ref = piece(source, m, half)
            return pltpu.make_async_remote_copy(
                src_ref=pa_ref.at[kp, :, :, own_lanes(core, m)] if prepared else ref,
                dst_ref=ref,
                send_sem=ssem.at[base + slot],
                recv_sem=rsem.at[base + slot],
                device_id=(shifted(axis, d), rep),
                device_id_type=MESH,
            )

        return dict(
            first_plus=copy(0, block(0), 1, None, True),
            first_minus=copy(1, block(0), -1, None, True),
            send_plus=copy(0, block(0), 1, None),
            send_minus=copy(1, block(0), -1, None),
            fwd_plus=copy(2, block(-1), 1, 0),
            fwd_minus=copy(3, block(1), -1, 1),
            from_minus=copy(0, block(-1), 1, None),
            from_plus=copy(1, block(1), -1, None),
            far_a=copy(2, block(2), 1, 0),
            far_b=copy(3, block(2), -1, 1),
            block=block,
        )

    crossings = []

    def cross(m, block):
        n = len(crossings)
        ref = piece(block, m, None)
        copy = pltpu.make_async_remote_copy(
            src_ref=ref,
            dst_ref=ref,
            send_sem=dssem.at[n],
            recv_sem=drsem.at[n],
            device_id=(other, rep),
            device_id_type=MESH,
        )
        copy.start()
        lanes = pl.ds(pl.multiple_of((1 - core) * 1024 + m * 512, 512), 512)
        theirs = pb_ref.at[block, :, :, lanes]
        arriving = pltpu.make_async_remote_copy(
            src_ref=theirs,
            dst_ref=theirs,
            send_sem=dssem.at[n],
            recv_sem=drsem.at[n],
            device_id=(other, rep),
            device_id_type=MESH,
        )
        crossings.append((copy, arriving))

    def c_copy(d, at):
        return pltpu.make_async_remote_copy(
            src_ref=call_ref.at[at],
            dst_ref=call_ref.at[at],
            send_sem=csem.at[d - 1],
            recv_sem=crsem.at[d - 1],
            device_id=(owner, (rep + d) % 4),
            device_id_type=MESH,
        )

    def make_pairs():
        by_row = ones_where(iota((VIDEOS, VIDEOS), 0) == vrows_ref[...])
        videos = iota((VIDEOS, 512), 0)
        row_a = dot(by_row, ones_where(videos == pairs_ref[0:1, :]), 1, 0)
        row_b = dot(by_row, ones_where(videos == pairs_ref[1:2, :]), 1, 0)
        hots_ref[0] = row_a.astype(BF16)
        hots_ref[1] = row_b.astype(BF16)
        call_ref[rep] = dot_exact(row_a * cot_ref[...], row_b.astype(BF16), 1)
        for d in (1, 2, 3):
            c_copy(d, rep).start()

    def make_weights():
        loads[2].wait()
        loads[3].wait()
        k1 = jnp.concatenate([k1_ref[n // 3, n % 3] for n in range(9)], axis=0)
        tiled = dot_exact(k1, ones_where(iota((32, 512), 1) % 32 == iota((32, 512), 0)))
        at = iota((144, 512), 0)
        w1 = jnp.zeros((144, 512), F32)
        for ti in range(3):
            for tj in range(3):
                w1 = jnp.where(at == tap_rows(ti, tj), tiled[ti * 3 + tj : ti * 3 + tj + 1], w1)
        w1_ref[...] = w1
        w2_ref[...] = jnp.zeros((512, 256), F32)
        for ti in range(3):
            for tj in range(3):
                for pi in range(2):
                    for pj in range(2):
                        row = ((pi + ti) * 4 + pj + tj) * 32
                        col = (pi * 2 + pj) * 64
                        w2_ref[row : row + 32, col : col + 64] = k2_ref[ti * 3 + tj]

    def frame_rows(shape):
        n = lane_of(shape)
        return ((n % 16) // 4) * 80 + (n // 144) * 36 + ((n % 144) // 16) * 4 + n % 4

    def make_own():
        chosen = ones_where(frame_rows((1, ROWS)) - rep * 80 == iota((80, ROWS), 0))
        for n in range(4):
            v = x_ref[:, :, :, n * 512 : n * 512 + 512].reshape(ROWS, 512)
            high = v.astype(BF16)
            rest = v - high.astype(F32)
            mid = rest.astype(BF16)
            low = (rest - mid.astype(F32)).astype(BF16)
            own_ref[:, n * 512 : n * 512 + 512] = (
                dot(chosen, high, 1, 0) + dot(chosen, mid, 1, 0) + dot(chosen, low, 1, 0)
            )

    offsets = (0, -1, 1, 2)
    ring1 = [ring(m, 0, m, 0, 0) for m in range(2)]
    ring2 = [{du: ring(m, 1 + n, m, du, 1) for n, du in enumerate(offsets)} for m in range(2)]

    def begin(r):
        r["send_plus"].start()
        r["send_minus"].start()

    @pl.when(core == kc)
    def _():
        sent[0].start()
        sent[1].start()
        for r in (ring1[0], ring1[1], ring2[0][0], ring2[1][0]):
            r["first_plus"].start()
            r["first_minus"].start()
        local.start()
        sent[2].start()

    @pl.when(core != kc)
    def _():
        for m in range(2):
            got[m].wait_recv()
            begin(ring1[m])
            begin(ring2[m][0])

    for d, arrive, forward in ((-1, "from_minus", "fwd_plus"), (1, "from_plus", "fwd_minus")):
        for m in range(2):
            ring1[m][arrive].wait_recv()
            ring1[m][forward].start()
            begin(ring2[m][d])
            cross(m, ring1[m]["block"](d))
    for m in range(2):
        ring1[m]["far_a"].wait_recv()
        ring1[m]["far_b"].wait_recv()
        begin(ring2[m][2])
        cross(m, ring1[m]["block"](2))
    beside = {0: make_pairs, -1: make_weights, 1: make_own}
    for du in offsets:
        for d, arrive, forward in ((-1, "from_minus", "fwd_plus"), (1, "from_plus", "fwd_minus")):
            for m in range(2):
                r = ring2[m][du]
                r[arrive].wait_recv()
                r[forward].start()
                cross(m, r["block"](d))
        if du in beside:
            beside[du]()
    for du in offsets:
        for m in range(2):
            r = ring2[m][du]
            r["far_a"].wait_recv()
            r["far_b"].wait_recv()
            cross(m, r["block"](2))

    for d in (1, 2, 3):
        c_copy(d, (rep + 4 - d) % 4).wait_recv()
    cots = (call_ref[0] + call_ref[1] + call_ref[2] + call_ref[3]) * loss_scale
    by_row = ones_where(iota((VIDEOS, VIDEOS), 0) == vrows_ref[...])
    lengths = dot(jnp.broadcast_to(counts_ref[...], (8, VIDEOS)).astype(F32).astype(BF16), by_row, 1, 1)
    lengths_half = lengths.astype(BF16)
    at = iota((VIDEOS, LANES), 0)
    lane = iota((1, LANES), 1)
    len_a = dot(lengths_half, ones_where(at == 2 * owner + lane // 256), 1, 0)[0:1]
    pick_b = ones_where(at == 4 * ((lane % 64) // 4) + rep)
    len_b = dot(lengths_half, pick_b, 1, 0)[0:1]
    ok_a = ((lane // 64) % 4 * 4).astype(F32) < len_a
    ok_b = (lane % 4 * 4).astype(F32) < len_b
    inv_a = 1.0 / quad_sum(jnp.where(ok_a, 1.0, 0.0), 64)
    inv_b = 1.0 / quad_sum(jnp.where(ok_b, 1.0, 0.0), 1)
    mine = iota((8, VIDEOS), 1) == 2 * owner + iota((8, VIDEOS), 0) % 2
    mine = ones_where(mine)
    high = cots.astype(BF16)
    rest = cots - high.astype(F32)
    mid = rest.astype(BF16)
    low = (rest - mid.astype(F32)).astype(BF16)
    cot = []
    for cb in (0, 1):
        c_rows = dot(mine, high, 1, cb) + dot(mine, mid, 1, cb) + dot(mine, low, 1, cb)
        spread = dot_exact(c_rows, pick_b)
        cot.append(jnp.where(lane < 256, spread[0:1], spread[1:2]))
    frames_b = iota((1, 256), 1)
    len_vb = dot(lengths_half, ones_where(iota((VIDEOS, 256), 0) == 4 * (frames_b // 16) + rep), 1, 0)[0:1]
    valid_b = (frames_b % 16).astype(F32) < len_vb
    rows_32 = iota((32, VIDEOS), 0)
    len_va = jnp.sum(
        jnp.where(iota((32, VIDEOS), 1) == 2 * owner + rows_32 // 16, jnp.broadcast_to(lengths[0:1], (32, VIDEOS)), 0.0),
        axis=1,
        keepdims=True,
    )
    valid = ((iota((32, 256), 0) % 16).astype(F32) < len_va) & valid_b

    for copy, arriving in crossings:
        arriving.wait_recv()

    @pl.when(core == kc)
    def _():
        local.wait()

    @pl.when(core != kc)
    def _():
        got[2].wait_recv()

    pa = pa_ref[...].reshape(ROWS, WIDTH)
    sum1 = jnp.zeros((ROWS, 256), F32)
    fm2 = jnp.zeros((32, 256), F32)
    for s in range(REGIONS):
        pbs = pb_ref[:, s].reshape(SEEN * FRAMES, WIDTH)
        e = jnp.exp(dot(pa, pbs, 1, 1) * (1.0 / region_temp))
        e_ref[s] = e
        sum1 = sum1 + e
        sum2 = jnp.sum(e.reshape(OWN, REGIONS, FRAMES, 256), axis=1).reshape(32, 256)
        q2_ref[s] = sum2
        fm2 = fm2 + jnp.log(sum2)
    q1_ref[...] = sum1
    fm1 = jnp.sum(jnp.log(sum1).reshape(OWN, REGIONS, FRAMES, 256), axis=1).reshape(32, 256)
    scale = region_temp / REGIONS
    fm = jnp.concatenate([jnp.where(valid, fm1 * scale, 0.0), jnp.where(valid, fm2 * scale, 0.0)], axis=0)
    spot = iota((256, 256), 0)
    perm = ones_where((spot % 4) * 64 + (spot // 16) * 4 + (spot % 16) // 4 == iota((256, 256), 1))
    fm_ref[...] = dot_exact(fm, perm)
    for g in range(2):
        for p in range(OWN):
            for i4 in range(4):
                base = g * 32 + p * 16 + i4 * 4
                at = g * LANES + p * 256 + i4 * 64
                for pj in range(4):
                    if g == 0:
                        for pi in range(4):
                            x0_ref[pi * 4 + pj : pi * 4 + pj + 1, at : at + 64] = fm_ref[
                                base + pi : base + pi + 1, pj * 64 : pj * 64 + 64
                            ]
                    else:
                        x0_ref[pj * 4 : pj * 4 + 4, at : at + 64] = fm_ref[base : base + 4, pj * 64 : pj * 64 + 64]

    x0 = x0_ref[...]
    xcat = split2(jnp.concatenate([block_shift(x0, du, dv) for du, dv in SHIFTS], axis=0))
    w1 = split2(w1_ref[...])
    stacked = jnp.concatenate([xcat[0], xcat[0], xcat[1]], axis=0)
    h1, ds1 = silu_pair(dot(jnp.concatenate([w1[0], w1[1], w1[0]], axis=0), stacked, 0, 0))
    pooled1 = []
    for qi in range(2):
        for qj in range(2):
            parts = [
                h1[((2 * qi + a) * 4 + 2 * qj + b) * 32 : ((2 * qi + a) * 4 + 2 * qj + b) * 32 + 32]
                for a in range(2)
                for b in range(2)
            ]
            pooled1.append((parts[0] + parts[1] + parts[2] + parts[3]) * 0.25)
    h1cat = split2(
        jnp.concatenate(
            [block_shift(pooled1[qi * 2 + qj], du, dv) for qi, du in EXT2 for qj, dv in EXT2], axis=0
        )
    )
    w2 = split2(w2_ref[...])
    h2, ds2 = silu_pair(dot3(w2, h1cat, 0, 0))
    pooled2 = (h2[0:64] + h2[64:128] + h2[128:192] + h2[192:256]) * 0.25
    h2cat = split2(jnp.concatenate([block_shift(pooled2, du, dv) for du, dv in SHIFTS], axis=0))
    w3 = split2(k3_ref[...])
    both = dot(jnp.concatenate([w3[0], w3[1]], axis=1), h2cat[0], 0, 0)
    h3, ds3 = silu_pair(both[:C3] + both[C3:] + dot(w3[0], h2cat[1], 0, 0))
    kl = jnp.sum(jnp.where(iota((C3, C3), 0) == iota((C3, C3), 1), kl_ref[...], 0.0), axis=1, keepdims=True)
    out = jnp.tanh(jnp.sum(h3 * kl, axis=0, keepdims=True))

    dz = []
    for g in range(2):
        o = out[:, g * LANES : (g + 1) * LANES]
        rows_ok, inv = ((ok_a, inv_a), (ok_b, inv_b))[g]
        weighted = jnp.where(ok_a & ok_b, jnp.exp(o * (1.0 / region_temp)), 0.0)
        row_sums = quad_sum(weighted, 1 if g == 0 else 64) + jnp.where(rows_ok, 0.0, 1.0)
        if g == 0:
            best = jnp.where(rows_ok, region_temp * jnp.log(row_sums), 0.0)
            ps = quad_sum(best, 64) * inv
        dout = cot[g] * inv * weighted / row_sums
        dz.append(dout * (1.0 - o * o))
    dz = jnp.concatenate(dz, axis=1)

    def scatter_copy(to):
        return pltpu.make_async_remote_copy(
            src_ref=acc_ref.at[pl.ds(pl.multiple_of(to * 48, 48), 48)],
            dst_ref=part_a.at[chip],
            send_sem=sa.at[to],
            recv_sem=ra.at[chip],
            device_id=(to * 2 + core, rep),
            device_id_type=MESH,
        )

    def scatter_start(to):
        @pl.when(chip != to)
        def _():
            scatter_copy(to).start()

    def scatter_arrives(source):
        return pltpu.make_async_remote_copy(
            src_ref=part_a.at[source],
            dst_ref=part_a.at[source],
            send_sem=sa.at[source],
            recv_sem=ra.at[source],
            device_id=(((chip + 1) % 16) * 2 + core, rep),
            device_id_type=MESH,
        )

    def column_copy(d):
        return pltpu.make_async_remote_copy(
            src_ref=part_b.at[place],
            dst_ref=part_b.at[place],
            send_sem=sb.at[d - 1],
            recv_sem=rb.at[d - 1],
            device_id=in_column(d),
            device_id_type=MESH,
        )

    def gather_copy(d, at):
        return pltpu.make_async_remote_copy(
            src_ref=all_ref.at[pl.ds(pl.multiple_of(at * 48, 48), 48)],
            dst_ref=all_ref.at[pl.ds(pl.multiple_of(at * 48, 48), 48)],
            send_sem=sc.at[d - 1],
            recv_sem=rc.at[d - 1],
            device_id=in_plane(d),
            device_id_type=MESH,
        )

    def first(pair):
        return pair[0][:, :LANES], pair[1][:, :LANES]

    lane = lane_of((1, 128))
    row = jnp.where(lane % 4 == rep, jnp.concatenate([ps[:, 0:64], ps[:, 256:320]], axis=1), 0.0)
    at = lax.broadcasted_iota(jnp.int32, (32, 128), 0)
    acc_ref[ROW_PS : ROW_PS + 32] = jnp.where(at == owner, row, 0.0)
    dz_first = jnp.broadcast_to(dz[:, :LANES], (8, LANES))
    gl = dot3(split2(dz_first), split2(h3[:, :LANES]), 1, 1)
    dpre3 = (dz * kl * ds3).astype(BF16)
    acc_ref[0:576] = dot2(first(h2cat), dpre3[:, :LANES], 1, 1) * (1.0 / loss_scale)
    for to in range(12):
        scatter_start(to)
    dh2cat = dot(jnp.concatenate([w3[0], w3[1]], axis=1), jnp.concatenate([dpre3, dpre3], axis=0), 1, 0)
    dpool2 = jnp.zeros((64, 2 * LANES), F32)
    for n, (du, dv) in enumerate(SHIFTS):
        dpool2 = dpool2 + block_shift(dh2cat[n * 64 : n * 64 + 64], -du, -dv)
    dpool2 = dpool2 * 0.25
    dpre2 = (jnp.concatenate([dpool2, dpool2, dpool2, dpool2], axis=0) * ds2).astype(BF16)
    g2 = dot2(first(h1cat), dpre2[:, :LANES], 1, 1)
    for ti in range(3):
        for tj in range(3):
            total = jnp.zeros((32, 64), F32)
            for pi in range(2):
                for pj in range(2):
                    row = ((pi + ti) * 4 + pj + tj) * 32
                    col = (pi * 2 + pj) * 64
                    total = total + g2[row : row + 32, col : col + 64]
            total = total * (1.0 / loss_scale)
            for half in range(2):
                n = (ti * 3 + tj) * 2 + half
                at = ROW_TWO + (n % 9) * 16
                acc_ref[at : at + 16, (n // 9) * 64 : (n // 9) * 64 + 64] = total[half * 16 : half * 16 + 16]
    dh1cat = dot2(w2, dpre2, 1, 0)
    dpool1 = [jnp.zeros((32, 2 * LANES), F32) for _ in range(4)]
    n = 0
    for qi, du in EXT2:
        for qj, dv in EXT2:
            dpool1[qi * 2 + qj] = dpool1[qi * 2 + qj] + block_shift(dh1cat[n * 32 : n * 32 + 32], -du, -dv)
            n += 1
    dpool1 = [d * 0.25 for d in dpool1]
    dpre1 = (
        jnp.concatenate([dpool1[(pi // 2) * 2 + pj // 2] for pi in range(4) for pj in range(4)], axis=0) * ds1
    ).astype(BF16)
    g1 = dot(jnp.concatenate(first(xcat), axis=0), dpre1[:, :LANES], 1, 1)
    g1 = g1[:144] + g1[144:]
    at = iota((144, 512), 0)
    rows = []
    for ti in range(3):
        for tj in range(3):
            v = jnp.sum(jnp.where(at == tap_rows(ti, tj), g1, 0.0), axis=0, keepdims=True)
            v = v[:, 0:128] + v[:, 128:256] + v[:, 256:384] + v[:, 384:512]
            v = v + pltpu.roll(v, 64, 1)
            rows.append(v + pltpu.roll(v, 32, 1))
    rows.append(gl[0:1])
    rows.append(jnp.zeros((6, 128), F32))
    acc_ref[ROW_ONE : ROW_ONE + 16] = jnp.concatenate(rows, axis=0) * (1.0 / loss_scale)
    for to in range(12, 16):
        scatter_start(to)
    dxcat = dot(jnp.concatenate([w1[0], w1[1]], axis=0), dpre1, 1, 0)
    dxcat = dxcat[:144] + dxcat[144:]
    dx0 = jnp.zeros((16, 2 * LANES), F32)
    for n, (du, dv) in enumerate(SHIFTS):
        dx0 = dx0 + block_shift(dxcat[n * 16 : n * 16 + 16], -du, -dv)
    x0_ref[...] = dx0
    for g in range(2):
        for p in range(OWN):
            for i4 in range(4):
                base = g * 32 + p * 16 + i4 * 4
                at = g * LANES + p * 256 + i4 * 64
                for pj in range(4):
                    if g == 0:
                        for pi in range(4):
                            fm_ref[base + pi : base + pi + 1, pj * 64 : pj * 64 + 64] = x0_ref[
                                pi * 4 + pj : pi * 4 + pj + 1, at : at + 64
                            ]
                    else:
                        fm_ref[base : base + 4, pj * 64 : pj * 64 + 64] = x0_ref[pj * 4 : pj * 4 + 4, at : at + 64]
    dfm = dot_exact(fm_ref[...], perm, 1)
    dfm1 = jnp.where(valid, dfm[:32], 0.0) * (1.0 / REGIONS)
    dfm2 = jnp.where(valid, dfm[32:], 0.0) * (1.0 / REGIONS)

    part_a[chip] = acc_ref[pl.ds(pl.multiple_of(chip * 48, 48), 48)]
    for d in range(1, 16):
        scatter_arrives((chip + 16 - d) % 16).wait_recv()
    total = part_a[0]
    for n in range(1, 16):
        total = total + part_a[n]
    part_b[place] = total
    for d in range(1, 8):
        column_copy(d).start()

    sum1 = q1_ref[...].reshape(OWN, REGIONS, FRAMES, 256)
    q1 = dfm1.reshape(OWN, 1, FRAMES, 256) / sum1
    rowperm = ones_where(frame_rows((1, ROWS)) == iota((320, ROWS), 0))
    for s in range(REGIONS):
        q2 = (dfm2 / q2_ref[s]).reshape(OWN, 1, FRAMES, 256)
        grad = (e_ref[s].reshape(OWN, REGIONS, FRAMES, 256) * (q1 + q2)).reshape(ROWS, 256).astype(BF16)
        grad_ref[s] = dot(rowperm, grad, 1, 0).astype(BF16)

    def way(n):
        return 1 if n < 2 else -1

    def rep_copy(kind, n):
        d = -way(n) if kind == 2 else way(n)
        of = (rep + 2) % 4 if kind == 0 else (rep + d + 4) % 4
        return pltpu.make_async_remote_copy(
            src_ref=send_ref.at[of, :, pl.ds(n * CHUNK, CHUNK)],
            dst_ref=recv_ref.at[kind, :, pl.ds(n * CHUNK, CHUNK)],
            send_sem=rs.at[n * 3 + kind],
            recv_sem=rr.at[n * 3 + kind],
            device_id=(owner, (rep + d + 4) % 4),
            device_id_type=MESH,
        )

    order = (0, 2, 1, 3)
    for n in order:
        cols = slice(n * CHUNK, (n + 1) * CHUNK)
        product = jnp.zeros((320, CHUNK), F32)
        for s in range(REGIONS):
            pbs = pb_ref[:, s, :, cols].reshape(SEEN * FRAMES, CHUNK)
            product = product + dot(grad_ref[s], pbs, 1, 0)
        product = product.reshape(SIDE, 80, CHUNK)
        rg_ref[:, :, cols] = product
        send_ref[:, :, cols] = product.astype(BF16)
        rep_copy(0, n).start()
        rep_copy(2, n).start()
        if n == 2:
            for d in range(1, 8):
                pltpu.make_async_remote_copy(
                    src_ref=part_b.at[(place + 8 - d) % 8],
                    dst_ref=part_b.at[(place + 8 - d) % 8],
                    send_sem=sb.at[d - 1],
                    recv_sem=rb.at[d - 1],
                    device_id=in_column(d),
                    device_id_type=MESH,
                ).wait_recv()
            total = part_b[0]
            for q in range(1, 8):
                total = total + part_b[q]
            all_ref[pl.ds(pl.multiple_of(chip * 48, 48), 48)] = total
            for d in range(1, 16):
                gather_copy(d, chip).start()
    for n in order:
        cols = slice(n * CHUNK, (n + 1) * CHUNK)
        of = (rep + way(n) + 4) % 4
        rep_copy(0, n).wait_recv()
        send_ref[of, :, cols] = (rg_ref[of, :, cols] + recv_ref[0, :, cols].astype(F32)).astype(BF16)
        rep_copy(1, n).start()
    for d in range(1, 16):
        gather_copy(d, (chip + 16 - d) % 16).wait_recv()
    table = all_ref[ROW_PS:ROW_ALL]
    found = jnp.zeros((1, 512), F32)
    for p in range(OWN):
        left = dot(ones_where(iota((32, VIDEOS), 1) == 2 * iota((32, VIDEOS), 0) + p), hots_ref[0], 1, 0)
        value = dot_exact(table[:, p * 64 : p * 64 + 64], hots_ref[1])
        found = found + jnp.sum(left * value, axis=0, keepdims=True)
    ps_ref[...] = found
    own = own_ref[...]
    inverse = lax.rsqrt(jnp.sum(own * own, axis=1, keepdims=True) + norm_eps)
    along = jnp.zeros((80, 1), F32)
    for n in order:
        cols = slice(n * CHUNK, (n + 1) * CHUNK)
        rep_copy(2, n).wait_recv()
        rep_copy(1, n).wait_recv()
        total = rg_ref[rep, :, cols] + recv_ref[2, :, cols].astype(F32) + recv_ref[1, :, cols].astype(F32)
        rg_ref[rep, :, cols] = total
        along = along + jnp.sum(own_ref[:, cols] * total, axis=1, keepdims=True)
    back = along * inverse * inverse * inverse
    for n in range(CHUNKS):
        cols = slice(n * CHUNK, (n + 1) * CHUNK)
        result = rg_ref[rep, :, cols] * inverse - own_ref[:, cols] * back
        for q in range(18):
            fg_ref[q, :, cols] = result[q * 4 : q * 4 + 4]

    for copy, arriving in crossings:
        copy.wait_send()
    for m in range(2):
        for r in [ring1[m]] + [ring2[m][du] for du in offsets]:
            for name in ("send_plus", "send_minus", "fwd_plus", "fwd_minus"):
                r[name].wait_send()

    @pl.when(core == kc)
    def _():
        for copy in sent:
            copy.wait_send()

    for d in (1, 2, 3):
        c_copy(d, rep).wait_send()
        for n in range(CHUNKS):
            rep_copy(d - 1, n).wait_send()
    for d in range(1, 16):
        scatter_copy((chip + d) % 16).wait_send()
        gather_copy(d, chip).wait_send()
    for d in range(1, 8):
        column_copy(d).wait_send()


def whole(*args):
    return pl.pallas_call(
        whole_kernel,
        name="training_step",
        out_shape=(
            jax.ShapeDtypeStruct((OWN * REGIONS, 4, WIDTH), F32),
            jax.ShapeDtypeStruct((1, 512), F32),
            jax.ShapeDtypeStruct((ROW_ALL, 128), F32),
        ),
        in_specs=[ANY_SPEC] + [VMEM_SPEC] * 5 + [ANY_SPEC] * 2 + [VMEM_SPEC],
        out_specs=(VMEM_SPEC,) * 3,
        scratch_shapes=[
            pltpu.VMEM((OWN, REGIONS, FRAMES, WIDTH), F32),
            pltpu.VMEM((9, 32, 64), F32),
            pltpu.VMEM((576, C3), F32),
            pltpu.VMEM((OWN, REGIONS, FRAMES, WIDTH), BF16),
            pltpu.VMEM((SEEN, REGIONS, FRAMES, WIDTH), BF16),
            pltpu.VMEM((SIDE, VIDEOS, VIDEOS), F32),
            pltpu.VMEM((2, VIDEOS, 512), BF16),
            pltpu.VMEM((144, 512), F32),
            pltpu.VMEM((512, 256), F32),
            pltpu.VMEM((80, WIDTH), F32),
            pltpu.VMEM((REGIONS, ROWS, 256), F32),
            pltpu.VMEM((ROWS, 256), F32),
            pltpu.VMEM((REGIONS, 32, 256), F32),
            pltpu.VMEM((64, 256), F32),
            pltpu.VMEM((16, 2 * LANES), F32),
            pltpu.VMEM((REGIONS, 320, 256), BF16),
            pltpu.VMEM((ROW_ALL, 128), F32),
            pltpu.VMEM((SIDE, 80, WIDTH), F32),
            pltpu.VMEM((SIDE, 80, WIDTH), BF16),
            pltpu.VMEM((3, 80, WIDTH), BF16),
            pltpu.VMEM((16, 48, 128), F32),
            pltpu.VMEM((8, 48, 128), F32),
        ]
        + [
            pltpu.SemaphoreType.DMA((n,))
            for n in (40, 40, 30, 30, 3, 3, 1, 4, 3, 3, 3 * CHUNKS, 3 * CHUNKS, 16, 16, 7, 7, 15, 15)
        ],
        compiler_params=pltpu.CompilerParams(
            collective_id=0, has_side_effects=True, vmem_limit_bytes=58 * 2**20
        ),
    )(*args)


def outputs_kernel(fg_in, ps_in, all_in, ps_ref, fg_ref, g1_ref, g2_ref, g3_ref, gl_ref):
    fg_ref[...] = fg_in[...]
    ps_ref[...] = ps_in[...]
    g3_ref[...] = all_in[0:ROW_TWO]
    for n in range(18):
        at = ROW_TWO + (n % 9) * 16
        g2_ref[n // 2, (n % 2) * 16 : (n % 2) * 16 + 16, :] = all_in[at : at + 16, (n // 9) * 64 : (n // 9) * 64 + 64]
    for n in range(9):
        g1_ref[n // 3, n % 3] = all_in[ROW_ONE + n : ROW_ONE + n + 1, 0:32]
    gl_ref[...] = all_in[ROW_ONE + 9 : ROW_ONE + 10]


def outputs(fg, ps, summed):
    return pl.pallas_call(
        outputs_kernel,
        name="outputs",
        out_shape=(
            jax.ShapeDtypeStruct((1, 512), F32),
            jax.ShapeDtypeStruct((OWN * REGIONS, 4, WIDTH), F32),
            jax.ShapeDtypeStruct((3, 3, 1, 32), F32),
            jax.ShapeDtypeStruct((9, 32, 64), F32),
            jax.ShapeDtypeStruct((576, C3), F32),
            jax.ShapeDtypeStruct((1, C3), F32),
        ),
        in_specs=[VMEM_SPEC] * 3,
        out_specs=(VMEM_SPEC,) * 6,
    )(fg, ps, summed)


def local(
    features, frame_counts, video_rows, pair_list, pair_cotangent, kernel_one, kernel_two, kernel_three, kernel_last
):
    fg, ps, summed = whole(
        features.transpose(0, 2, 1, 3),
        frame_counts.reshape(1, VIDEOS),
        video_rows.reshape(1, VIDEOS),
        pair_list.T,
        pair_cotangent.reshape(1, 512),
        kernel_one,
        kernel_two.reshape(9, 32, 64),
        kernel_three.reshape(576, C3),
        kernel_last.reshape(1, C3),
    )
    ps, fg, g1, g2, g3, gl = outputs(fg, ps, summed)
    return (
        ps.reshape(512),
        fg.reshape(OWN, REGIONS, 4, WIDTH).transpose(0, 2, 1, 3),
        g1,
        g2.reshape(3, 3, 32, 64),
        g3.reshape(3, 3, 64, C3),
        gl.reshape(C3),
    )


def solution(mesh):
    placed = (P("owner", None, None, None), P(), P(), P("rep", None), P("rep"), P(), P(), P(), P())
    return jax.shard_map(
        local,
        mesh=mesh,
        in_specs=placed,
        out_specs=(P("rep"), P("owner", "rep", None, None), P(), P(), P(), P()),
        check_vma=False,
    )
```

```python
import jax
import jax.numpy as jnp
from jax import lax
from jax.experimental import pallas as pl
from jax.experimental.pallas import tpu as pltpu
from jax.sharding import PartitionSpec as P

MESH = pl.DeviceIdType.MESH
VMEM_SPEC = pl.BlockSpec(memory_space=pltpu.VMEM)
ANY_SPEC = pl.BlockSpec(memory_space=pl.ANY)
F32 = jnp.float32
BF16 = jnp.bfloat16

REGIONS = 9
FRAMES = 16
WIDTH = 2048
VIDEOS = 64
SIDE = 4
OWN = 2
SEEN = 16
ROWS = OWN * REGIONS * FRAMES
LANES = OWN * SEEN * 16

ROW_TWO = 576
ROW_ONE = 720
ROW_PS = 736
ROW_ALL = 768

region_temp = 0.1
loss_scale = 131072.0
norm_eps = 1e-06
C3 = 128


CHUNKS = 4
CHUNK = WIDTH // CHUNKS


def split2(v):
    high = v.astype(BF16)
    return high, (v - high.astype(F32)).astype(BF16)


def dot(a, b, ca, cb):
    return lax.dot_general(a, b, (((ca,), (cb,)), ((), ())), preferred_element_type=F32)


def dot3(a, b, ca, cb):
    (ah, al), (bh, bl) = a, b
    return dot(ah, bh, ca, cb) + dot(ah, bl, ca, cb) + dot(al, bh, ca, cb)


def dot2(a, b, ca, cb):
    return dot(a[0], b, ca, cb) + dot(a[1], b, ca, cb)


def dot_exact(v, chosen, cb=0):
    high = v.astype(BF16)
    rest = v - high.astype(F32)
    mid = rest.astype(BF16)
    low = (rest - mid.astype(F32)).astype(BF16)
    return dot(high, chosen, 1, cb) + dot(mid, chosen, 1, cb) + dot(low, chosen, 1, cb)


def lane_of(shape):
    return lax.broadcasted_iota(jnp.int32, shape, len(shape) - 1)


def moved(v, di, dj):
    if di == 0 and dj == 0:
        return v
    out = pltpu.roll(v, (-(di * 64 + dj)) % LANES, 1)
    lane = lane_of((1, LANES))
    i4, j4 = (lane // 64) % 4, lane % 4
    ok = (i4 + di >= 0) & (i4 + di < 4) & (j4 + dj >= 0) & (j4 + dj < 4)
    return jnp.where(ok, out, 0.0)


def block_shift(v, du, dv):
    return jnp.concatenate([moved(v[:, :LANES], du, dv), moved(v[:, LANES:], dv, du)], axis=1)


def quad_sum(v, stride):
    lane = lane_of((1, LANES))
    for step in (stride, 2 * stride):
        low = (lane // step) % 2 == 0
        v = v + jnp.where(low, pltpu.roll(v, LANES - step, 1), pltpu.roll(v, step, 1))
    return v


def silu_pair(v):
    s = 1.0 / (1.0 + jnp.exp(-v))
    return v * s, s * (1.0 + v * (1.0 - s))


def iota(shape, axis):
    return lax.broadcasted_iota(jnp.int32, shape, axis)


def ones_where(condition):
    return jnp.where(condition, 1.0, 0.0).astype(BF16)


def tap_rows(ti, tj):
    plane = lane_of((1, 512)) // 32
    ei, ej = plane // 4 + ti + 3, plane % 4 + tj + 3
    return ((ei // 4) * 3 + ej // 4) * 16 + (ei % 4) * 4 + ej % 4


SHIFTS = [(du, dv) for du in (-1, 0, 1) for dv in (-1, 0, 1)]
EXT2 = [(1, -1), (0, 0), (1, 0), (0, 1)]


def whole_kernel(
    x_hbm, counts_ref, vrows_ref, pairs_ref, cot_ref, k1_ref, k2_hbm, k3_hbm, kl_ref,
    fg_ref, ps_ref, all_ref,
    x_ref, k2_ref, k3_ref, pa_ref, pb_ref, call_ref, hots_ref, w1_ref, w2_ref, own_ref,
    e_ref, q1_ref, q2_ref, fm_ref, x0_ref, grad_ref, acc_ref, rg_ref, send_ref, recv_ref, part_a, part_b,
    ssem, rsem, dssem, drsem, csem, crsem, lsem, insem, hs, hr, rs, rr, sa, ra, sb, rb, sc, rc,
):
    owner = lax.axis_index("owner")
    rep = lax.axis_index("rep")
    z, x, core = owner // 8, (owner // 2) % 4, owner % 2
    chip = owner // 2
    place = core * 4 + rep
    other = owner + 1 - 2 * core

    def in_plane(d):
        return (((chip + d) % 16) * 2 + core, rep)

    def in_column(d):
        to = (place + d) % 8
        return (chip * 2 + to // 4, to % 4)

    def shifted(axis, d):
        if axis == 0:
            return z * 8 + ((x + d + 4) % 4) * 2 + core
        return ((z + d + 4) % 4) * 8 + x * 2 + core

    def chip_at(first, du, dv):
        dx, dz = (du, dv) if first == 0 else (dv, du)
        return ((z + dz + 4) % 4) * 4 + (x + dx + 4) % 4

    loads = [pltpu.make_async_copy(x_hbm.at[p], x_ref.at[p], insem.at[p]) for p in range(OWN)]
    loads.append(pltpu.make_async_copy(k2_hbm, k2_ref, insem.at[2]))
    loads.append(pltpu.make_async_copy(k3_hbm, k3_ref, insem.at[3]))
    for load in loads:
        load.start()
    barrier = pltpu.get_barrier_semaphore()
    for axis in (0, 1):
        for d in (1, -1):
            pl.semaphore_signal(barrier, inc=1, device_id=(shifted(axis, d), rep), device_id_type=MESH)
    for d in range(1, 8):
        pl.semaphore_signal(barrier, inc=1, device_id=in_column(d), device_id_type=MESH)

    for p in range(OWN):
        loads[p].wait()
        values = x_ref[p]
        summed = jnp.sum(values * values, axis=-1, keepdims=True) + norm_eps
        pa_ref[p] = (values * lax.rsqrt(summed)).astype(BF16)

    pl.semaphore_wait(barrier, 11)

    kc, kp = rep // 2, rep % 2
    local = pltpu.make_async_copy(pa_ref.at[kp], pb_ref.at[chip], lsem.at[0])

    def own_lanes(to, m):
        return pl.ds(pl.multiple_of(to * 1024 + m * 512, 512), 512)

    def to_other(n, lanes):
        return pltpu.make_async_remote_copy(
            src_ref=pa_ref.at[kp, :, :, lanes],
            dst_ref=pb_ref.at[chip, :, :, lanes],
            send_sem=hs.at[n],
            recv_sem=hr.at[n],
            device_id=(other, rep),
            device_id_type=MESH,
        )

    sent = [to_other(0, own_lanes(1 - core, 0)), to_other(1, own_lanes(1 - core, 1))]
    sent.append(to_other(2, pl.ds(pl.multiple_of(core * 1024, 1024), 1024)))
    got = [to_other(0, own_lanes(core, 0)), to_other(1, own_lanes(core, 1))]
    got.append(to_other(2, pl.ds(pl.multiple_of((1 - core) * 1024, 1024), 1024)))

    def piece(block, m, half):
        if half is None:
            lanes = pl.ds(pl.multiple_of(core * 1024 + m * 512, 512), 512)
        else:
            lanes = pl.ds(pl.multiple_of(core * 1024 + m * 512 + half * 256, 256), 256)
        return pb_ref.at[block, :, :, lanes]

    def ring(m, index, first, du, along):
        base = (m * 5 + index) * 4
        axis = first if along == 0 else 1 - first

        def block(d):
            return chip_at(first, d, 0) if along == 0 else chip_at(first, du, d)

        def copy(slot, source, d, half, prepared=False):
            ref = piece(source, m, half)
            return pltpu.make_async_remote_copy(
                src_ref=pa_ref.at[kp, :, :, own_lanes(core, m)] if prepared else ref,
                dst_ref=ref,
                send_sem=ssem.at[base + slot],
                recv_sem=rsem.at[base + slot],
                device_id=(shifted(axis, d), rep),
                device_id_type=MESH,
            )

        return dict(
            first_plus=copy(0, block(0), 1, None, True),
            first_minus=copy(1, block(0), -1, None, True),
            send_plus=copy(0, block(0), 1, None),
            send_minus=copy(1, block(0), -1, None),
            fwd_plus=copy(2, block(-1), 1, 0),
            fwd_minus=copy(3, block(1), -1, 1),
            from_minus=copy(0, block(-1), 1, None),
            from_plus=copy(1, block(1), -1, None),
            far_a=copy(2, block(2), 1, 0),
            far_b=copy(3, block(2), -1, 1),
            block=block,
        )

    crossings = []

    def cross(m, block):
        n = len(crossings)
        ref = piece(block, m, None)
        copy = pltpu.make_async_remote_copy(
            src_ref=ref,
            dst_ref=ref,
            send_sem=dssem.at[n],
            recv_sem=drsem.at[n],
            device_id=(other, rep),
            device_id_type=MESH,
        )
        copy.start()
        lanes = pl.ds(pl.multiple_of((1 - core) * 1024 + m * 512, 512), 512)
        theirs = pb_ref.at[block, :, :, lanes]
        arriving = pltpu.make_async_remote_copy(
            src_ref=theirs,
            dst_ref=theirs,
            send_sem=dssem.at[n],
            recv_sem=drsem.at[n],
            device_id=(other, rep),
            device_id_type=MESH,
        )
        crossings.append((copy, arriving))

    def c_copy(d, at):
        return pltpu.make_async_remote_copy(
            src_ref=call_ref.at[at],
            dst_ref=call_ref.at[at],
            send_sem=csem.at[d - 1],
            recv_sem=crsem.at[d - 1],
            device_id=(owner, (rep + d) % 4),
            device_id_type=MESH,
        )

    def make_pairs():
        by_row = ones_where(iota((VIDEOS, VIDEOS), 0) == vrows_ref[...])
        videos = iota((VIDEOS, 512), 0)
        row_a = dot(by_row, ones_where(videos == pairs_ref[0:1, :]), 1, 0)
        row_b = dot(by_row, ones_where(videos == pairs_ref[1:2, :]), 1, 0)
        hots_ref[0] = row_a.astype(BF16)
        hots_ref[1] = row_b.astype(BF16)
        call_ref[rep] = dot_exact(row_a * cot_ref[...], row_b.astype(BF16), 1)
        for d in (1, 2, 3):
            c_copy(d, rep).start()

    def make_weights():
        loads[2].wait()
        loads[3].wait()
        k1 = jnp.concatenate([k1_ref[n // 3, n % 3] for n in range(9)], axis=0)
        tiled = dot_exact(k1, ones_where(iota((32, 512), 1) % 32 == iota((32, 512), 0)))
        at = iota((144, 512), 0)
        w1 = jnp.zeros((144, 512), F32)
        for ti in range(3):
            for tj in range(3):
                w1 = jnp.where(at == tap_rows(ti, tj), tiled[ti * 3 + tj : ti * 3 + tj + 1], w1)
        w1_ref[...] = w1
        w2_ref[...] = jnp.zeros((512, 256), F32)
        for ti in range(3):
            for tj in range(3):
                for pi in range(2):
                    for pj in range(2):
                        row = ((pi + ti) * 4 + pj + tj) * 32
                        col = (pi * 2 + pj) * 64
                        w2_ref[row : row + 32, col : col + 64] = k2_ref[ti * 3 + tj]

    def frame_rows(shape):
        n = lane_of(shape)
        return ((n % 16) // 4) * 80 + (n // 144) * 36 + ((n % 144) // 16) * 4 + n % 4

    def make_own():
        chosen = ones_where(frame_rows((1, ROWS)) - rep * 80 == iota((80, ROWS), 0))
        for n in range(4):
            v = x_ref[:, :, :, n * 512 : n * 512 + 512].reshape(ROWS, 512)
            high = v.astype(BF16)
            rest = v - high.astype(F32)
            mid = rest.astype(BF16)
            low = (rest - mid.astype(F32)).astype(BF16)
            own_ref[:, n * 512 : n * 512 + 512] = (
                dot(chosen, high, 1, 0) + dot(chosen, mid, 1, 0) + dot(chosen, low, 1, 0)
            )

    offsets = (0, -1, 1, 2)
    ring1 = [ring(m, 0, m, 0, 0) for m in range(2)]
    ring2 = [{du: ring(m, 1 + n, m, du, 1) for n, du in enumerate(offsets)} for m in range(2)]

    def begin(r):
        r["send_plus"].start()
        r["send_minus"].start()

    @pl.when(core == kc)
    def _():
        sent[0].start()
        sent[1].start()
        for r in (ring1[0], ring1[1], ring2[0][0], ring2[1][0]):
            r["first_plus"].start()
            r["first_minus"].start()
        local.start()
        sent[2].start()

    @pl.when(core != kc)
    def _():
        for m in range(2):
            got[m].wait_recv()
            begin(ring1[m])
            begin(ring2[m][0])

    for d, arrive, forward in ((-1, "from_minus", "fwd_plus"), (1, "from_plus", "fwd_minus")):
        for m in range(2):
            ring1[m][arrive].wait_recv()
            ring1[m][forward].start()
            begin(ring2[m][d])
            cross(m, ring1[m]["block"](d))
    for m in range(2):
        ring1[m]["far_a"].wait_recv()
        ring1[m]["far_b"].wait_recv()
        begin(ring2[m][2])
        cross(m, ring1[m]["block"](2))
    beside = {0: make_pairs, -1: make_weights, 1: make_own}
    for du in offsets:
        for d, arrive, forward in ((-1, "from_minus", "fwd_plus"), (1, "from_plus", "fwd_minus")):
            for m in range(2):
                r = ring2[m][du]
                r[arrive].wait_recv()
                r[forward].start()
                cross(m, r["block"](d))
        if du in beside:
            beside[du]()
    for du in offsets:
        for m in range(2):
            r = ring2[m][du]
            r["far_a"].wait_recv()
            r["far_b"].wait_recv()
            cross(m, r["block"](2))

    for d in (1, 2, 3):
        c_copy(d, (rep + 4 - d) % 4).wait_recv()
    cots = (call_ref[0] + call_ref[1] + call_ref[2] + call_ref[3]) * loss_scale
    by_row = ones_where(iota((VIDEOS, VIDEOS), 0) == vrows_ref[...])
    lengths = dot(jnp.broadcast_to(counts_ref[...], (8, VIDEOS)).astype(F32).astype(BF16), by_row, 1, 1)
    lengths_half = lengths.astype(BF16)
    at = iota((VIDEOS, LANES), 0)
    lane = iota((1, LANES), 1)
    len_a = dot(lengths_half, ones_where(at == 2 * owner + lane // 256), 1, 0)[0:1]
    pick_b = ones_where(at == 4 * ((lane % 64) // 4) + rep)
    len_b = dot(lengths_half, pick_b, 1, 0)[0:1]
    ok_a = ((lane // 64) % 4 * 4).astype(F32) < len_a
    ok_b = (lane % 4 * 4).astype(F32) < len_b
    inv_a = 1.0 / quad_sum(jnp.where(ok_a, 1.0, 0.0), 64)
    inv_b = 1.0 / quad_sum(jnp.where(ok_b, 1.0, 0.0), 1)
    mine = iota((8, VIDEOS), 1) == 2 * owner + iota((8, VIDEOS), 0) % 2
    mine = ones_where(mine)
    high = cots.astype(BF16)
    rest = cots - high.astype(F32)
    mid = rest.astype(BF16)
    low = (rest - mid.astype(F32)).astype(BF16)
    cot = []
    for cb in (0, 1):
        c_rows = dot(mine, high, 1, cb) + dot(mine, mid, 1, cb) + dot(mine, low, 1, cb)
        spread = dot_exact(c_rows, pick_b)
        cot.append(jnp.where(lane < 256, spread[0:1], spread[1:2]))
    frames_b = iota((1, 256), 1)
    len_vb = dot(lengths_half, ones_where(iota((VIDEOS, 256), 0) == 4 * (frames_b // 16) + rep), 1, 0)[0:1]
    valid_b = (frames_b % 16).astype(F32) < len_vb
    rows_32 = iota((32, VIDEOS), 0)
    len_va = jnp.sum(
        jnp.where(iota((32, VIDEOS), 1) == 2 * owner + rows_32 // 16, jnp.broadcast_to(lengths[0:1], (32, VIDEOS)), 0.0),
        axis=1,
        keepdims=True,
    )
    valid = ((iota((32, 256), 0) % 16).astype(F32) < len_va) & valid_b

    for copy, arriving in crossings:
        arriving.wait_recv()

    @pl.when(core == kc)
    def _():
        local.wait()

    @pl.when(core != kc)
    def _():
        got[2].wait_recv()

    pa = pa_ref[...].reshape(ROWS, WIDTH)
    sum1 = jnp.zeros((ROWS, 256), F32)
    fm2 = jnp.zeros((32, 256), F32)
    for s in range(REGIONS):
        pbs = pb_ref[:, s].reshape(SEEN * FRAMES, WIDTH)
        e = jnp.exp(dot(pa, pbs, 1, 1) * (1.0 / region_temp))
        e_ref[s] = e
        sum1 = sum1 + e
        sum2 = jnp.sum(e.reshape(OWN, REGIONS, FRAMES, 256), axis=1).reshape(32, 256)
        q2_ref[s] = sum2
        fm2 = fm2 + jnp.log(sum2)
    q1_ref[...] = sum1
    fm1 = jnp.sum(jnp.log(sum1).reshape(OWN, REGIONS, FRAMES, 256), axis=1).reshape(32, 256)
    scale = region_temp / REGIONS
    fm = jnp.concatenate([jnp.where(valid, fm1 * scale, 0.0), jnp.where(valid, fm2 * scale, 0.0)], axis=0)
    spot = iota((256, 256), 0)
    perm = ones_where((spot % 4) * 64 + (spot // 16) * 4 + (spot % 16) // 4 == iota((256, 256), 1))
    fm_ref[...] = dot_exact(fm, perm)
    for g in range(2):
        for p in range(OWN):
            for i4 in range(4):
                base = g * 32 + p * 16 + i4 * 4
                at = g * LANES + p * 256 + i4 * 64
                for pj in range(4):
                    if g == 0:
                        for pi in range(4):
                            x0_ref[pi * 4 + pj : pi * 4 + pj + 1, at : at + 64] = fm_ref[
                                base + pi : base + pi + 1, pj * 64 : pj * 64 + 64
                            ]
                    else:
                        x0_ref[pj * 4 : pj * 4 + 4, at : at + 64] = fm_ref[base : base + 4, pj * 64 : pj * 64 + 64]

    x0 = x0_ref[...]
    xcat = split2(jnp.concatenate([block_shift(x0, du, dv) for du, dv in SHIFTS], axis=0))
    w1 = split2(w1_ref[...])
    stacked = jnp.concatenate([xcat[0], xcat[0], xcat[1]], axis=0)
    h1, ds1 = silu_pair(dot(jnp.concatenate([w1[0], w1[1], w1[0]], axis=0), stacked, 0, 0))
    pooled1 = []
    for qi in range(2):
        for qj in range(2):
            parts = [
                h1[((2 * qi + a) * 4 + 2 * qj + b) * 32 : ((2 * qi + a) * 4 + 2 * qj + b) * 32 + 32]
                for a in range(2)
                for b in range(2)
            ]
            pooled1.append((parts[0] + parts[1] + parts[2] + parts[3]) * 0.25)
    h1cat = split2(
        jnp.concatenate(
            [block_shift(pooled1[qi * 2 + qj], du, dv) for qi, du in EXT2 for qj, dv in EXT2], axis=0
        )
    )
    w2 = split2(w2_ref[...])
    h2, ds2 = silu_pair(dot3(w2, h1cat, 0, 0))
    pooled2 = (h2[0:64] + h2[64:128] + h2[128:192] + h2[192:256]) * 0.25
    h2cat = split2(jnp.concatenate([block_shift(pooled2, du, dv) for du, dv in SHIFTS], axis=0))
    w3 = split2(k3_ref[...])
    both = dot(jnp.concatenate([w3[0], w3[1]], axis=1), h2cat[0], 0, 0)
    h3, ds3 = silu_pair(both[:C3] + both[C3:] + dot(w3[0], h2cat[1], 0, 0))
    kl = jnp.sum(jnp.where(iota((C3, C3), 0) == iota((C3, C3), 1), kl_ref[...], 0.0), axis=1, keepdims=True)
    out = jnp.tanh(jnp.sum(h3 * kl, axis=0, keepdims=True))

    dz = []
    for g in range(2):
        o = out[:, g * LANES : (g + 1) * LANES]
        rows_ok, inv = ((ok_a, inv_a), (ok_b, inv_b))[g]
        weighted = jnp.where(ok_a & ok_b, jnp.exp(o * (1.0 / region_temp)), 0.0)
        row_sums = quad_sum(weighted, 1 if g == 0 else 64) + jnp.where(rows_ok, 0.0, 1.0)
        if g == 0:
            best = jnp.where(rows_ok, region_temp * jnp.log(row_sums), 0.0)
            ps = quad_sum(best, 64) * inv
        dout = cot[g] * inv * weighted / row_sums
        dz.append(dout * (1.0 - o * o))
    dz = jnp.concatenate(dz, axis=1)

    def scatter_copy(to):
        return pltpu.make_async_remote_copy(
            src_ref=acc_ref.at[pl.ds(pl.multiple_of(to * 48, 48), 48)],
            dst_ref=part_a.at[chip],
            send_sem=sa.at[to],
            recv_sem=ra.at[chip],
            device_id=(to * 2 + core, rep),
            device_id_type=MESH,
        )

    def scatter_start(to):
        @pl.when(chip != to)
        def _():
            scatter_copy(to).start()

    def scatter_arrives(source):
        return pltpu.make_async_remote_copy(
            src_ref=part_a.at[source],
            dst_ref=part_a.at[source],
            send_sem=sa.at[source],
            recv_sem=ra.at[source],
            device_id=(((chip + 1) % 16) * 2 + core, rep),
            device_id_type=MESH,
        )

    def column_copy(d):
        return pltpu.make_async_remote_copy(
            src_ref=part_b.at[place],
            dst_ref=part_b.at[place],
            send_sem=sb.at[d - 1],
            recv_sem=rb.at[d - 1],
            device_id=in_column(d),
            device_id_type=MESH,
        )

    def gather_copy(d, at):
        return pltpu.make_async_remote_copy(
            src_ref=all_ref.at[pl.ds(pl.multiple_of(at * 48, 48), 48)],
            dst_ref=all_ref.at[pl.ds(pl.multiple_of(at * 48, 48), 48)],
            send_sem=sc.at[d - 1],
            recv_sem=rc.at[d - 1],
            device_id=in_plane(d),
            device_id_type=MESH,
        )

    def first(pair):
        return pair[0][:, :LANES], pair[1][:, :LANES]

    lane = lane_of((1, 128))
    row = jnp.where(lane % 4 == rep, jnp.concatenate([ps[:, 0:64], ps[:, 256:320]], axis=1), 0.0)
    at = lax.broadcasted_iota(jnp.int32, (32, 128), 0)
    acc_ref[ROW_PS : ROW_PS + 32] = jnp.where(at == owner, row, 0.0)
    dz_first = jnp.broadcast_to(dz[:, :LANES], (8, LANES))
    gl = dot3(split2(dz_first), split2(h3[:, :LANES]), 1, 1)
    dpre3, dpre3_low = split2(dz * kl * ds3)
    acc_ref[0:576] = dot2(first(h2cat), dpre3[:, :LANES], 1, 1) * (1.0 / loss_scale)
    for to in range(12):
        scatter_start(to)
    dh2cat = dot(jnp.concatenate([w3[0], w3[1]], axis=1), jnp.concatenate([dpre3, dpre3], axis=0), 1, 0)
    dh2cat = dh2cat + dot(w3[0], dpre3_low, 1, 0)
    dpool2 = jnp.zeros((64, 2 * LANES), F32)
    for n, (du, dv) in enumerate(SHIFTS):
        dpool2 = dpool2 + block_shift(dh2cat[n * 64 : n * 64 + 64], -du, -dv)
    dpool2 = dpool2 * 0.25
    dpre2, dpre2_low = split2(jnp.concatenate([dpool2, dpool2, dpool2, dpool2], axis=0) * ds2)
    g2 = dot2(first(h1cat), dpre2[:, :LANES], 1, 1)
    for ti in range(3):
        for tj in range(3):
            total = jnp.zeros((32, 64), F32)
            for pi in range(2):
                for pj in range(2):
                    row = ((pi + ti) * 4 + pj + tj) * 32
                    col = (pi * 2 + pj) * 64
                    total = total + g2[row : row + 32, col : col + 64]
            total = total * (1.0 / loss_scale)
            for half in range(2):
                n = (ti * 3 + tj) * 2 + half
                at = ROW_TWO + (n % 9) * 16
                acc_ref[at : at + 16, (n // 9) * 64 : (n // 9) * 64 + 64] = total[half * 16 : half * 16 + 16]
    dh1cat = dot2(w2, dpre2, 1, 0) + dot(w2[0], dpre2_low, 1, 0)
    dpool1 = [jnp.zeros((32, 2 * LANES), F32) for _ in range(4)]
    n = 0
    for qi, du in EXT2:
        for qj, dv in EXT2:
            dpool1[qi * 2 + qj] = dpool1[qi * 2 + qj] + block_shift(dh1cat[n * 32 : n * 32 + 32], -du, -dv)
            n += 1
    dpool1 = [d * 0.25 for d in dpool1]
    dpre1, dpre1_low = split2(
        jnp.concatenate([dpool1[(pi // 2) * 2 + pj // 2] for pi in range(4) for pj in range(4)], axis=0) * ds1
    )
    g1 = dot(jnp.concatenate(first(xcat), axis=0), dpre1[:, :LANES], 1, 1)
    g1 = g1[:144] + g1[144:]
    at = iota((144, 512), 0)
    rows = []
    for ti in range(3):
        for tj in range(3):
            v = jnp.sum(jnp.where(at == tap_rows(ti, tj), g1, 0.0), axis=0, keepdims=True)
            v = v[:, 0:128] + v[:, 128:256] + v[:, 256:384] + v[:, 384:512]
            v = v + pltpu.roll(v, 64, 1)
            rows.append(v + pltpu.roll(v, 32, 1))
    rows.append(gl[0:1])
    rows.append(jnp.zeros((6, 128), F32))
    acc_ref[ROW_ONE : ROW_ONE + 16] = jnp.concatenate(rows, axis=0) * (1.0 / loss_scale)
    for to in range(12, 16):
        scatter_start(to)
    dxcat = dot(jnp.concatenate([w1[0], w1[1]], axis=0), dpre1, 1, 0)
    dxcat = dxcat[:144] + dxcat[144:] + dot(w1[0], dpre1_low, 1, 0)
    dx0 = jnp.zeros((16, 2 * LANES), F32)
    for n, (du, dv) in enumerate(SHIFTS):
        dx0 = dx0 + block_shift(dxcat[n * 16 : n * 16 + 16], -du, -dv)
    x0_ref[...] = dx0
    for g in range(2):
        for p in range(OWN):
            for i4 in range(4):
                base = g * 32 + p * 16 + i4 * 4
                at = g * LANES + p * 256 + i4 * 64
                for pj in range(4):
                    if g == 0:
                        for pi in range(4):
                            fm_ref[base + pi : base + pi + 1, pj * 64 : pj * 64 + 64] = x0_ref[
                                pi * 4 + pj : pi * 4 + pj + 1, at : at + 64
                            ]
                    else:
                        fm_ref[base : base + 4, pj * 64 : pj * 64 + 64] = x0_ref[pj * 4 : pj * 4 + 4, at : at + 64]
    dfm = dot_exact(fm_ref[...], perm, 1)
    dfm1 = jnp.where(valid, dfm[:32], 0.0) * (1.0 / REGIONS)
    dfm2 = jnp.where(valid, dfm[32:], 0.0) * (1.0 / REGIONS)

    part_a[chip] = acc_ref[pl.ds(pl.multiple_of(chip * 48, 48), 48)]
    for d in range(1, 16):
        scatter_arrives((chip + 16 - d) % 16).wait_recv()
    total = part_a[0]
    for n in range(1, 16):
        total = total + part_a[n]
    part_b[place] = total
    for d in range(1, 8):
        column_copy(d).start()

    sum1 = q1_ref[...].reshape(OWN, REGIONS, FRAMES, 256)
    q1 = dfm1.reshape(OWN, 1, FRAMES, 256) / sum1
    rowperm = ones_where(frame_rows((1, ROWS)) == iota((320, ROWS), 0))
    for s in range(REGIONS):
        q2 = (dfm2 / q2_ref[s]).reshape(OWN, 1, FRAMES, 256)
        grad = (e_ref[s].reshape(OWN, REGIONS, FRAMES, 256) * (q1 + q2)).reshape(ROWS, 256).astype(BF16)
        grad_ref[s] = dot(rowperm, grad, 1, 0).astype(BF16)

    def way(n):
        return 1 if n < 2 else -1

    def rep_copy(kind, n):
        d = -way(n) if kind == 2 else way(n)
        of = (rep + 2) % 4 if kind == 0 else (rep + d + 4) % 4
        return pltpu.make_async_remote_copy(
            src_ref=send_ref.at[of, :, pl.ds(n * CHUNK, CHUNK)],
            dst_ref=recv_ref.at[kind, :, pl.ds(n * CHUNK, CHUNK)],
            send_sem=rs.at[n * 3 + kind],
            recv_sem=rr.at[n * 3 + kind],
            device_id=(owner, (rep + d + 4) % 4),
            device_id_type=MESH,
        )

    order = (0, 2, 1, 3)
    for n in order:
        cols = slice(n * CHUNK, (n + 1) * CHUNK)
        product = jnp.zeros((320, CHUNK), F32)
        for s in range(REGIONS):
            pbs = pb_ref[:, s, :, cols].reshape(SEEN * FRAMES, CHUNK)
            product = product + dot(grad_ref[s], pbs, 1, 0)
        product = product.reshape(SIDE, 80, CHUNK)
        rg_ref[:, :, cols] = product
        send_ref[:, :, cols] = product.astype(BF16)
        rep_copy(0, n).start()
        rep_copy(2, n).start()
        if n == 2:
            for d in range(1, 8):
                pltpu.make_async_remote_copy(
                    src_ref=part_b.at[(place + 8 - d) % 8],
                    dst_ref=part_b.at[(place + 8 - d) % 8],
                    send_sem=sb.at[d - 1],
                    recv_sem=rb.at[d - 1],
                    device_id=in_column(d),
                    device_id_type=MESH,
                ).wait_recv()
            total = part_b[0]
            for q in range(1, 8):
                total = total + part_b[q]
            all_ref[pl.ds(pl.multiple_of(chip * 48, 48), 48)] = total
            for d in range(1, 16):
                gather_copy(d, chip).start()
    for n in order:
        cols = slice(n * CHUNK, (n + 1) * CHUNK)
        of = (rep + way(n) + 4) % 4
        rep_copy(0, n).wait_recv()
        send_ref[of, :, cols] = (rg_ref[of, :, cols] + recv_ref[0, :, cols].astype(F32)).astype(BF16)
        rep_copy(1, n).start()
    for d in range(1, 16):
        gather_copy(d, (chip + 16 - d) % 16).wait_recv()
    table = all_ref[ROW_PS:ROW_ALL]
    found = jnp.zeros((1, 512), F32)
    for p in range(OWN):
        left = dot(ones_where(iota((32, VIDEOS), 1) == 2 * iota((32, VIDEOS), 0) + p), hots_ref[0], 1, 0)
        value = dot_exact(table[:, p * 64 : p * 64 + 64], hots_ref[1])
        found = found + jnp.sum(left * value, axis=0, keepdims=True)
    ps_ref[...] = found
    own = own_ref[...]
    inverse = lax.rsqrt(jnp.sum(own * own, axis=1, keepdims=True) + norm_eps)
    along = jnp.zeros((80, 1), F32)
    for n in order:
        cols = slice(n * CHUNK, (n + 1) * CHUNK)
        rep_copy(2, n).wait_recv()
        rep_copy(1, n).wait_recv()
        total = rg_ref[rep, :, cols] + recv_ref[2, :, cols].astype(F32) + recv_ref[1, :, cols].astype(F32)
        rg_ref[rep, :, cols] = total
        along = along + jnp.sum(own_ref[:, cols] * total, axis=1, keepdims=True)
    back = along * inverse * inverse * inverse
    for n in range(CHUNKS):
        cols = slice(n * CHUNK, (n + 1) * CHUNK)
        result = rg_ref[rep, :, cols] * inverse - own_ref[:, cols] * back
        for q in range(18):
            fg_ref[q, :, cols] = result[q * 4 : q * 4 + 4]

    for copy, arriving in crossings:
        copy.wait_send()
    for m in range(2):
        for r in [ring1[m]] + [ring2[m][du] for du in offsets]:
            for name in ("send_plus", "send_minus", "fwd_plus", "fwd_minus"):
                r[name].wait_send()

    @pl.when(core == kc)
    def _():
        for copy in sent:
            copy.wait_send()

    for d in (1, 2, 3):
        c_copy(d, rep).wait_send()
        for n in range(CHUNKS):
            rep_copy(d - 1, n).wait_send()
    for d in range(1, 16):
        scatter_copy((chip + d) % 16).wait_send()
        gather_copy(d, chip).wait_send()
    for d in range(1, 8):
        column_copy(d).wait_send()


def whole(*args):
    return pl.pallas_call(
        whole_kernel,
        name="training_step",
        out_shape=(
            jax.ShapeDtypeStruct((OWN * REGIONS, 4, WIDTH), F32),
            jax.ShapeDtypeStruct((1, 512), F32),
            jax.ShapeDtypeStruct((ROW_ALL, 128), F32),
        ),
        in_specs=[ANY_SPEC] + [VMEM_SPEC] * 5 + [ANY_SPEC] * 2 + [VMEM_SPEC],
        out_specs=(VMEM_SPEC,) * 3,
        scratch_shapes=[
            pltpu.VMEM((OWN, REGIONS, FRAMES, WIDTH), F32),
            pltpu.VMEM((9, 32, 64), F32),
            pltpu.VMEM((576, C3), F32),
            pltpu.VMEM((OWN, REGIONS, FRAMES, WIDTH), BF16),
            pltpu.VMEM((SEEN, REGIONS, FRAMES, WIDTH), BF16),
            pltpu.VMEM((SIDE, VIDEOS, VIDEOS), F32),
            pltpu.VMEM((2, VIDEOS, 512), BF16),
            pltpu.VMEM((144, 512), F32),
            pltpu.VMEM((512, 256), F32),
            pltpu.VMEM((80, WIDTH), F32),
            pltpu.VMEM((REGIONS, ROWS, 256), F32),
            pltpu.VMEM((ROWS, 256), F32),
            pltpu.VMEM((REGIONS, 32, 256), F32),
            pltpu.VMEM((64, 256), F32),
            pltpu.VMEM((16, 2 * LANES), F32),
            pltpu.VMEM((REGIONS, 320, 256), BF16),
            pltpu.VMEM((ROW_ALL, 128), F32),
            pltpu.VMEM((SIDE, 80, WIDTH), F32),
            pltpu.VMEM((SIDE, 80, WIDTH), BF16),
            pltpu.VMEM((3, 80, WIDTH), BF16),
            pltpu.VMEM((16, 48, 128), F32),
            pltpu.VMEM((8, 48, 128), F32),
        ]
        + [
            pltpu.SemaphoreType.DMA((n,))
            for n in (40, 40, 30, 30, 3, 3, 1, 4, 3, 3, 3 * CHUNKS, 3 * CHUNKS, 16, 16, 7, 7, 15, 15)
        ],
        compiler_params=pltpu.CompilerParams(
            collective_id=0, has_side_effects=True, vmem_limit_bytes=58 * 2**20
        ),
    )(*args)


def outputs_kernel(fg_in, ps_in, all_in, ps_ref, fg_ref, g1_ref, g2_ref, g3_ref, gl_ref):
    fg_ref[...] = fg_in[...]
    ps_ref[...] = ps_in[...]
    g3_ref[...] = all_in[0:ROW_TWO]
    for n in range(18):
        at = ROW_TWO + (n % 9) * 16
        g2_ref[n // 2, (n % 2) * 16 : (n % 2) * 16 + 16, :] = all_in[at : at + 16, (n // 9) * 64 : (n // 9) * 64 + 64]
    for n in range(9):
        g1_ref[n // 3, n % 3] = all_in[ROW_ONE + n : ROW_ONE + n + 1, 0:32]
    gl_ref[...] = all_in[ROW_ONE + 9 : ROW_ONE + 10]


def outputs(fg, ps, summed):
    return pl.pallas_call(
        outputs_kernel,
        name="outputs",
        out_shape=(
            jax.ShapeDtypeStruct((1, 512), F32),
            jax.ShapeDtypeStruct((OWN * REGIONS, 4, WIDTH), F32),
            jax.ShapeDtypeStruct((3, 3, 1, 32), F32),
            jax.ShapeDtypeStruct((9, 32, 64), F32),
            jax.ShapeDtypeStruct((576, C3), F32),
            jax.ShapeDtypeStruct((1, C3), F32),
        ),
        in_specs=[VMEM_SPEC] * 3,
        out_specs=(VMEM_SPEC,) * 6,
    )(fg, ps, summed)


def local(
    features, frame_counts, video_rows, pair_list, pair_cotangent, kernel_one, kernel_two, kernel_three, kernel_last
):
    fg, ps, summed = whole(
        features.transpose(0, 2, 1, 3),
        frame_counts.reshape(1, VIDEOS),
        video_rows.reshape(1, VIDEOS),
        pair_list.T,
        pair_cotangent.reshape(1, 512),
        kernel_one,
        kernel_two.reshape(9, 32, 64),
        kernel_three.reshape(576, C3),
        kernel_last.reshape(1, C3),
    )
    ps, fg, g1, g2, g3, gl = outputs(fg, ps, summed)
    return (
        ps.reshape(512),
        fg.reshape(OWN, REGIONS, 4, WIDTH).transpose(0, 2, 1, 3),
        g1,
        g2.reshape(3, 3, 32, 64),
        g3.reshape(3, 3, 64, C3),
        gl.reshape(C3),
    )


def solution(mesh):
    placed = (P("owner", None, None, None), P(), P(), P("rep", None), P("rep"), P(), P(), P(), P())
    return jax.shard_map(
        local,
        mesh=mesh,
        in_specs=placed,
        out_specs=(P("rep"), P("owner", "rep", None, None), P(), P(), P(), P()),
        check_vma=False,
    )
```

```python
import jax
import jax.numpy as jnp
from jax import lax
from jax.experimental import pallas as pl
from jax.experimental.pallas import tpu as pltpu
from jax.sharding import PartitionSpec as P

MESH = pl.DeviceIdType.MESH
VMEM_SPEC = pl.BlockSpec(memory_space=pltpu.VMEM)
ANY_SPEC = pl.BlockSpec(memory_space=pl.ANY)
F32 = jnp.float32
BF16 = jnp.bfloat16

REGIONS = 9
FRAMES = 16
WIDTH = 2048
VIDEOS = 64
SIDE = 4
OWN = 2
SEEN = 16
ROWS = OWN * REGIONS * FRAMES
LANES = OWN * SEEN * 16

ROW_TWO = 576
ROW_ONE = 720
ROW_PS = 736
ROW_ALL = 768

region_temp = 0.1
loss_scale = 131072.0
norm_eps = 1e-06
C3 = 128


CHUNKS = 4
CHUNK = WIDTH // CHUNKS


def split2(v):
    high = v.astype(BF16)
    return high, (v - high.astype(F32)).astype(BF16)


def dot(a, b, ca, cb):
    return lax.dot_general(a, b, (((ca,), (cb,)), ((), ())), preferred_element_type=F32)


def dot3(a, b, ca, cb):
    (ah, al), (bh, bl) = a, b
    return dot(ah, bh, ca, cb) + dot(ah, bl, ca, cb) + dot(al, bh, ca, cb)


def dot2(a, b, ca, cb):
    return dot(a[0], b, ca, cb) + dot(a[1], b, ca, cb)


def dot_exact(v, chosen, cb=0):
    high = v.astype(BF16)
    rest = v - high.astype(F32)
    mid = rest.astype(BF16)
    low = (rest - mid.astype(F32)).astype(BF16)
    return dot(high, chosen, 1, cb) + dot(mid, chosen, 1, cb) + dot(low, chosen, 1, cb)


def lane_of(shape):
    return lax.broadcasted_iota(jnp.int32, shape, len(shape) - 1)


def moved(v, di, dj):
    if di == 0 and dj == 0:
        return v
    out = pltpu.roll(v, (-(di * 64 + dj)) % LANES, 1)
    lane = lane_of((1, LANES))
    i4, j4 = (lane // 64) % 4, lane % 4
    ok = (i4 + di >= 0) & (i4 + di < 4) & (j4 + dj >= 0) & (j4 + dj < 4)
    return jnp.where(ok, out, 0.0)


def block_shift(v, du, dv):
    return jnp.concatenate([moved(v[:, :LANES], du, dv), moved(v[:, LANES:], dv, du)], axis=1)


def quad_sum(v, stride):
    lane = lane_of((1, LANES))
    for step in (stride, 2 * stride):
        low = (lane // step) % 2 == 0
        v = v + jnp.where(low, pltpu.roll(v, LANES - step, 1), pltpu.roll(v, step, 1))
    return v


def silu_pair(v):
    s = 1.0 / (1.0 + jnp.exp(-v))
    return v * s, s * (1.0 + v * (1.0 - s))


def iota(shape, axis):
    return lax.broadcasted_iota(jnp.int32, shape, axis)


def ones_where(condition):
    return jnp.where(condition, 1.0, 0.0).astype(BF16)


def tap_rows(ti, tj):
    plane = lane_of((1, 512)) // 32
    ei, ej = plane // 4 + ti + 3, plane % 4 + tj + 3
    return ((ei // 4) * 3 + ej // 4) * 16 + (ei % 4) * 4 + ej % 4


SHIFTS = [(du, dv) for du in (-1, 0, 1) for dv in (-1, 0, 1)]
EXT2 = [(1, -1), (0, 0), (1, 0), (0, 1)]


def whole_kernel(
    x_hbm, counts_ref, vrows_ref, pairs_ref, cot_ref, k1_ref, k2_hbm, k3_hbm, kl_ref,
    fg_ref, ps_ref, all_ref,
    x_ref, k2_ref, k3_ref, pa_ref, pb_ref, call_ref, hots_ref, w1_ref, w2_ref, own_ref,
    e_ref, q1_ref, q2_ref, fm_ref, x0_ref, grad_ref, acc_ref, rg_ref, send_ref, recv_ref, part_a, part_b, acc_half, part_half, all_half,
    ssem, rsem, dssem, drsem, csem, crsem, lsem, insem, hs, hr, rs, rr, sa, ra, sb, rb, sc, rc,
):
    owner = lax.axis_index("owner")
    rep = lax.axis_index("rep")
    z, x, core = owner // 8, (owner // 2) % 4, owner % 2
    chip = owner // 2
    place = core * 4 + rep
    other = owner + 1 - 2 * core

    def in_plane(d):
        return (((chip + d) % 16) * 2 + core, rep)

    def in_column(d):
        to = (place + d) % 8
        return (chip * 2 + to // 4, to % 4)

    def shifted(axis, d):
        if axis == 0:
            return z * 8 + ((x + d + 4) % 4) * 2 + core
        return ((z + d + 4) % 4) * 8 + x * 2 + core

    def chip_at(first, du, dv):
        dx, dz = (du, dv) if first == 0 else (dv, du)
        return ((z + dz + 4) % 4) * 4 + (x + dx + 4) % 4

    loads = [pltpu.make_async_copy(x_hbm.at[p], x_ref.at[p], insem.at[p]) for p in range(OWN)]
    loads.append(pltpu.make_async_copy(k2_hbm, k2_ref, insem.at[2]))
    loads.append(pltpu.make_async_copy(k3_hbm, k3_ref, insem.at[3]))
    for load in loads:
        load.start()
    barrier = pltpu.get_barrier_semaphore()
    for axis in (0, 1):
        for d in (1, -1):
            pl.semaphore_signal(barrier, inc=1, device_id=(shifted(axis, d), rep), device_id_type=MESH)
    for d in range(1, 8):
        pl.semaphore_signal(barrier, inc=1, device_id=in_column(d), device_id_type=MESH)

    for p in range(OWN):
        loads[p].wait()
        values = x_ref[p]
        summed = jnp.sum(values * values, axis=-1, keepdims=True) + norm_eps
        pa_ref[p] = (values * lax.rsqrt(summed)).astype(BF16)

    pl.semaphore_wait(barrier, 11)

    kc, kp = rep // 2, rep % 2
    local = pltpu.make_async_copy(pa_ref.at[kp], pb_ref.at[chip], lsem.at[0])

    def own_lanes(to, m):
        return pl.ds(pl.multiple_of(to * 1024 + m * 512, 512), 512)

    def to_other(n, lanes):
        return pltpu.make_async_remote_copy(
            src_ref=pa_ref.at[kp, :, :, lanes],
            dst_ref=pb_ref.at[chip, :, :, lanes],
            send_sem=hs.at[n],
            recv_sem=hr.at[n],
            device_id=(other, rep),
            device_id_type=MESH,
        )

    sent = [to_other(0, own_lanes(1 - core, 0)), to_other(1, own_lanes(1 - core, 1))]
    sent.append(to_other(2, pl.ds(pl.multiple_of(core * 1024, 1024), 1024)))
    got = [to_other(0, own_lanes(core, 0)), to_other(1, own_lanes(core, 1))]
    got.append(to_other(2, pl.ds(pl.multiple_of((1 - core) * 1024, 1024), 1024)))

    def piece(block, m, half):
        if half is None:
            lanes = pl.ds(pl.multiple_of(core * 1024 + m * 512, 512), 512)
        else:
            lanes = pl.ds(pl.multiple_of(core * 1024 + m * 512 + half * 256, 256), 256)
        return pb_ref.at[block, :, :, lanes]

    def ring(m, index, first, du, along):
        base = (m * 5 + index) * 4
        axis = first if along == 0 else 1 - first

        def block(d):
            return chip_at(first, d, 0) if along == 0 else chip_at(first, du, d)

        def copy(slot, source, d, half, prepared=False):
            ref = piece(source, m, half)
            return pltpu.make_async_remote_copy(
                src_ref=pa_ref.at[kp, :, :, own_lanes(core, m)] if prepared else ref,
                dst_ref=ref,
                send_sem=ssem.at[base + slot],
                recv_sem=rsem.at[base + slot],
                device_id=(shifted(axis, d), rep),
                device_id_type=MESH,
            )

        return dict(
            first_plus=copy(0, block(0), 1, None, True),
            first_minus=copy(1, block(0), -1, None, True),
            send_plus=copy(0, block(0), 1, None),
            send_minus=copy(1, block(0), -1, None),
            fwd_plus=copy(2, block(-1), 1, 0),
            fwd_minus=copy(3, block(1), -1, 1),
            from_minus=copy(0, block(-1), 1, None),
            from_plus=copy(1, block(1), -1, None),
            far_a=copy(2, block(2), 1, 0),
            far_b=copy(3, block(2), -1, 1),
            block=block,
        )

    crossings = []

    def cross(m, block):
        n = len(crossings)
        ref = piece(block, m, None)
        copy = pltpu.make_async_remote_copy(
            src_ref=ref,
            dst_ref=ref,
            send_sem=dssem.at[n],
            recv_sem=drsem.at[n],
            device_id=(other, rep),
            device_id_type=MESH,
        )
        copy.start()
        lanes = pl.ds(pl.multiple_of((1 - core) * 1024 + m * 512, 512), 512)
        theirs = pb_ref.at[block, :, :, lanes]
        arriving = pltpu.make_async_remote_copy(
            src_ref=theirs,
            dst_ref=theirs,
            send_sem=dssem.at[n],
            recv_sem=drsem.at[n],
            device_id=(other, rep),
            device_id_type=MESH,
        )
        crossings.append((copy, arriving))

    def c_copy(d, at):
        return pltpu.make_async_remote_copy(
            src_ref=call_ref.at[at],
            dst_ref=call_ref.at[at],
            send_sem=csem.at[d - 1],
            recv_sem=crsem.at[d - 1],
            device_id=(owner, (rep + d) % 4),
            device_id_type=MESH,
        )

    def make_pairs():
        by_row = ones_where(iota((VIDEOS, VIDEOS), 0) == vrows_ref[...])
        videos = iota((VIDEOS, 512), 0)
        row_a = dot(by_row, ones_where(videos == pairs_ref[0:1, :]), 1, 0)
        row_b = dot(by_row, ones_where(videos == pairs_ref[1:2, :]), 1, 0)
        hots_ref[0] = row_a.astype(BF16)
        hots_ref[1] = row_b.astype(BF16)
        call_ref[rep] = dot_exact(row_a * cot_ref[...], row_b.astype(BF16), 1)
        for d in (1, 2, 3):
            c_copy(d, rep).start()

    def make_weights():
        loads[2].wait()
        loads[3].wait()
        k1 = jnp.concatenate([k1_ref[n // 3, n % 3] for n in range(9)], axis=0)
        tiled = dot_exact(k1, ones_where(iota((32, 512), 1) % 32 == iota((32, 512), 0)))
        at = iota((144, 512), 0)
        w1 = jnp.zeros((144, 512), F32)
        for ti in range(3):
            for tj in range(3):
                w1 = jnp.where(at == tap_rows(ti, tj), tiled[ti * 3 + tj : ti * 3 + tj + 1], w1)
        w1_ref[...] = w1
        w2_ref[...] = jnp.zeros((512, 256), F32)
        for ti in range(3):
            for tj in range(3):
                for pi in range(2):
                    for pj in range(2):
                        row = ((pi + ti) * 4 + pj + tj) * 32
                        col = (pi * 2 + pj) * 64
                        w2_ref[row : row + 32, col : col + 64] = k2_ref[ti * 3 + tj]

    def frame_rows(shape):
        n = lane_of(shape)
        return ((n % 16) // 4) * 80 + (n // 144) * 36 + ((n % 144) // 16) * 4 + n % 4

    def make_own():
        chosen = ones_where(frame_rows((1, ROWS)) - rep * 80 == iota((80, ROWS), 0))
        for n in range(4):
            v = x_ref[:, :, :, n * 512 : n * 512 + 512].reshape(ROWS, 512)
            high = v.astype(BF16)
            rest = v - high.astype(F32)
            mid = rest.astype(BF16)
            low = (rest - mid.astype(F32)).astype(BF16)
            own_ref[:, n * 512 : n * 512 + 512] = (
                dot(chosen, high, 1, 0) + dot(chosen, mid, 1, 0) + dot(chosen, low, 1, 0)
            )

    offsets = (0, -1, 1, 2)
    ring1 = [ring(m, 0, m, 0, 0) for m in range(2)]
    ring2 = [{du: ring(m, 1 + n, m, du, 1) for n, du in enumerate(offsets)} for m in range(2)]

    def begin(r):
        r["send_plus"].start()
        r["send_minus"].start()

    @pl.when(core == kc)
    def _():
        sent[0].start()
        sent[1].start()
        for r in (ring1[0], ring1[1], ring2[0][0], ring2[1][0]):
            r["first_plus"].start()
            r["first_minus"].start()
        local.start()
        sent[2].start()

    @pl.when(core != kc)
    def _():
        for m in range(2):
            got[m].wait_recv()
            begin(ring1[m])
            begin(ring2[m][0])

    for d, arrive, forward in ((-1, "from_minus", "fwd_plus"), (1, "from_plus", "fwd_minus")):
        for m in range(2):
            ring1[m][arrive].wait_recv()
            ring1[m][forward].start()
            begin(ring2[m][d])
            cross(m, ring1[m]["block"](d))
    for m in range(2):
        ring1[m]["far_a"].wait_recv()
        ring1[m]["far_b"].wait_recv()
        begin(ring2[m][2])
        cross(m, ring1[m]["block"](2))
    beside = {0: make_pairs, -1: make_weights, 1: make_own}
    for du in offsets:
        for d, arrive, forward in ((-1, "from_minus", "fwd_plus"), (1, "from_plus", "fwd_minus")):
            for m in range(2):
                r = ring2[m][du]
                r[arrive].wait_recv()
                r[forward].start()
                cross(m, r["block"](d))
        if du in beside:
            beside[du]()
    for du in offsets:
        for m in range(2):
            r = ring2[m][du]
            r["far_a"].wait_recv()
            r["far_b"].wait_recv()
            cross(m, r["block"](2))

    for d in (1, 2, 3):
        c_copy(d, (rep + 4 - d) % 4).wait_recv()
    cots = (call_ref[0] + call_ref[1] + call_ref[2] + call_ref[3]) * loss_scale
    by_row = ones_where(iota((VIDEOS, VIDEOS), 0) == vrows_ref[...])
    lengths = dot(jnp.broadcast_to(counts_ref[...], (8, VIDEOS)).astype(F32).astype(BF16), by_row, 1, 1)
    lengths_half = lengths.astype(BF16)
    at = iota((VIDEOS, LANES), 0)
    lane = iota((1, LANES), 1)
    len_a = dot(lengths_half, ones_where(at == 2 * owner + lane // 256), 1, 0)[0:1]
    pick_b = ones_where(at == 4 * ((lane % 64) // 4) + rep)
    len_b = dot(lengths_half, pick_b, 1, 0)[0:1]
    ok_a = ((lane // 64) % 4 * 4).astype(F32) < len_a
    ok_b = (lane % 4 * 4).astype(F32) < len_b
    inv_a = 1.0 / quad_sum(jnp.where(ok_a, 1.0, 0.0), 64)
    inv_b = 1.0 / quad_sum(jnp.where(ok_b, 1.0, 0.0), 1)
    mine = iota((8, VIDEOS), 1) == 2 * owner + iota((8, VIDEOS), 0) % 2
    mine = ones_where(mine)
    high = cots.astype(BF16)
    rest = cots - high.astype(F32)
    mid = rest.astype(BF16)
    low = (rest - mid.astype(F32)).astype(BF16)
    cot = []
    for cb in (0, 1):
        c_rows = dot(mine, high, 1, cb) + dot(mine, mid, 1, cb) + dot(mine, low, 1, cb)
        spread = dot_exact(c_rows, pick_b)
        cot.append(jnp.where(lane < 256, spread[0:1], spread[1:2]))
    frames_b = iota((1, 256), 1)
    len_vb = dot(lengths_half, ones_where(iota((VIDEOS, 256), 0) == 4 * (frames_b // 16) + rep), 1, 0)[0:1]
    valid_b = (frames_b % 16).astype(F32) < len_vb
    rows_32 = iota((32, VIDEOS), 0)
    len_va = jnp.sum(
        jnp.where(iota((32, VIDEOS), 1) == 2 * owner + rows_32 // 16, jnp.broadcast_to(lengths[0:1], (32, VIDEOS)), 0.0),
        axis=1,
        keepdims=True,
    )
    valid = ((iota((32, 256), 0) % 16).astype(F32) < len_va) & valid_b

    for copy, arriving in crossings:
        arriving.wait_recv()

    @pl.when(core == kc)
    def _():
        local.wait()

    @pl.when(core != kc)
    def _():
        got[2].wait_recv()

    pa = pa_ref[...].reshape(ROWS, WIDTH)
    sum1 = jnp.zeros((ROWS, 256), F32)
    fm2 = jnp.zeros((32, 256), F32)
    for s in range(REGIONS):
        pbs = pb_ref[:, s].reshape(SEEN * FRAMES, WIDTH)
        e = jnp.exp(dot(pa, pbs, 1, 1) * (1.0 / region_temp))
        e_ref[s] = e
        sum1 = sum1 + e
        sum2 = jnp.sum(e.reshape(OWN, REGIONS, FRAMES, 256), axis=1).reshape(32, 256)
        q2_ref[s] = sum2
        fm2 = fm2 + jnp.log(sum2)
    q1_ref[...] = sum1
    fm1 = jnp.sum(jnp.log(sum1).reshape(OWN, REGIONS, FRAMES, 256), axis=1).reshape(32, 256)
    scale = region_temp / REGIONS
    fm = jnp.concatenate([jnp.where(valid, fm1 * scale, 0.0), jnp.where(valid, fm2 * scale, 0.0)], axis=0)
    spot = iota((256, 256), 0)
    perm = ones_where((spot % 4) * 64 + (spot // 16) * 4 + (spot % 16) // 4 == iota((256, 256), 1))
    fm_ref[...] = dot_exact(fm, perm)
    for g in range(2):
        for p in range(OWN):
            for i4 in range(4):
                base = g * 32 + p * 16 + i4 * 4
                at = g * LANES + p * 256 + i4 * 64
                for pj in range(4):
                    if g == 0:
                        for pi in range(4):
                            x0_ref[pi * 4 + pj : pi * 4 + pj + 1, at : at + 64] = fm_ref[
                                base + pi : base + pi + 1, pj * 64 : pj * 64 + 64
                            ]
                    else:
                        x0_ref[pj * 4 : pj * 4 + 4, at : at + 64] = fm_ref[base : base + 4, pj * 64 : pj * 64 + 64]

    x0 = x0_ref[...]
    xcat = split2(jnp.concatenate([block_shift(x0, du, dv) for du, dv in SHIFTS], axis=0))
    w1 = split2(w1_ref[...])
    stacked = jnp.concatenate([xcat[0], xcat[0], xcat[1]], axis=0)
    h1, ds1 = silu_pair(dot(jnp.concatenate([w1[0], w1[1], w1[0]], axis=0), stacked, 0, 0))
    pooled1 = []
    for qi in range(2):
        for qj in range(2):
            parts = [
                h1[((2 * qi + a) * 4 + 2 * qj + b) * 32 : ((2 * qi + a) * 4 + 2 * qj + b) * 32 + 32]
                for a in range(2)
                for b in range(2)
            ]
            pooled1.append((parts[0] + parts[1] + parts[2] + parts[3]) * 0.25)
    h1cat = split2(
        jnp.concatenate(
            [block_shift(pooled1[qi * 2 + qj], du, dv) for qi, du in EXT2 for qj, dv in EXT2], axis=0
        )
    )
    w2 = split2(w2_ref[...])
    h2, ds2 = silu_pair(dot3(w2, h1cat, 0, 0))
    pooled2 = (h2[0:64] + h2[64:128] + h2[128:192] + h2[192:256]) * 0.25
    h2cat = split2(jnp.concatenate([block_shift(pooled2, du, dv) for du, dv in SHIFTS], axis=0))
    w3 = split2(k3_ref[...])
    both = dot(jnp.concatenate([w3[0], w3[1]], axis=1), h2cat[0], 0, 0)
    h3, ds3 = silu_pair(both[:C3] + both[C3:] + dot(w3[0], h2cat[1], 0, 0))
    kl = jnp.sum(jnp.where(iota((C3, C3), 0) == iota((C3, C3), 1), kl_ref[...], 0.0), axis=1, keepdims=True)
    out = jnp.tanh(jnp.sum(h3 * kl, axis=0, keepdims=True))

    dz = []
    for g in range(2):
        o = out[:, g * LANES : (g + 1) * LANES]
        rows_ok, inv = ((ok_a, inv_a), (ok_b, inv_b))[g]
        weighted = jnp.where(ok_a & ok_b, jnp.exp(o * (1.0 / region_temp)), 0.0)
        row_sums = quad_sum(weighted, 1 if g == 0 else 64) + jnp.where(rows_ok, 0.0, 1.0)
        if g == 0:
            best = jnp.where(rows_ok, region_temp * jnp.log(row_sums), 0.0)
            ps = quad_sum(best, 64) * inv
        dout = cot[g] * inv * weighted / row_sums
        dz.append(dout * (1.0 - o * o))
    dz = jnp.concatenate(dz, axis=1)

    def scatter_copy(to):
        return pltpu.make_async_remote_copy(
            src_ref=acc_ref.at[720:768] if to == 15 else acc_half.at[to * 48 : to * 48 + 48],
            dst_ref=part_a.at[chip] if to == 15 else part_half.at[chip],
            send_sem=sa.at[to],
            recv_sem=ra.at[chip],
            device_id=(to * 2 + core, rep),
            device_id_type=MESH,
        )

    def scatter_start(to):
        @pl.when(chip != to)
        def _():
            scatter_copy(to).start()

    def scatter_arrives(source, parts):
        return pltpu.make_async_remote_copy(
            src_ref=parts.at[source],
            dst_ref=parts.at[source],
            send_sem=sa.at[source],
            recv_sem=ra.at[source],
            device_id=(((chip + 1) % 16) * 2 + core, rep),
            device_id_type=MESH,
        )

    def column_copy(d):
        return pltpu.make_async_remote_copy(
            src_ref=part_b.at[place],
            dst_ref=part_b.at[place],
            send_sem=sb.at[d - 1],
            recv_sem=rb.at[d - 1],
            device_id=in_column(d),
            device_id_type=MESH,
        )

    def gather_copy(d, at, last):
        rows = pl.ds(pl.multiple_of(at * 48, 48), 48)
        block = all_ref.at[720:768] if last else all_half.at[rows]
        return pltpu.make_async_remote_copy(
            src_ref=block,
            dst_ref=block,
            send_sem=sc.at[d - 1],
            recv_sem=rc.at[d - 1],
            device_id=in_plane(d),
            device_id_type=MESH,
        )

    def first(pair):
        return pair[0][:, :LANES], pair[1][:, :LANES]

    lane = lane_of((1, 128))
    row = jnp.where(lane % 4 == rep, jnp.concatenate([ps[:, 0:64], ps[:, 256:320]], axis=1), 0.0)
    at = lax.broadcasted_iota(jnp.int32, (32, 128), 0)
    acc_ref[ROW_PS : ROW_PS + 32] = jnp.where(at == owner, row, 0.0)
    dz_first = jnp.broadcast_to(dz[:, :LANES], (8, LANES))
    gl = dot3(split2(dz_first), split2(h3[:, :LANES]), 1, 1)
    dpre3, dpre3_low = split2(dz * kl * ds3)
    acc_ref[0:576] = dot2(first(h2cat), dpre3[:, :LANES], 1, 1) * (1.0 / loss_scale)
    acc_half[0:576] = acc_ref[0:576].astype(BF16)
    for to in range(12):
        scatter_start(to)
    dh2cat = dot(jnp.concatenate([w3[0], w3[1]], axis=1), jnp.concatenate([dpre3, dpre3], axis=0), 1, 0)
    dh2cat = dh2cat + dot(w3[0], dpre3_low, 1, 0)
    dpool2 = jnp.zeros((64, 2 * LANES), F32)
    for n, (du, dv) in enumerate(SHIFTS):
        dpool2 = dpool2 + block_shift(dh2cat[n * 64 : n * 64 + 64], -du, -dv)
    dpool2 = dpool2 * 0.25
    dpre2, dpre2_low = split2(jnp.concatenate([dpool2, dpool2, dpool2, dpool2], axis=0) * ds2)
    g2 = dot2(first(h1cat), dpre2[:, :LANES], 1, 1)
    for ti in range(3):
        for tj in range(3):
            total = jnp.zeros((32, 64), F32)
            for pi in range(2):
                for pj in range(2):
                    row = ((pi + ti) * 4 + pj + tj) * 32
                    col = (pi * 2 + pj) * 64
                    total = total + g2[row : row + 32, col : col + 64]
            total = total * (1.0 / loss_scale)
            for half in range(2):
                n = (ti * 3 + tj) * 2 + half
                at = ROW_TWO + (n % 9) * 16
                acc_ref[at : at + 16, (n // 9) * 64 : (n // 9) * 64 + 64] = total[half * 16 : half * 16 + 16]
    dh1cat = dot2(w2, dpre2, 1, 0) + dot(w2[0], dpre2_low, 1, 0)
    dpool1 = [jnp.zeros((32, 2 * LANES), F32) for _ in range(4)]
    n = 0
    for qi, du in EXT2:
        for qj, dv in EXT2:
            dpool1[qi * 2 + qj] = dpool1[qi * 2 + qj] + block_shift(dh1cat[n * 32 : n * 32 + 32], -du, -dv)
            n += 1
    dpool1 = [d * 0.25 for d in dpool1]
    dpre1, dpre1_low = split2(
        jnp.concatenate([dpool1[(pi // 2) * 2 + pj // 2] for pi in range(4) for pj in range(4)], axis=0) * ds1
    )
    g1 = dot(jnp.concatenate(first(xcat), axis=0), dpre1[:, :LANES], 1, 1)
    g1 = g1[:144] + g1[144:]
    at = iota((144, 512), 0)
    rows = []
    for ti in range(3):
        for tj in range(3):
            v = jnp.sum(jnp.where(at == tap_rows(ti, tj), g1, 0.0), axis=0, keepdims=True)
            v = v[:, 0:128] + v[:, 128:256] + v[:, 256:384] + v[:, 384:512]
            v = v + pltpu.roll(v, 64, 1)
            rows.append(v + pltpu.roll(v, 32, 1))
    rows.append(gl[0:1])
    rows.append(jnp.zeros((6, 128), F32))
    acc_ref[ROW_ONE : ROW_ONE + 16] = jnp.concatenate(rows, axis=0) * (1.0 / loss_scale)
    acc_half[576:720] = acc_ref[576:720].astype(BF16)
    for to in range(12, 16):
        scatter_start(to)
    dxcat = dot(jnp.concatenate([w1[0], w1[1]], axis=0), dpre1, 1, 0)
    dxcat = dxcat[:144] + dxcat[144:] + dot(w1[0], dpre1_low, 1, 0)
    dx0 = jnp.zeros((16, 2 * LANES), F32)
    for n, (du, dv) in enumerate(SHIFTS):
        dx0 = dx0 + block_shift(dxcat[n * 16 : n * 16 + 16], -du, -dv)
    x0_ref[...] = dx0
    for g in range(2):
        for p in range(OWN):
            for i4 in range(4):
                base = g * 32 + p * 16 + i4 * 4
                at = g * LANES + p * 256 + i4 * 64
                for pj in range(4):
                    if g == 0:
                        for pi in range(4):
                            fm_ref[base + pi : base + pi + 1, pj * 64 : pj * 64 + 64] = x0_ref[
                                pi * 4 + pj : pi * 4 + pj + 1, at : at + 64
                            ]
                    else:
                        fm_ref[base : base + 4, pj * 64 : pj * 64 + 64] = x0_ref[pj * 4 : pj * 4 + 4, at : at + 64]
    dfm = dot_exact(fm_ref[...], perm, 1)
    dfm1 = jnp.where(valid, dfm[:32], 0.0) * (1.0 / REGIONS)
    dfm2 = jnp.where(valid, dfm[32:], 0.0) * (1.0 / REGIONS)

    def scatter_sum(parts):
        total = acc_ref[pl.ds(pl.multiple_of(chip * 48, 48), 48)]
        for d in range(1, 16):
            source = (chip + 16 - d) % 16
            scatter_arrives(source, parts).wait_recv()
            total = total + parts[source].astype(F32)
        part_b[place] = total

    @pl.when(chip == 15)
    def _():
        scatter_sum(part_a)

    @pl.when(chip != 15)
    def _():
        scatter_sum(part_half)

    for d in range(1, 8):
        column_copy(d).start()

    sum1 = q1_ref[...].reshape(OWN, REGIONS, FRAMES, 256)
    q1 = dfm1.reshape(OWN, 1, FRAMES, 256) / sum1
    rowperm = ones_where(frame_rows((1, ROWS)) == iota((320, ROWS), 0))
    for s in range(REGIONS):
        q2 = (dfm2 / q2_ref[s]).reshape(OWN, 1, FRAMES, 256)
        grad = (e_ref[s].reshape(OWN, REGIONS, FRAMES, 256) * (q1 + q2)).reshape(ROWS, 256).astype(BF16)
        grad_ref[s] = dot(rowperm, grad, 1, 0).astype(BF16)

    def way(n):
        return 1 if n < 2 else -1

    def rep_copy(kind, n):
        d = -way(n) if kind == 2 else way(n)
        of = (rep + 2) % 4 if kind == 0 else (rep + d + 4) % 4
        return pltpu.make_async_remote_copy(
            src_ref=send_ref.at[of, :, pl.ds(n * CHUNK, CHUNK)],
            dst_ref=recv_ref.at[kind, :, pl.ds(n * CHUNK, CHUNK)],
            send_sem=rs.at[n * 3 + kind],
            recv_sem=rr.at[n * 3 + kind],
            device_id=(owner, (rep + d + 4) % 4),
            device_id_type=MESH,
        )

    order = (0, 2, 1, 3)
    for n in order:
        cols = slice(n * CHUNK, (n + 1) * CHUNK)
        product = jnp.zeros((320, CHUNK), F32)
        for s in range(REGIONS):
            pbs = pb_ref[:, s, :, cols].reshape(SEEN * FRAMES, CHUNK)
            product = product + dot(grad_ref[s], pbs, 1, 0)
        product = product.reshape(SIDE, 80, CHUNK)
        rg_ref[:, :, cols] = product
        send_ref[:, :, cols] = product.astype(BF16)
        rep_copy(0, n).start()
        rep_copy(2, n).start()
        if n == 2:
            for d in range(1, 8):
                pltpu.make_async_remote_copy(
                    src_ref=part_b.at[(place + 8 - d) % 8],
                    dst_ref=part_b.at[(place + 8 - d) % 8],
                    send_sem=sb.at[d - 1],
                    recv_sem=rb.at[d - 1],
                    device_id=in_column(d),
                    device_id_type=MESH,
                ).wait_recv()
            total = part_b[0]
            for q in range(1, 8):
                total = total + part_b[q]

            @pl.when(chip == 15)
            def _():
                all_ref[720:768] = total
                for d in range(1, 16):
                    gather_copy(d, chip, True).start()

            @pl.when(chip != 15)
            def _():
                all_half[pl.ds(pl.multiple_of(chip * 48, 48), 48)] = total.astype(BF16)
                for d in range(1, 16):
                    gather_copy(d, chip, False).start()

    for n in order:
        cols = slice(n * CHUNK, (n + 1) * CHUNK)
        of = (rep + way(n) + 4) % 4
        rep_copy(0, n).wait_recv()
        send_ref[of, :, cols] = (rg_ref[of, :, cols] + recv_ref[0, :, cols].astype(F32)).astype(BF16)
        rep_copy(1, n).start()
    for d in range(1, 16):
        source = (chip + 16 - d) % 16

        @pl.when(source == 15)
        def _(d=d, source=source):
            gather_copy(d, source, True).wait_recv()

        @pl.when(source != 15)
        def _(d=d, source=source):
            gather_copy(d, source, False).wait_recv()

    all_ref[0:720] = all_half[0:720].astype(F32)
    table = all_ref[ROW_PS:ROW_ALL]
    found = jnp.zeros((1, 512), F32)
    for p in range(OWN):
        left = dot(ones_where(iota((32, VIDEOS), 1) == 2 * iota((32, VIDEOS), 0) + p), hots_ref[0], 1, 0)
        value = dot_exact(table[:, p * 64 : p * 64 + 64], hots_ref[1])
        found = found + jnp.sum(left * value, axis=0, keepdims=True)
    ps_ref[...] = found
    own = own_ref[...]
    inverse = lax.rsqrt(jnp.sum(own * own, axis=1, keepdims=True) + norm_eps)
    along = jnp.zeros((80, 1), F32)
    for n in order:
        cols = slice(n * CHUNK, (n + 1) * CHUNK)
        rep_copy(2, n).wait_recv()
        rep_copy(1, n).wait_recv()
        total = rg_ref[rep, :, cols] + recv_ref[2, :, cols].astype(F32) + recv_ref[1, :, cols].astype(F32)
        rg_ref[rep, :, cols] = total
        along = along + jnp.sum(own_ref[:, cols] * total, axis=1, keepdims=True)
    back = along * inverse * inverse * inverse
    for n in range(CHUNKS):
        cols = slice(n * CHUNK, (n + 1) * CHUNK)
        result = rg_ref[rep, :, cols] * inverse - own_ref[:, cols] * back
        for q in range(18):
            fg_ref[q, :, cols] = result[q * 4 : q * 4 + 4]

    for copy, arriving in crossings:
        copy.wait_send()
    for m in range(2):
        for r in [ring1[m]] + [ring2[m][du] for du in offsets]:
            for name in ("send_plus", "send_minus", "fwd_plus", "fwd_minus"):
                r[name].wait_send()

    @pl.when(core == kc)
    def _():
        for copy in sent:
            copy.wait_send()

    for d in (1, 2, 3):
        c_copy(d, rep).wait_send()
        for n in range(CHUNKS):
            rep_copy(d - 1, n).wait_send()
    for to in range(16):

        @pl.when(chip != to)
        def _(to=to):
            scatter_copy(to).wait_send()

    @pl.when(chip == 15)
    def _():
        for d in range(1, 16):
            gather_copy(d, chip, True).wait_send()

    @pl.when(chip != 15)
    def _():
        for d in range(1, 16):
            gather_copy(d, chip, False).wait_send()

    for d in range(1, 8):
        column_copy(d).wait_send()


def whole(*args):
    return pl.pallas_call(
        whole_kernel,
        name="training_step",
        out_shape=(
            jax.ShapeDtypeStruct((OWN * REGIONS, 4, WIDTH), F32),
            jax.ShapeDtypeStruct((1, 512), F32),
            jax.ShapeDtypeStruct((ROW_ALL, 128), F32),
        ),
        in_specs=[ANY_SPEC] + [VMEM_SPEC] * 5 + [ANY_SPEC] * 2 + [VMEM_SPEC],
        out_specs=(VMEM_SPEC,) * 3,
        scratch_shapes=[
            pltpu.VMEM((OWN, REGIONS, FRAMES, WIDTH), F32),
            pltpu.VMEM((9, 32, 64), F32),
            pltpu.VMEM((576, C3), F32),
            pltpu.VMEM((OWN, REGIONS, FRAMES, WIDTH), BF16),
            pltpu.VMEM((SEEN, REGIONS, FRAMES, WIDTH), BF16),
            pltpu.VMEM((SIDE, VIDEOS, VIDEOS), F32),
            pltpu.VMEM((2, VIDEOS, 512), BF16),
            pltpu.VMEM((144, 512), F32),
            pltpu.VMEM((512, 256), F32),
            pltpu.VMEM((80, WIDTH), F32),
            pltpu.VMEM((REGIONS, ROWS, 256), F32),
            pltpu.VMEM((ROWS, 256), F32),
            pltpu.VMEM((REGIONS, 32, 256), F32),
            pltpu.VMEM((64, 256), F32),
            pltpu.VMEM((16, 2 * LANES), F32),
            pltpu.VMEM((REGIONS, 320, 256), BF16),
            pltpu.VMEM((ROW_ALL, 128), F32),
            pltpu.VMEM((SIDE, 80, WIDTH), F32),
            pltpu.VMEM((SIDE, 80, WIDTH), BF16),
            pltpu.VMEM((3, 80, WIDTH), BF16),
            pltpu.VMEM((16, 48, 128), F32),
            pltpu.VMEM((8, 48, 128), F32),
            pltpu.VMEM((720, 128), BF16),
            pltpu.VMEM((16, 48, 128), BF16),
            pltpu.VMEM((ROW_ALL, 128), BF16),
        ]
        + [
            pltpu.SemaphoreType.DMA((n,))
            for n in (40, 40, 30, 30, 3, 3, 1, 4, 3, 3, 3 * CHUNKS, 3 * CHUNKS, 16, 16, 7, 7, 15, 15)
        ],
        compiler_params=pltpu.CompilerParams(
            collective_id=0, has_side_effects=True, vmem_limit_bytes=58 * 2**20
        ),
    )(*args)


def outputs_kernel(fg_in, ps_in, all_in, ps_ref, fg_ref, g1_ref, g2_ref, g3_ref, gl_ref):
    fg_ref[...] = fg_in[...]
    ps_ref[...] = ps_in[...]
    g3_ref[...] = all_in[0:ROW_TWO]
    for n in range(18):
        at = ROW_TWO + (n % 9) * 16
        g2_ref[n // 2, (n % 2) * 16 : (n % 2) * 16 + 16, :] = all_in[at : at + 16, (n // 9) * 64 : (n // 9) * 64 + 64]
    for n in range(9):
        g1_ref[n // 3, n % 3] = all_in[ROW_ONE + n : ROW_ONE + n + 1, 0:32]
    gl_ref[...] = all_in[ROW_ONE + 9 : ROW_ONE + 10]


def outputs(fg, ps, summed):
    return pl.pallas_call(
        outputs_kernel,
        name="outputs",
        out_shape=(
            jax.ShapeDtypeStruct((1, 512), F32),
            jax.ShapeDtypeStruct((OWN * REGIONS, 4, WIDTH), F32),
            jax.ShapeDtypeStruct((3, 3, 1, 32), F32),
            jax.ShapeDtypeStruct((9, 32, 64), F32),
            jax.ShapeDtypeStruct((576, C3), F32),
            jax.ShapeDtypeStruct((1, C3), F32),
        ),
        in_specs=[VMEM_SPEC] * 3,
        out_specs=(VMEM_SPEC,) * 6,
    )(fg, ps, summed)


def local(
    features, frame_counts, video_rows, pair_list, pair_cotangent, kernel_one, kernel_two, kernel_three, kernel_last
):
    fg, ps, summed = whole(
        features.transpose(0, 2, 1, 3),
        frame_counts.reshape(1, VIDEOS),
        video_rows.reshape(1, VIDEOS),
        pair_list.T,
        pair_cotangent.reshape(1, 512),
        kernel_one,
        kernel_two.reshape(9, 32, 64),
        kernel_three.reshape(576, C3),
        kernel_last.reshape(1, C3),
    )
    ps, fg, g1, g2, g3, gl = outputs(fg, ps, summed)
    return (
        ps.reshape(512),
        fg.reshape(OWN, REGIONS, 4, WIDTH).transpose(0, 2, 1, 3),
        g1,
        g2.reshape(3, 3, 32, 64),
        g3.reshape(3, 3, 64, C3),
        gl.reshape(C3),
    )


def solution(mesh):
    placed = (P("owner", None, None, None), P(), P(), P("rep", None), P("rep"), P(), P(), P(), P())
    return jax.shard_map(
        local,
        mesh=mesh,
        in_specs=placed,
        out_specs=(P("rep"), P("owner", "rep", None, None), P(), P(), P(), P()),
        check_vma=False,
    )
```

```python
import jax
import jax.numpy as jnp
from jax import lax
from jax.experimental import pallas as pl
from jax.experimental.pallas import tpu as pltpu
from jax.sharding import PartitionSpec as P

MESH = pl.DeviceIdType.MESH
VMEM_SPEC = pl.BlockSpec(memory_space=pltpu.VMEM)
ANY_SPEC = pl.BlockSpec(memory_space=pl.ANY)
F32 = jnp.float32
BF16 = jnp.bfloat16

REGIONS = 9
FRAMES = 16
WIDTH = 2048
VIDEOS = 64
SIDE = 4
OWN = 2
SEEN = 16
ROWS = OWN * REGIONS * FRAMES
LANES = OWN * SEEN * 16

ROW_TWO = 576
ROW_ONE = 720
ROW_PS = 736
ROW_ALL = 768

region_temp = 0.1
loss_scale = 131072.0
norm_eps = 1e-06
C3 = 128


CHUNKS = 4
CHUNK = WIDTH // CHUNKS


def split2(v):
    high = v.astype(BF16)
    return high, (v - high.astype(F32)).astype(BF16)


def dot(a, b, ca, cb):
    return lax.dot_general(a, b, (((ca,), (cb,)), ((), ())), preferred_element_type=F32)


def dot3(a, b, ca, cb):
    (ah, al), (bh, bl) = a, b
    return dot(ah, bh, ca, cb) + dot(ah, bl, ca, cb) + dot(al, bh, ca, cb)


def dot2(a, b, ca, cb):
    return dot(a[0], b, ca, cb) + dot(a[1], b, ca, cb)


def dot_exact(v, chosen, cb=0):
    high = v.astype(BF16)
    rest = v - high.astype(F32)
    mid = rest.astype(BF16)
    low = (rest - mid.astype(F32)).astype(BF16)
    return dot(high, chosen, 1, cb) + dot(mid, chosen, 1, cb) + dot(low, chosen, 1, cb)


def lane_of(shape):
    return lax.broadcasted_iota(jnp.int32, shape, len(shape) - 1)


def moved(v, di, dj):
    if di == 0 and dj == 0:
        return v
    out = pltpu.roll(v, (-(di * 64 + dj)) % LANES, 1)
    lane = lane_of((1, LANES))
    i4, j4 = (lane // 64) % 4, lane % 4
    ok = (i4 + di >= 0) & (i4 + di < 4) & (j4 + dj >= 0) & (j4 + dj < 4)
    return jnp.where(ok, out, 0.0)


def block_shift(v, du, dv):
    return jnp.concatenate([moved(v[:, :LANES], du, dv), moved(v[:, LANES:], dv, du)], axis=1)


def quad_sum(v, stride):
    lane = lane_of((1, LANES))
    for step in (stride, 2 * stride):
        low = (lane // step) % 2 == 0
        v = v + jnp.where(low, pltpu.roll(v, LANES - step, 1), pltpu.roll(v, step, 1))
    return v


def silu_pair(v):
    s = 1.0 / (1.0 + jnp.exp(-v))
    return v * s, s * (1.0 + v * (1.0 - s))


def iota(shape, axis):
    return lax.broadcasted_iota(jnp.int32, shape, axis)


def ones_where(condition):
    return jnp.where(condition, 1.0, 0.0).astype(BF16)


def tap_rows(ti, tj):
    plane = lane_of((1, 512)) // 32
    ei, ej = plane // 4 + ti + 3, plane % 4 + tj + 3
    return ((ei // 4) * 3 + ej // 4) * 16 + (ei % 4) * 4 + ej % 4


SHIFTS = [(du, dv) for du in (-1, 0, 1) for dv in (-1, 0, 1)]
EXT2 = [(1, -1), (0, 0), (1, 0), (0, 1)]


def whole_kernel(
    x_hbm, counts_ref, vrows_ref, pairs_ref, cot_ref, k1_ref, k2_hbm, k3_hbm, kl_ref,
    fg_ref, ps_ref, all_ref,
    x_ref, k2_ref, k3_ref, pa_ref, pb_ref, call_ref, hots_ref, w1_ref, w2_ref, own_ref,
    e_ref, q1_ref, q2_ref, fm_ref, x0_ref, grad_ref, acc_ref, rg_ref, send_ref, recv_ref, part_a, part_b, acc_half, part_half, all_half,
    ssem, rsem, dssem, drsem, csem, crsem, lsem, insem, hs, hr, rs, rr, sa, ra, sb, rb, sc, rc,
):
    owner = lax.axis_index("owner")
    rep = lax.axis_index("rep")
    z, x, core = owner // 8, (owner // 2) % 4, owner % 2
    chip = owner // 2
    place = core * 4 + rep
    other = owner + 1 - 2 * core

    def in_plane(d):
        return (((chip + d) % 16) * 2 + core, rep)

    def in_column(d):
        to = (place + d) % 8
        return (chip * 2 + to // 4, to % 4)

    def shifted(axis, d):
        if axis == 0:
            return z * 8 + ((x + d + 4) % 4) * 2 + core
        return ((z + d + 4) % 4) * 8 + x * 2 + core

    def chip_at(first, du, dv):
        dx, dz = (du, dv) if first == 0 else (dv, du)
        return ((z + dz + 4) % 4) * 4 + (x + dx + 4) % 4

    loads = [pltpu.make_async_copy(x_hbm.at[p], x_ref.at[p], insem.at[p]) for p in range(OWN)]
    loads.append(pltpu.make_async_copy(k2_hbm, k2_ref, insem.at[2]))
    loads.append(pltpu.make_async_copy(k3_hbm, k3_ref, insem.at[3]))
    for load in loads:
        load.start()
    barrier = pltpu.get_barrier_semaphore()
    for axis in (0, 1):
        for d in (1, -1):
            pl.semaphore_signal(barrier, inc=1, device_id=(shifted(axis, d), rep), device_id_type=MESH)
    for d in range(1, 8):
        pl.semaphore_signal(barrier, inc=1, device_id=in_column(d), device_id_type=MESH)

    for p in range(OWN):
        loads[p].wait()
        values = x_ref[p]
        summed = jnp.sum(values * values, axis=-1, keepdims=True) + norm_eps
        pa_ref[p] = (values * lax.rsqrt(summed)).astype(BF16)

    pl.semaphore_wait(barrier, 11)

    kc, kp = rep // 2, rep % 2
    local = pltpu.make_async_copy(pa_ref.at[kp], pb_ref.at[chip], lsem.at[0])

    def own_lanes(to, m):
        return pl.ds(pl.multiple_of(to * 1024 + m * 512, 512), 512)

    def to_other(n, lanes):
        return pltpu.make_async_remote_copy(
            src_ref=pa_ref.at[kp, :, :, lanes],
            dst_ref=pb_ref.at[chip, :, :, lanes],
            send_sem=hs.at[n],
            recv_sem=hr.at[n],
            device_id=(other, rep),
            device_id_type=MESH,
        )

    sent = [to_other(0, own_lanes(1 - core, 0)), to_other(1, own_lanes(1 - core, 1))]
    sent.append(to_other(2, pl.ds(pl.multiple_of(core * 1024, 1024), 1024)))
    got = [to_other(0, own_lanes(core, 0)), to_other(1, own_lanes(core, 1))]
    got.append(to_other(2, pl.ds(pl.multiple_of((1 - core) * 1024, 1024), 1024)))

    def piece(block, m, half):
        if half is None:
            lanes = pl.ds(pl.multiple_of(core * 1024 + m * 512, 512), 512)
        else:
            lanes = pl.ds(pl.multiple_of(core * 1024 + m * 512 + half * 256, 256), 256)
        return pb_ref.at[block, :, :, lanes]

    def ring(m, index, first, du, along):
        base = (m * 5 + index) * 4
        axis = first if along == 0 else 1 - first

        def block(d):
            return chip_at(first, d, 0) if along == 0 else chip_at(first, du, d)

        def copy(slot, source, d, half, prepared=False):
            ref = piece(source, m, half)
            return pltpu.make_async_remote_copy(
                src_ref=pa_ref.at[kp, :, :, own_lanes(core, m)] if prepared else ref,
                dst_ref=ref,
                send_sem=ssem.at[base + slot],
                recv_sem=rsem.at[base + slot],
                device_id=(shifted(axis, d), rep),
                device_id_type=MESH,
            )

        return dict(
            first_plus=copy(0, block(0), 1, None, True),
            first_minus=copy(1, block(0), -1, None, True),
            send_plus=copy(0, block(0), 1, None),
            send_minus=copy(1, block(0), -1, None),
            fwd_plus=copy(2, block(-1), 1, 0),
            fwd_minus=copy(3, block(1), -1, 1),
            from_minus=copy(0, block(-1), 1, None),
            from_plus=copy(1, block(1), -1, None),
            far_a=copy(2, block(2), 1, 0),
            far_b=copy(3, block(2), -1, 1),
            block=block,
        )

    crossings = []

    def cross(m, block):
        n = len(crossings)
        ref = piece(block, m, None)
        copy = pltpu.make_async_remote_copy(
            src_ref=ref,
            dst_ref=ref,
            send_sem=dssem.at[n],
            recv_sem=drsem.at[n],
            device_id=(other, rep),
            device_id_type=MESH,
        )
        copy.start()
        lanes = pl.ds(pl.multiple_of((1 - core) * 1024 + m * 512, 512), 512)
        theirs = pb_ref.at[block, :, :, lanes]
        arriving = pltpu.make_async_remote_copy(
            src_ref=theirs,
            dst_ref=theirs,
            send_sem=dssem.at[n],
            recv_sem=drsem.at[n],
            device_id=(other, rep),
            device_id_type=MESH,
        )
        crossings.append((copy, arriving))

    def c_copy(d, at):
        return pltpu.make_async_remote_copy(
            src_ref=call_ref.at[at],
            dst_ref=call_ref.at[at],
            send_sem=csem.at[d - 1],
            recv_sem=crsem.at[d - 1],
            device_id=(owner, (rep + d) % 4),
            device_id_type=MESH,
        )

    def make_pairs():
        by_row = ones_where(iota((VIDEOS, VIDEOS), 0) == vrows_ref[...])
        videos = iota((VIDEOS, 512), 0)
        row_a = dot(by_row, ones_where(videos == pairs_ref[0:1, :]), 1, 0)
        row_b = dot(by_row, ones_where(videos == pairs_ref[1:2, :]), 1, 0)
        hots_ref[0] = row_a.astype(BF16)
        hots_ref[1] = row_b.astype(BF16)
        call_ref[rep] = dot_exact(row_a * cot_ref[...], row_b.astype(BF16), 1)
        for d in (1, 2, 3):
            c_copy(d, rep).start()

    def make_weights():
        loads[2].wait()
        loads[3].wait()
        k1 = jnp.concatenate([k1_ref[n // 3, n % 3] for n in range(9)], axis=0)
        tiled = dot_exact(k1, ones_where(iota((32, 512), 1) % 32 == iota((32, 512), 0)))
        at = iota((144, 512), 0)
        w1 = jnp.zeros((144, 512), F32)
        for ti in range(3):
            for tj in range(3):
                w1 = jnp.where(at == tap_rows(ti, tj), tiled[ti * 3 + tj : ti * 3 + tj + 1], w1)
        w1_ref[...] = w1
        w2_ref[...] = jnp.zeros((512, 256), F32)
        for ti in range(3):
            for tj in range(3):
                for pi in range(2):
                    for pj in range(2):
                        row = ((pi + ti) * 4 + pj + tj) * 32
                        col = (pi * 2 + pj) * 64
                        w2_ref[row : row + 32, col : col + 64] = k2_ref[ti * 3 + tj]

    def frame_rows(shape):
        n = lane_of(shape)
        return ((n % 16) // 4) * 80 + (n // 144) * 36 + ((n % 144) // 16) * 4 + n % 4

    def make_own():
        chosen = ones_where(frame_rows((1, ROWS)) - rep * 80 == iota((80, ROWS), 0))
        for n in range(4):
            v = x_ref[:, :, :, n * 512 : n * 512 + 512].reshape(ROWS, 512)
            high = v.astype(BF16)
            rest = v - high.astype(F32)
            mid = rest.astype(BF16)
            low = (rest - mid.astype(F32)).astype(BF16)
            own_ref[:, n * 512 : n * 512 + 512] = (
                dot(chosen, high, 1, 0) + dot(chosen, mid, 1, 0) + dot(chosen, low, 1, 0)
            )

    offsets = (0, -1, 1, 2)
    ring1 = [ring(m, 0, m, 0, 0) for m in range(2)]
    ring2 = [{du: ring(m, 1 + n, m, du, 1) for n, du in enumerate(offsets)} for m in range(2)]

    def begin(r):
        r["send_plus"].start()
        r["send_minus"].start()

    @pl.when(core == kc)
    def _():
        sent[0].start()
        sent[1].start()
        for r in (ring1[0], ring1[1], ring2[0][0], ring2[1][0]):
            r["first_plus"].start()
            r["first_minus"].start()
        local.start()
        sent[2].start()

    @pl.when(core != kc)
    def _():
        for m in range(2):
            got[m].wait_recv()
            begin(ring1[m])
            begin(ring2[m][0])

    for d, arrive, forward in ((-1, "from_minus", "fwd_plus"), (1, "from_plus", "fwd_minus")):
        for m in range(2):
            ring1[m][arrive].wait_recv()
            ring1[m][forward].start()
            begin(ring2[m][d])
            cross(m, ring1[m]["block"](d))
    for m in range(2):
        ring1[m]["far_a"].wait_recv()
        ring1[m]["far_b"].wait_recv()
        begin(ring2[m][2])
        cross(m, ring1[m]["block"](2))
    beside = {0: make_pairs, -1: make_weights, 1: make_own}
    for du in offsets:
        for d, arrive, forward in ((-1, "from_minus", "fwd_plus"), (1, "from_plus", "fwd_minus")):
            for m in range(2):
                r = ring2[m][du]
                r[arrive].wait_recv()
                r[forward].start()
                cross(m, r["block"](d))
        if du in beside:
            beside[du]()
    for du in offsets:
        for m in range(2):
            r = ring2[m][du]
            r["far_a"].wait_recv()
            r["far_b"].wait_recv()
            cross(m, r["block"](2))

    for d in (1, 2, 3):
        c_copy(d, (rep + 4 - d) % 4).wait_recv()
    cots = (call_ref[0] + call_ref[1] + call_ref[2] + call_ref[3]) * loss_scale
    by_row = ones_where(iota((VIDEOS, VIDEOS), 0) == vrows_ref[...])
    lengths = dot(jnp.broadcast_to(counts_ref[...], (8, VIDEOS)).astype(F32).astype(BF16), by_row, 1, 1)
    lengths_half = lengths.astype(BF16)
    at = iota((VIDEOS, LANES), 0)
    lane = iota((1, LANES), 1)
    len_a = dot(lengths_half, ones_where(at == 2 * owner + lane // 256), 1, 0)[0:1]
    pick_b = ones_where(at == 4 * ((lane % 64) // 4) + rep)
    len_b = dot(lengths_half, pick_b, 1, 0)[0:1]
    ok_a = ((lane // 64) % 4 * 4).astype(F32) < len_a
    ok_b = (lane % 4 * 4).astype(F32) < len_b
    inv_a = 1.0 / quad_sum(jnp.where(ok_a, 1.0, 0.0), 64)
    inv_b = 1.0 / quad_sum(jnp.where(ok_b, 1.0, 0.0), 1)
    mine = iota((8, VIDEOS), 1) == 2 * owner + iota((8, VIDEOS), 0) % 2
    mine = ones_where(mine)
    high = cots.astype(BF16)
    rest = cots - high.astype(F32)
    mid = rest.astype(BF16)
    low = (rest - mid.astype(F32)).astype(BF16)
    cot = []
    for cb in (0, 1):
        c_rows = dot(mine, high, 1, cb) + dot(mine, mid, 1, cb) + dot(mine, low, 1, cb)
        spread = dot_exact(c_rows, pick_b)
        cot.append(jnp.where(lane < 256, spread[0:1], spread[1:2]))
    frames_b = iota((1, 256), 1)
    len_vb = dot(lengths_half, ones_where(iota((VIDEOS, 256), 0) == 4 * (frames_b // 16) + rep), 1, 0)[0:1]
    valid_b = (frames_b % 16).astype(F32) < len_vb
    rows_32 = iota((32, VIDEOS), 0)
    len_va = jnp.sum(
        jnp.where(iota((32, VIDEOS), 1) == 2 * owner + rows_32 // 16, jnp.broadcast_to(lengths[0:1], (32, VIDEOS)), 0.0),
        axis=1,
        keepdims=True,
    )
    valid = ((iota((32, 256), 0) % 16).astype(F32) < len_va) & valid_b

    @pl.when(core == kc)
    def _():
        local.wait()

    def half_scores(half, s):
        lanes = pl.ds(pl.multiple_of(half * 1024, 1024), 1024)
        left = pa_ref[:, :, :, lanes].reshape(ROWS, 1024)
        return dot(left, pb_ref[:, s, :, lanes].reshape(SEEN * FRAMES, 1024), 1, 1)

    for s in range(REGIONS):
        e_ref[s] = half_scores(core, s)
    for copy, arriving in crossings:
        arriving.wait_recv()

    @pl.when(core != kc)
    def _():
        got[2].wait_recv()

    sum1 = jnp.zeros((ROWS, 256), F32)
    fm2 = jnp.zeros((32, 256), F32)
    for s in range(REGIONS):
        e = jnp.exp((e_ref[s] + half_scores(1 - core, s)) * (1.0 / region_temp))
        e_ref[s] = e
        sum1 = sum1 + e
        sum2 = jnp.sum(e.reshape(OWN, REGIONS, FRAMES, 256), axis=1).reshape(32, 256)
        q2_ref[s] = sum2
        fm2 = fm2 + jnp.log(sum2)
    q1_ref[...] = sum1
    fm1 = jnp.sum(jnp.log(sum1).reshape(OWN, REGIONS, FRAMES, 256), axis=1).reshape(32, 256)
    scale = region_temp / REGIONS
    fm = jnp.concatenate([jnp.where(valid, fm1 * scale, 0.0), jnp.where(valid, fm2 * scale, 0.0)], axis=0)
    spot = iota((256, 256), 0)
    perm = ones_where((spot % 4) * 64 + (spot // 16) * 4 + (spot % 16) // 4 == iota((256, 256), 1))
    fm_ref[...] = dot_exact(fm, perm)
    for g in range(2):
        for p in range(OWN):
            for i4 in range(4):
                base = g * 32 + p * 16 + i4 * 4
                at = g * LANES + p * 256 + i4 * 64
                for pj in range(4):
                    if g == 0:
                        for pi in range(4):
                            x0_ref[pi * 4 + pj : pi * 4 + pj + 1, at : at + 64] = fm_ref[
                                base + pi : base + pi + 1, pj * 64 : pj * 64 + 64
                            ]
                    else:
                        x0_ref[pj * 4 : pj * 4 + 4, at : at + 64] = fm_ref[base : base + 4, pj * 64 : pj * 64 + 64]

    x0 = x0_ref[...]
    xcat = split2(jnp.concatenate([block_shift(x0, du, dv) for du, dv in SHIFTS], axis=0))
    w1 = split2(w1_ref[...])
    stacked = jnp.concatenate([xcat[0], xcat[0], xcat[1]], axis=0)
    h1, ds1 = silu_pair(dot(jnp.concatenate([w1[0], w1[1], w1[0]], axis=0), stacked, 0, 0))
    pooled1 = []
    for qi in range(2):
        for qj in range(2):
            parts = [
                h1[((2 * qi + a) * 4 + 2 * qj + b) * 32 : ((2 * qi + a) * 4 + 2 * qj + b) * 32 + 32]
                for a in range(2)
                for b in range(2)
            ]
            pooled1.append((parts[0] + parts[1] + parts[2] + parts[3]) * 0.25)
    h1cat = split2(
        jnp.concatenate(
            [block_shift(pooled1[qi * 2 + qj], du, dv) for qi, du in EXT2 for qj, dv in EXT2], axis=0
        )
    )
    w2 = split2(w2_ref[...])
    h2, ds2 = silu_pair(dot3(w2, h1cat, 0, 0))
    pooled2 = (h2[0:64] + h2[64:128] + h2[128:192] + h2[192:256]) * 0.25
    h2cat = split2(jnp.concatenate([block_shift(pooled2, du, dv) for du, dv in SHIFTS], axis=0))
    w3 = split2(k3_ref[...])
    both = dot(jnp.concatenate([w3[0], w3[1]], axis=1), h2cat[0], 0, 0)
    h3, ds3 = silu_pair(both[:C3] + both[C3:] + dot(w3[0], h2cat[1], 0, 0))
    kl = jnp.sum(jnp.where(iota((C3, C3), 0) == iota((C3, C3), 1), kl_ref[...], 0.0), axis=1, keepdims=True)
    out = jnp.tanh(jnp.sum(h3 * kl, axis=0, keepdims=True))

    dz = []
    for g in range(2):
        o = out[:, g * LANES : (g + 1) * LANES]
        rows_ok, inv = ((ok_a, inv_a), (ok_b, inv_b))[g]
        weighted = jnp.where(ok_a & ok_b, jnp.exp(o * (1.0 / region_temp)), 0.0)
        row_sums = quad_sum(weighted, 1 if g == 0 else 64) + jnp.where(rows_ok, 0.0, 1.0)
        if g == 0:
            best = jnp.where(rows_ok, region_temp * jnp.log(row_sums), 0.0)
            ps = quad_sum(best, 64) * inv
        dout = cot[g] * inv * weighted / row_sums
        dz.append(dout * (1.0 - o * o))
    dz = jnp.concatenate(dz, axis=1)

    def scatter_copy(to):
        return pltpu.make_async_remote_copy(
            src_ref=acc_ref.at[720:768] if to == 15 else acc_half.at[to * 48 : to * 48 + 48],
            dst_ref=part_a.at[chip] if to == 15 else part_half.at[chip],
            send_sem=sa.at[to],
            recv_sem=ra.at[chip],
            device_id=(to * 2 + core, rep),
            device_id_type=MESH,
        )

    def scatter_start(to):
        @pl.when(chip != to)
        def _():
            scatter_copy(to).start()

    def scatter_arrives(source, parts):
        return pltpu.make_async_remote_copy(
            src_ref=parts.at[source],
            dst_ref=parts.at[source],
            send_sem=sa.at[source],
            recv_sem=ra.at[source],
            device_id=(((chip + 1) % 16) * 2 + core, rep),
            device_id_type=MESH,
        )

    def column_copy(d):
        return pltpu.make_async_remote_copy(
            src_ref=part_b.at[place],
            dst_ref=part_b.at[place],
            send_sem=sb.at[d - 1],
            recv_sem=rb.at[d - 1],
            device_id=in_column(d),
            device_id_type=MESH,
        )

    def gather_copy(d, at, last):
        rows = pl.ds(pl.multiple_of(at * 48, 48), 48)
        block = all_ref.at[720:768] if last else all_half.at[rows]
        return pltpu.make_async_remote_copy(
            src_ref=block,
            dst_ref=block,
            send_sem=sc.at[d - 1],
            recv_sem=rc.at[d - 1],
            device_id=in_plane(d),
            device_id_type=MESH,
        )

    def first(pair):
        return pair[0][:, :LANES], pair[1][:, :LANES]

    lane = lane_of((1, 128))
    row = jnp.where(lane % 4 == rep, jnp.concatenate([ps[:, 0:64], ps[:, 256:320]], axis=1), 0.0)
    at = lax.broadcasted_iota(jnp.int32, (32, 128), 0)
    acc_ref[ROW_PS : ROW_PS + 32] = jnp.where(at == owner, row, 0.0)
    dz_first = jnp.broadcast_to(dz[:, :LANES], (8, LANES))
    gl = dot3(split2(dz_first), split2(h3[:, :LANES]), 1, 1)
    dpre3, dpre3_low = split2(dz * kl * ds3)
    acc_ref[0:576] = dot2(first(h2cat), dpre3[:, :LANES], 1, 1) * (1.0 / loss_scale)
    acc_half[0:576] = acc_ref[0:576].astype(BF16)
    for to in range(12):
        scatter_start(to)
    dh2cat = dot(jnp.concatenate([w3[0], w3[1]], axis=1), jnp.concatenate([dpre3, dpre3], axis=0), 1, 0)
    dh2cat = dh2cat + dot(w3[0], dpre3_low, 1, 0)
    dpool2 = jnp.zeros((64, 2 * LANES), F32)
    for n, (du, dv) in enumerate(SHIFTS):
        dpool2 = dpool2 + block_shift(dh2cat[n * 64 : n * 64 + 64], -du, -dv)
    dpool2 = dpool2 * 0.25
    dpre2, dpre2_low = split2(jnp.concatenate([dpool2, dpool2, dpool2, dpool2], axis=0) * ds2)
    g2 = dot2(first(h1cat), dpre2[:, :LANES], 1, 1)
    for ti in range(3):
        for tj in range(3):
            total = jnp.zeros((32, 64), F32)
            for pi in range(2):
                for pj in range(2):
                    row = ((pi + ti) * 4 + pj + tj) * 32
                    col = (pi * 2 + pj) * 64
                    total = total + g2[row : row + 32, col : col + 64]
            total = total * (1.0 / loss_scale)
            for half in range(2):
                n = (ti * 3 + tj) * 2 + half
                at = ROW_TWO + (n % 9) * 16
                acc_ref[at : at + 16, (n // 9) * 64 : (n // 9) * 64 + 64] = total[half * 16 : half * 16 + 16]
    dh1cat = dot2(w2, dpre2, 1, 0) + dot(w2[0], dpre2_low, 1, 0)
    dpool1 = [jnp.zeros((32, 2 * LANES), F32) for _ in range(4)]
    n = 0
    for qi, du in EXT2:
        for qj, dv in EXT2:
            dpool1[qi * 2 + qj] = dpool1[qi * 2 + qj] + block_shift(dh1cat[n * 32 : n * 32 + 32], -du, -dv)
            n += 1
    dpool1 = [d * 0.25 for d in dpool1]
    dpre1, dpre1_low = split2(
        jnp.concatenate([dpool1[(pi // 2) * 2 + pj // 2] for pi in range(4) for pj in range(4)], axis=0) * ds1
    )
    g1 = dot(jnp.concatenate(first(xcat), axis=0), dpre1[:, :LANES], 1, 1)
    g1 = g1[:144] + g1[144:]
    at = iota((144, 512), 0)
    rows = []
    for ti in range(3):
        for tj in range(3):
            v = jnp.sum(jnp.where(at == tap_rows(ti, tj), g1, 0.0), axis=0, keepdims=True)
            v = v[:, 0:128] + v[:, 128:256] + v[:, 256:384] + v[:, 384:512]
            v = v + pltpu.roll(v, 64, 1)
            rows.append(v + pltpu.roll(v, 32, 1))
    rows.append(gl[0:1])
    rows.append(jnp.zeros((6, 128), F32))
    acc_ref[ROW_ONE : ROW_ONE + 16] = jnp.concatenate(rows, axis=0) * (1.0 / loss_scale)
    acc_half[576:720] = acc_ref[576:720].astype(BF16)
    for to in range(12, 16):
        scatter_start(to)
    dxcat = dot(jnp.concatenate([w1[0], w1[1]], axis=0), dpre1, 1, 0)
    dxcat = dxcat[:144] + dxcat[144:] + dot(w1[0], dpre1_low, 1, 0)
    dx0 = jnp.zeros((16, 2 * LANES), F32)
    for n, (du, dv) in enumerate(SHIFTS):
        dx0 = dx0 + block_shift(dxcat[n * 16 : n * 16 + 16], -du, -dv)
    x0_ref[...] = dx0
    for g in range(2):
        for p in range(OWN):
            for i4 in range(4):
                base = g * 32 + p * 16 + i4 * 4
                at = g * LANES + p * 256 + i4 * 64
                for pj in range(4):
                    if g == 0:
                        for pi in range(4):
                            fm_ref[base + pi : base + pi + 1, pj * 64 : pj * 64 + 64] = x0_ref[
                                pi * 4 + pj : pi * 4 + pj + 1, at : at + 64
                            ]
                    else:
                        fm_ref[base : base + 4, pj * 64 : pj * 64 + 64] = x0_ref[pj * 4 : pj * 4 + 4, at : at + 64]
    dfm = dot_exact(fm_ref[...], perm, 1)
    dfm1 = jnp.where(valid, dfm[:32], 0.0) * (1.0 / REGIONS)
    dfm2 = jnp.where(valid, dfm[32:], 0.0) * (1.0 / REGIONS)

    def scatter_sum(parts):
        total = acc_ref[pl.ds(pl.multiple_of(chip * 48, 48), 48)]
        for d in range(1, 16):
            source = (chip + 16 - d) % 16
            scatter_arrives(source, parts).wait_recv()
            total = total + parts[source].astype(F32)
        part_b[place] = total

    @pl.when(chip == 15)
    def _():
        scatter_sum(part_a)

    @pl.when(chip != 15)
    def _():
        scatter_sum(part_half)

    for d in range(1, 8):
        column_copy(d).start()

    sum1 = q1_ref[...].reshape(OWN, REGIONS, FRAMES, 256)
    q1 = dfm1.reshape(OWN, 1, FRAMES, 256) / sum1
    rowperm = ones_where(frame_rows((1, ROWS)) == iota((320, ROWS), 0))
    for s in range(REGIONS):
        q2 = (dfm2 / q2_ref[s]).reshape(OWN, 1, FRAMES, 256)
        grad = (e_ref[s].reshape(OWN, REGIONS, FRAMES, 256) * (q1 + q2)).reshape(ROWS, 256).astype(BF16)
        grad_ref[s] = dot(rowperm, grad, 1, 0).astype(BF16)

    def way(n):
        return 1 if n < 2 else -1

    def rep_copy(kind, n):
        d = -way(n) if kind == 2 else way(n)
        of = (rep + 2) % 4 if kind == 0 else (rep + d + 4) % 4
        return pltpu.make_async_remote_copy(
            src_ref=send_ref.at[of, :, pl.ds(n * CHUNK, CHUNK)],
            dst_ref=recv_ref.at[kind, :, pl.ds(n * CHUNK, CHUNK)],
            send_sem=rs.at[n * 3 + kind],
            recv_sem=rr.at[n * 3 + kind],
            device_id=(owner, (rep + d + 4) % 4),
            device_id_type=MESH,
        )

    order = (0, 2, 1, 3)
    for n in order:
        cols = slice(n * CHUNK, (n + 1) * CHUNK)
        product = jnp.zeros((320, CHUNK), F32)
        for s in range(REGIONS):
            pbs = pb_ref[:, s, :, cols].reshape(SEEN * FRAMES, CHUNK)
            product = product + dot(grad_ref[s], pbs, 1, 0)
        product = product.reshape(SIDE, 80, CHUNK)
        rg_ref[:, :, cols] = product
        send_ref[:, :, cols] = product.astype(BF16)
        rep_copy(0, n).start()
        rep_copy(2, n).start()
        if n == 2:
            for d in range(1, 8):
                pltpu.make_async_remote_copy(
                    src_ref=part_b.at[(place + 8 - d) % 8],
                    dst_ref=part_b.at[(place + 8 - d) % 8],
                    send_sem=sb.at[d - 1],
                    recv_sem=rb.at[d - 1],
                    device_id=in_column(d),
                    device_id_type=MESH,
                ).wait_recv()
            total = part_b[0]
            for q in range(1, 8):
                total = total + part_b[q]

            @pl.when(chip == 15)
            def _():
                all_ref[720:768] = total
                for d in range(1, 16):
                    gather_copy(d, chip, True).start()

            @pl.when(chip != 15)
            def _():
                all_half[pl.ds(pl.multiple_of(chip * 48, 48), 48)] = total.astype(BF16)
                for d in range(1, 16):
                    gather_copy(d, chip, False).start()

    for n in order:
        cols = slice(n * CHUNK, (n + 1) * CHUNK)
        of = (rep + way(n) + 4) % 4
        rep_copy(0, n).wait_recv()
        send_ref[of, :, cols] = (rg_ref[of, :, cols] + recv_ref[0, :, cols].astype(F32)).astype(BF16)
        rep_copy(1, n).start()
    for d in range(1, 16):
        source = (chip + 16 - d) % 16

        @pl.when(source == 15)
        def _(d=d, source=source):
            gather_copy(d, source, True).wait_recv()

        @pl.when(source != 15)
        def _(d=d, source=source):
            gather_copy(d, source, False).wait_recv()

    all_ref[0:720] = all_half[0:720].astype(F32)
    table = all_ref[ROW_PS:ROW_ALL]
    found = jnp.zeros((1, 512), F32)
    for p in range(OWN):
        left = dot(ones_where(iota((32, VIDEOS), 1) == 2 * iota((32, VIDEOS), 0) + p), hots_ref[0], 1, 0)
        value = dot_exact(table[:, p * 64 : p * 64 + 64], hots_ref[1])
        found = found + jnp.sum(left * value, axis=0, keepdims=True)
    ps_ref[...] = found
    own = own_ref[...]
    inverse = lax.rsqrt(jnp.sum(own * own, axis=1, keepdims=True) + norm_eps)
    along = jnp.zeros((80, 1), F32)
    for n in order:
        cols = slice(n * CHUNK, (n + 1) * CHUNK)
        rep_copy(2, n).wait_recv()
        rep_copy(1, n).wait_recv()
        total = rg_ref[rep, :, cols] + recv_ref[2, :, cols].astype(F32) + recv_ref[1, :, cols].astype(F32)
        rg_ref[rep, :, cols] = total
        along = along + jnp.sum(own_ref[:, cols] * total, axis=1, keepdims=True)
    back = along * inverse * inverse * inverse
    for n in range(CHUNKS):
        cols = slice(n * CHUNK, (n + 1) * CHUNK)
        result = rg_ref[rep, :, cols] * inverse - own_ref[:, cols] * back
        for q in range(18):
            fg_ref[q, :, cols] = result[q * 4 : q * 4 + 4]

    for copy, arriving in crossings:
        copy.wait_send()
    for m in range(2):
        for r in [ring1[m]] + [ring2[m][du] for du in offsets]:
            for name in ("send_plus", "send_minus", "fwd_plus", "fwd_minus"):
                r[name].wait_send()

    @pl.when(core == kc)
    def _():
        for copy in sent:
            copy.wait_send()

    for d in (1, 2, 3):
        c_copy(d, rep).wait_send()
        for n in range(CHUNKS):
            rep_copy(d - 1, n).wait_send()
    for to in range(16):

        @pl.when(chip != to)
        def _(to=to):
            scatter_copy(to).wait_send()

    @pl.when(chip == 15)
    def _():
        for d in range(1, 16):
            gather_copy(d, chip, True).wait_send()

    @pl.when(chip != 15)
    def _():
        for d in range(1, 16):
            gather_copy(d, chip, False).wait_send()

    for d in range(1, 8):
        column_copy(d).wait_send()


def whole(*args):
    return pl.pallas_call(
        whole_kernel,
        name="training_step",
        out_shape=(
            jax.ShapeDtypeStruct((OWN * REGIONS, 4, WIDTH), F32),
            jax.ShapeDtypeStruct((1, 512), F32),
            jax.ShapeDtypeStruct((ROW_ALL, 128), F32),
        ),
        in_specs=[ANY_SPEC] + [VMEM_SPEC] * 5 + [ANY_SPEC] * 2 + [VMEM_SPEC],
        out_specs=(VMEM_SPEC,) * 3,
        scratch_shapes=[
            pltpu.VMEM((OWN, REGIONS, FRAMES, WIDTH), F32),
            pltpu.VMEM((9, 32, 64), F32),
            pltpu.VMEM((576, C3), F32),
            pltpu.VMEM((OWN, REGIONS, FRAMES, WIDTH), BF16),
            pltpu.VMEM((SEEN, REGIONS, FRAMES, WIDTH), BF16),
            pltpu.VMEM((SIDE, VIDEOS, VIDEOS), F32),
            pltpu.VMEM((2, VIDEOS, 512), BF16),
            pltpu.VMEM((144, 512), F32),
            pltpu.VMEM((512, 256), F32),
            pltpu.VMEM((80, WIDTH), F32),
            pltpu.VMEM((REGIONS, ROWS, 256), F32),
            pltpu.VMEM((ROWS, 256), F32),
            pltpu.VMEM((REGIONS, 32, 256), F32),
            pltpu.VMEM((64, 256), F32),
            pltpu.VMEM((16, 2 * LANES), F32),
            pltpu.VMEM((REGIONS, 320, 256), BF16),
            pltpu.VMEM((ROW_ALL, 128), F32),
            pltpu.VMEM((SIDE, 80, WIDTH), F32),
            pltpu.VMEM((SIDE, 80, WIDTH), BF16),
            pltpu.VMEM((3, 80, WIDTH), BF16),
            pltpu.VMEM((16, 48, 128), F32),
            pltpu.VMEM((8, 48, 128), F32),
            pltpu.VMEM((720, 128), BF16),
            pltpu.VMEM((16, 48, 128), BF16),
            pltpu.VMEM((ROW_ALL, 128), BF16),
        ]
        + [
            pltpu.SemaphoreType.DMA((n,))
            for n in (40, 40, 30, 30, 3, 3, 1, 4, 3, 3, 3 * CHUNKS, 3 * CHUNKS, 16, 16, 7, 7, 15, 15)
        ],
        compiler_params=pltpu.CompilerParams(
            collective_id=0, has_side_effects=True, vmem_limit_bytes=58 * 2**20
        ),
    )(*args)


def outputs_kernel(fg_in, ps_in, all_in, ps_ref, fg_ref, g1_ref, g2_ref, g3_ref, gl_ref):
    fg_ref[...] = fg_in[...]
    ps_ref[...] = ps_in[...]
    g3_ref[...] = all_in[0:ROW_TWO]
    for n in range(18):
        at = ROW_TWO + (n % 9) * 16
        g2_ref[n // 2, (n % 2) * 16 : (n % 2) * 16 + 16, :] = all_in[at : at + 16, (n // 9) * 64 : (n // 9) * 64 + 64]
    for n in range(9):
        g1_ref[n // 3, n % 3] = all_in[ROW_ONE + n : ROW_ONE + n + 1, 0:32]
    gl_ref[...] = all_in[ROW_ONE + 9 : ROW_ONE + 10]


def outputs(fg, ps, summed):
    return pl.pallas_call(
        outputs_kernel,
        name="outputs",
        out_shape=(
            jax.ShapeDtypeStruct((1, 512), F32),
            jax.ShapeDtypeStruct((OWN * REGIONS, 4, WIDTH), F32),
            jax.ShapeDtypeStruct((3, 3, 1, 32), F32),
            jax.ShapeDtypeStruct((9, 32, 64), F32),
            jax.ShapeDtypeStruct((576, C3), F32),
            jax.ShapeDtypeStruct((1, C3), F32),
        ),
        in_specs=[VMEM_SPEC] * 3,
        out_specs=(VMEM_SPEC,) * 6,
    )(fg, ps, summed)


def local(
    features, frame_counts, video_rows, pair_list, pair_cotangent, kernel_one, kernel_two, kernel_three, kernel_last
):
    fg, ps, summed = whole(
        features.transpose(0, 2, 1, 3),
        frame_counts.reshape(1, VIDEOS),
        video_rows.reshape(1, VIDEOS),
        pair_list.T,
        pair_cotangent.reshape(1, 512),
        kernel_one,
        kernel_two.reshape(9, 32, 64),
        kernel_three.reshape(576, C3),
        kernel_last.reshape(1, C3),
    )
    ps, fg, g1, g2, g3, gl = outputs(fg, ps, summed)
    return (
        ps.reshape(512),
        fg.reshape(OWN, REGIONS, 4, WIDTH).transpose(0, 2, 1, 3),
        g1,
        g2.reshape(3, 3, 32, 64),
        g3.reshape(3, 3, 64, C3),
        gl.reshape(C3),
    )


def solution(mesh):
    placed = (P("owner", None, None, None), P(), P(), P("rep", None), P("rep"), P(), P(), P(), P())
    return jax.shard_map(
        local,
        mesh=mesh,
        in_specs=placed,
        out_specs=(P("rep"), P("owner", "rep", None, None), P(), P(), P(), P()),
        check_vma=False,
    )
```

```python
import jax
import jax.numpy as jnp
from jax import lax
from jax.experimental import pallas as pl
from jax.experimental.pallas import tpu as pltpu
from jax.sharding import PartitionSpec as P

MESH = pl.DeviceIdType.MESH
VMEM_SPEC = pl.BlockSpec(memory_space=pltpu.VMEM)
ANY_SPEC = pl.BlockSpec(memory_space=pl.ANY)
F32 = jnp.float32
BF16 = jnp.bfloat16

REGIONS = 9
FRAMES = 16
WIDTH = 2048
VIDEOS = 64
SIDE = 4
OWN = 2
SEEN = 16
ROWS = OWN * REGIONS * FRAMES
LANES = OWN * SEEN * 16

ROW_TWO = 576
ROW_ONE = 720
ROW_PS = 736
ROW_ALL = 768

region_temp = 0.1
loss_scale = 131072.0
norm_eps = 1e-06
C3 = 128


CHUNKS = 4
CHUNK = WIDTH // CHUNKS


def split2(v):
    high = v.astype(BF16)
    return high, (v - high.astype(F32)).astype(BF16)


def dot(a, b, ca, cb):
    return lax.dot_general(a, b, (((ca,), (cb,)), ((), ())), preferred_element_type=F32)


def dot3(a, b, ca, cb):
    (ah, al), (bh, bl) = a, b
    return dot(ah, bh, ca, cb) + dot(ah, bl, ca, cb) + dot(al, bh, ca, cb)


def dot2(a, b, ca, cb):
    return dot(a[0], b, ca, cb) + dot(a[1], b, ca, cb)


def dot_exact(v, chosen, cb=0):
    high = v.astype(BF16)
    rest = v - high.astype(F32)
    mid = rest.astype(BF16)
    low = (rest - mid.astype(F32)).astype(BF16)
    return dot(high, chosen, 1, cb) + dot(mid, chosen, 1, cb) + dot(low, chosen, 1, cb)


def lane_of(shape):
    return lax.broadcasted_iota(jnp.int32, shape, len(shape) - 1)


def moved(v, di, dj):
    if di == 0 and dj == 0:
        return v
    out = pltpu.roll(v, (-(di * 64 + dj)) % LANES, 1)
    lane = lane_of((1, LANES))
    i4, j4 = (lane // 64) % 4, lane % 4
    ok = (i4 + di >= 0) & (i4 + di < 4) & (j4 + dj >= 0) & (j4 + dj < 4)
    return jnp.where(ok, out, 0.0)


def block_shift(v, du, dv):
    return jnp.concatenate([moved(v[:, :LANES], du, dv), moved(v[:, LANES:], dv, du)], axis=1)


def quad_sum(v, stride):
    lane = lane_of((1, LANES))
    for step in (stride, 2 * stride):
        low = (lane // step) % 2 == 0
        v = v + jnp.where(low, pltpu.roll(v, LANES - step, 1), pltpu.roll(v, step, 1))
    return v


def silu_pair(v):
    s = 1.0 / (1.0 + jnp.exp(-v))
    return v * s, s * (1.0 + v * (1.0 - s))


def iota(shape, axis):
    return lax.broadcasted_iota(jnp.int32, shape, axis)


def ones_where(condition):
    return jnp.where(condition, 1.0, 0.0).astype(BF16)


def tap_rows(ti, tj):
    plane = lane_of((1, 512)) // 32
    ei, ej = plane // 4 + ti + 3, plane % 4 + tj + 3
    return ((ei // 4) * 3 + ej // 4) * 16 + (ei % 4) * 4 + ej % 4


SHIFTS = [(du, dv) for du in (-1, 0, 1) for dv in (-1, 0, 1)]
EXT2 = [(1, -1), (0, 0), (1, 0), (0, 1)]


def whole_kernel(
    x_hbm, counts_ref, vrows_ref, pairs_ref, cot_ref, k1_ref, k2_hbm, k3_hbm, kl_ref,
    fg_ref, ps_ref, all_ref,
    x_ref, k2_ref, k3_ref, pa_ref, pb_ref, call_ref, hots_ref, w1_ref, w2_ref, own_ref,
    e_ref, q1_ref, q2_ref, fm_ref, x0_ref, grad_ref, acc_ref, rg_ref, send_ref, recv_ref, part_a, part_b, acc_half, part_half, all_half,
    ssem, rsem, dssem, drsem, csem, crsem, lsem, insem, hs, hr, rs, rr, sa, ra, sb, rb, sc, rc,
):
    owner = lax.axis_index("owner")
    rep = lax.axis_index("rep")
    z, x, core = owner // 8, (owner // 2) % 4, owner % 2
    chip = owner // 2
    place = core * 4 + rep
    other = owner + 1 - 2 * core

    def in_plane(d):
        return (((chip + d) % 16) * 2 + core, rep)

    def in_column(d):
        to = (place + d) % 8
        return (chip * 2 + to // 4, to % 4)

    def shifted(axis, d):
        if axis == 0:
            return z * 8 + ((x + d + 4) % 4) * 2 + core
        return ((z + d + 4) % 4) * 8 + x * 2 + core

    def chip_at(first, du, dv):
        dx, dz = (du, dv) if first == 0 else (dv, du)
        return ((z + dz + 4) % 4) * 4 + (x + dx + 4) % 4

    loads = [pltpu.make_async_copy(x_hbm.at[p], x_ref.at[p], insem.at[p]) for p in range(OWN)]
    loads.append(pltpu.make_async_copy(k2_hbm, k2_ref, insem.at[2]))
    loads.append(pltpu.make_async_copy(k3_hbm, k3_ref, insem.at[3]))
    for load in loads:
        load.start()
    barrier = pltpu.get_barrier_semaphore()
    for axis in (0, 1):
        for d in (1, -1):
            pl.semaphore_signal(barrier, inc=1, device_id=(shifted(axis, d), rep), device_id_type=MESH)
    for d in range(1, 8):
        pl.semaphore_signal(barrier, inc=1, device_id=in_column(d), device_id_type=MESH)

    for p in range(OWN):
        loads[p].wait()
        values = x_ref[p]
        summed = jnp.sum(values * values, axis=-1, keepdims=True) + norm_eps
        pa_ref[p] = (values * lax.rsqrt(summed)).astype(BF16)

    pl.semaphore_wait(barrier, 11)

    kc, kp = rep // 2, rep % 2
    local = pltpu.make_async_copy(pa_ref.at[kp], pb_ref.at[chip], lsem.at[0])

    def own_lanes(to, m):
        return pl.ds(pl.multiple_of(to * 1024 + m * 512, 512), 512)

    def to_other(n, lanes):
        return pltpu.make_async_remote_copy(
            src_ref=pa_ref.at[kp, :, :, lanes],
            dst_ref=pb_ref.at[chip, :, :, lanes],
            send_sem=hs.at[n],
            recv_sem=hr.at[n],
            device_id=(other, rep),
            device_id_type=MESH,
        )

    sent = [to_other(0, own_lanes(1 - core, 0)), to_other(1, own_lanes(1 - core, 1))]
    sent.append(to_other(2, pl.ds(pl.multiple_of(core * 1024, 1024), 1024)))
    got = [to_other(0, own_lanes(core, 0)), to_other(1, own_lanes(core, 1))]
    got.append(to_other(2, pl.ds(pl.multiple_of((1 - core) * 1024, 1024), 1024)))

    def piece(block, m, half):
        if half is None:
            lanes = pl.ds(pl.multiple_of(core * 1024 + m * 512, 512), 512)
        else:
            lanes = pl.ds(pl.multiple_of(core * 1024 + m * 512 + half * 256, 256), 256)
        return pb_ref.at[block, :, :, lanes]

    def ring(m, index, first, du, along):
        base = (m * 5 + index) * 4
        axis = first if along == 0 else 1 - first

        def block(d):
            return chip_at(first, d, 0) if along == 0 else chip_at(first, du, d)

        def copy(slot, source, d, half, prepared=False):
            ref = piece(source, m, half)
            return pltpu.make_async_remote_copy(
                src_ref=pa_ref.at[kp, :, :, own_lanes(core, m)] if prepared else ref,
                dst_ref=ref,
                send_sem=ssem.at[base + slot],
                recv_sem=rsem.at[base + slot],
                device_id=(shifted(axis, d), rep),
                device_id_type=MESH,
            )

        return dict(
            first_plus=copy(0, block(0), 1, None, True),
            first_minus=copy(1, block(0), -1, None, True),
            send_plus=copy(0, block(0), 1, None),
            send_minus=copy(1, block(0), -1, None),
            fwd_plus=copy(2, block(-1), 1, 0),
            fwd_minus=copy(3, block(1), -1, 1),
            from_minus=copy(0, block(-1), 1, None),
            from_plus=copy(1, block(1), -1, None),
            far_a=copy(2, block(2), 1, 0),
            far_b=copy(3, block(2), -1, 1),
            block=block,
        )

    crossings = []

    def cross(m, block):
        n = len(crossings)
        ref = piece(block, m, None)
        copy = pltpu.make_async_remote_copy(
            src_ref=ref,
            dst_ref=ref,
            send_sem=dssem.at[n],
            recv_sem=drsem.at[n],
            device_id=(other, rep),
            device_id_type=MESH,
        )
        copy.start()
        lanes = pl.ds(pl.multiple_of((1 - core) * 1024 + m * 512, 512), 512)
        theirs = pb_ref.at[block, :, :, lanes]
        arriving = pltpu.make_async_remote_copy(
            src_ref=theirs,
            dst_ref=theirs,
            send_sem=dssem.at[n],
            recv_sem=drsem.at[n],
            device_id=(other, rep),
            device_id_type=MESH,
        )
        crossings.append((copy, arriving))

    def c_copy(d, at):
        return pltpu.make_async_remote_copy(
            src_ref=call_ref.at[at],
            dst_ref=call_ref.at[at],
            send_sem=csem.at[d - 1],
            recv_sem=crsem.at[d - 1],
            device_id=(owner, (rep + d) % 4),
            device_id_type=MESH,
        )

    def make_pairs():
        by_row = ones_where(iota((VIDEOS, VIDEOS), 0) == vrows_ref[...])
        videos = iota((VIDEOS, 512), 0)
        row_a = dot(by_row, ones_where(videos == pairs_ref[0:1, :]), 1, 0)
        row_b = dot(by_row, ones_where(videos == pairs_ref[1:2, :]), 1, 0)
        hots_ref[0] = row_a.astype(BF16)
        hots_ref[1] = row_b.astype(BF16)
        call_ref[rep] = dot_exact(row_a * cot_ref[...], row_b.astype(BF16), 1)
        for d in (1, 2, 3):
            c_copy(d, rep).start()

    def make_weights():
        loads[2].wait()
        loads[3].wait()
        k1 = jnp.concatenate([k1_ref[n // 3, n % 3] for n in range(9)], axis=0)
        tiled = dot_exact(k1, ones_where(iota((32, 512), 1) % 32 == iota((32, 512), 0)))
        at = iota((144, 512), 0)
        w1 = jnp.zeros((144, 512), F32)
        for ti in range(3):
            for tj in range(3):
                w1 = jnp.where(at == tap_rows(ti, tj), tiled[ti * 3 + tj : ti * 3 + tj + 1], w1)
        w1_ref[...] = w1
        w2_ref[...] = jnp.zeros((512, 256), F32)
        for ti in range(3):
            for tj in range(3):
                for pi in range(2):
                    for pj in range(2):
                        row = ((pi + ti) * 4 + pj + tj) * 32
                        col = (pi * 2 + pj) * 64
                        w2_ref[row : row + 32, col : col + 64] = k2_ref[ti * 3 + tj]

    def frame_rows(shape):
        n = lane_of(shape)
        return ((n % 16) // 4) * 80 + (n // 144) * 36 + ((n % 144) // 16) * 4 + n % 4

    def make_own():
        chosen = ones_where(frame_rows((1, ROWS)) - rep * 80 == iota((80, ROWS), 0))
        for n in range(4):
            v = x_ref[:, :, :, n * 512 : n * 512 + 512].reshape(ROWS, 512)
            high = v.astype(BF16)
            rest = v - high.astype(F32)
            mid = rest.astype(BF16)
            low = (rest - mid.astype(F32)).astype(BF16)
            own_ref[:, n * 512 : n * 512 + 512] = (
                dot(chosen, high, 1, 0) + dot(chosen, mid, 1, 0) + dot(chosen, low, 1, 0)
            )

    offsets = (0, -1, 1, 2)
    ring1 = [ring(m, 0, m, 0, 0) for m in range(2)]
    ring2 = [{du: ring(m, 1 + n, m, du, 1) for n, du in enumerate(offsets)} for m in range(2)]

    def begin(r):
        r["send_plus"].start()
        r["send_minus"].start()

    @pl.when(core == kc)
    def _():
        sent[0].start()
        sent[1].start()
        for r in (ring1[0], ring1[1], ring2[0][0], ring2[1][0]):
            r["first_plus"].start()
            r["first_minus"].start()
        local.start()
        sent[2].start()

    @pl.when(core != kc)
    def _():
        for m in range(2):
            got[m].wait_recv()
            begin(ring1[m])
            begin(ring2[m][0])

    for d, arrive, forward in ((-1, "from_minus", "fwd_plus"), (1, "from_plus", "fwd_minus")):
        for m in range(2):
            ring1[m][arrive].wait_recv()
            ring1[m][forward].start()
            begin(ring2[m][d])
            cross(m, ring1[m]["block"](d))
    for m in range(2):
        ring1[m]["far_a"].wait_recv()
        ring1[m]["far_b"].wait_recv()
        begin(ring2[m][2])
        cross(m, ring1[m]["block"](2))
    beside = {0: make_pairs, -1: make_weights, 1: make_own}
    for du in offsets:
        for d, arrive, forward in ((-1, "from_minus", "fwd_plus"), (1, "from_plus", "fwd_minus")):
            for m in range(2):
                r = ring2[m][du]
                r[arrive].wait_recv()
                r[forward].start()
                cross(m, r["block"](d))
        if du in beside:
            beside[du]()
    for d in (1, 2, 3):
        c_copy(d, (rep + 4 - d) % 4).wait_recv()
    cots = (call_ref[0] + call_ref[1] + call_ref[2] + call_ref[3]) * loss_scale
    by_row = ones_where(iota((VIDEOS, VIDEOS), 0) == vrows_ref[...])
    lengths = dot(jnp.broadcast_to(counts_ref[...], (8, VIDEOS)).astype(F32).astype(BF16), by_row, 1, 1)
    lengths_half = lengths.astype(BF16)
    at = iota((VIDEOS, LANES), 0)
    lane = iota((1, LANES), 1)
    len_a = dot(lengths_half, ones_where(at == 2 * owner + lane // 256), 1, 0)[0:1]
    pick_b = ones_where(at == 4 * ((lane % 64) // 4) + rep)
    len_b = dot(lengths_half, pick_b, 1, 0)[0:1]
    ok_a = ((lane // 64) % 4 * 4).astype(F32) < len_a
    ok_b = (lane % 4 * 4).astype(F32) < len_b
    inv_a = 1.0 / quad_sum(jnp.where(ok_a, 1.0, 0.0), 64)
    inv_b = 1.0 / quad_sum(jnp.where(ok_b, 1.0, 0.0), 1)
    mine = iota((8, VIDEOS), 1) == 2 * owner + iota((8, VIDEOS), 0) % 2
    mine = ones_where(mine)
    high = cots.astype(BF16)
    rest = cots - high.astype(F32)
    mid = rest.astype(BF16)
    low = (rest - mid.astype(F32)).astype(BF16)
    cot = []
    for cb in (0, 1):
        c_rows = dot(mine, high, 1, cb) + dot(mine, mid, 1, cb) + dot(mine, low, 1, cb)
        spread = dot_exact(c_rows, pick_b)
        cot.append(jnp.where(lane < 256, spread[0:1], spread[1:2]))
    frames_b = iota((1, 256), 1)
    len_vb = dot(lengths_half, ones_where(iota((VIDEOS, 256), 0) == 4 * (frames_b // 16) + rep), 1, 0)[0:1]
    valid_b = (frames_b % 16).astype(F32) < len_vb
    rows_32 = iota((32, VIDEOS), 0)
    len_va = jnp.sum(
        jnp.where(iota((32, VIDEOS), 1) == 2 * owner + rows_32 // 16, jnp.broadcast_to(lengths[0:1], (32, VIDEOS)), 0.0),
        axis=1,
        keepdims=True,
    )
    valid = ((iota((32, 256), 0) % 16).astype(F32) < len_va) & valid_b

    for du in offsets:
        for m in range(2):
            r = ring2[m][du]
            r["far_a"].wait_recv()
            r["far_b"].wait_recv()
            cross(m, r["block"](2))

    @pl.when(core == kc)
    def _():
        local.wait()

    def half_scores(half, s):
        lanes = pl.ds(pl.multiple_of(half * 1024, 1024), 1024)
        left = pa_ref[:, :, :, lanes].reshape(ROWS, 1024)
        return dot(left, pb_ref[:, s, :, lanes].reshape(SEEN * FRAMES, 1024), 1, 1)

    for s in range(REGIONS):
        e_ref[s] = half_scores(core, s)
    for copy, arriving in crossings:
        arriving.wait_recv()

    @pl.when(core != kc)
    def _():
        got[2].wait_recv()

    sum1 = jnp.zeros((ROWS, 256), F32)
    fm2 = jnp.zeros((32, 256), F32)
    for s in range(REGIONS):
        e = jnp.exp((e_ref[s] + half_scores(1 - core, s)) * (1.0 / region_temp))
        e_ref[s] = e
        sum1 = sum1 + e
        sum2 = jnp.sum(e.reshape(OWN, REGIONS, FRAMES, 256), axis=1).reshape(32, 256)
        q2_ref[s] = sum2
        fm2 = fm2 + jnp.log(sum2)
    q1_ref[...] = sum1
    fm1 = jnp.sum(jnp.log(sum1).reshape(OWN, REGIONS, FRAMES, 256), axis=1).reshape(32, 256)
    scale = region_temp / REGIONS
    fm = jnp.concatenate([jnp.where(valid, fm1 * scale, 0.0), jnp.where(valid, fm2 * scale, 0.0)], axis=0)
    spot = iota((256, 256), 0)
    perm = ones_where((spot % 4) * 64 + (spot // 16) * 4 + (spot % 16) // 4 == iota((256, 256), 1))
    fm_ref[...] = dot_exact(fm, perm)
    for g in range(2):
        for p in range(OWN):
            for i4 in range(4):
                base = g * 32 + p * 16 + i4 * 4
                at = g * LANES + p * 256 + i4 * 64
                for pj in range(4):
                    if g == 0:
                        for pi in range(4):
                            x0_ref[pi * 4 + pj : pi * 4 + pj + 1, at : at + 64] = fm_ref[
                                base + pi : base + pi + 1, pj * 64 : pj * 64 + 64
                            ]
                    else:
                        x0_ref[pj * 4 : pj * 4 + 4, at : at + 64] = fm_ref[base : base + 4, pj * 64 : pj * 64 + 64]

    x0 = x0_ref[...]
    xcat = split2(jnp.concatenate([block_shift(x0, du, dv) for du, dv in SHIFTS], axis=0))
    w1 = split2(w1_ref[...])
    stacked = jnp.concatenate([xcat[0], xcat[0], xcat[1]], axis=0)
    h1, ds1 = silu_pair(dot(jnp.concatenate([w1[0], w1[1], w1[0]], axis=0), stacked, 0, 0))
    pooled1 = []
    for qi in range(2):
        for qj in range(2):
            parts = [
                h1[((2 * qi + a) * 4 + 2 * qj + b) * 32 : ((2 * qi + a) * 4 + 2 * qj + b) * 32 + 32]
                for a in range(2)
                for b in range(2)
            ]
            pooled1.append((parts[0] + parts[1] + parts[2] + parts[3]) * 0.25)
    h1cat = split2(
        jnp.concatenate(
            [block_shift(pooled1[qi * 2 + qj], du, dv) for qi, du in EXT2 for qj, dv in EXT2], axis=0
        )
    )
    w2 = split2(w2_ref[...])
    h2, ds2 = silu_pair(dot3(w2, h1cat, 0, 0))
    pooled2 = (h2[0:64] + h2[64:128] + h2[128:192] + h2[192:256]) * 0.25
    h2cat = split2(jnp.concatenate([block_shift(pooled2, du, dv) for du, dv in SHIFTS], axis=0))
    w3 = split2(k3_ref[...])
    both = dot(jnp.concatenate([w3[0], w3[1]], axis=1), h2cat[0], 0, 0)
    h3, ds3 = silu_pair(both[:C3] + both[C3:] + dot(w3[0], h2cat[1], 0, 0))
    kl = jnp.sum(jnp.where(iota((C3, C3), 0) == iota((C3, C3), 1), kl_ref[...], 0.0), axis=1, keepdims=True)
    out = jnp.tanh(jnp.sum(h3 * kl, axis=0, keepdims=True))

    dz = []
    for g in range(2):
        o = out[:, g * LANES : (g + 1) * LANES]
        rows_ok, inv = ((ok_a, inv_a), (ok_b, inv_b))[g]
        weighted = jnp.where(ok_a & ok_b, jnp.exp(o * (1.0 / region_temp)), 0.0)
        row_sums = quad_sum(weighted, 1 if g == 0 else 64) + jnp.where(rows_ok, 0.0, 1.0)
        if g == 0:
            best = jnp.where(rows_ok, region_temp * jnp.log(row_sums), 0.0)
            ps = quad_sum(best, 64) * inv
        dout = cot[g] * inv * weighted / row_sums
        dz.append(dout * (1.0 - o * o))
    dz = jnp.concatenate(dz, axis=1)

    def scatter_copy(to):
        return pltpu.make_async_remote_copy(
            src_ref=acc_ref.at[720:768] if to == 15 else acc_half.at[to * 48 : to * 48 + 48],
            dst_ref=part_a.at[chip] if to == 15 else part_half.at[chip],
            send_sem=sa.at[to],
            recv_sem=ra.at[chip],
            device_id=(to * 2 + core, rep),
            device_id_type=MESH,
        )

    def scatter_start(to):
        @pl.when(chip != to)
        def _():
            scatter_copy(to).start()

    def scatter_arrives(source, parts):
        return pltpu.make_async_remote_copy(
            src_ref=parts.at[source],
            dst_ref=parts.at[source],
            send_sem=sa.at[source],
            recv_sem=ra.at[source],
            device_id=(((chip + 1) % 16) * 2 + core, rep),
            device_id_type=MESH,
        )

    def column_copy(d):
        return pltpu.make_async_remote_copy(
            src_ref=part_b.at[place],
            dst_ref=part_b.at[place],
            send_sem=sb.at[d - 1],
            recv_sem=rb.at[d - 1],
            device_id=in_column(d),
            device_id_type=MESH,
        )

    def gather_copy(d, at, last):
        rows = pl.ds(pl.multiple_of(at * 48, 48), 48)
        block = all_ref.at[720:768] if last else all_half.at[rows]
        return pltpu.make_async_remote_copy(
            src_ref=block,
            dst_ref=block,
            send_sem=sc.at[d - 1],
            recv_sem=rc.at[d - 1],
            device_id=in_plane(d),
            device_id_type=MESH,
        )

    def first(pair):
        return pair[0][:, :LANES], pair[1][:, :LANES]

    lane = lane_of((1, 128))
    row = jnp.where(lane % 4 == rep, jnp.concatenate([ps[:, 0:64], ps[:, 256:320]], axis=1), 0.0)
    at = lax.broadcasted_iota(jnp.int32, (32, 128), 0)
    acc_ref[ROW_PS : ROW_PS + 32] = jnp.where(at == owner, row, 0.0)
    dz_first = jnp.broadcast_to(dz[:, :LANES], (8, LANES))
    gl = dot3(split2(dz_first), split2(h3[:, :LANES]), 1, 1)
    dpre3, dpre3_low = split2(dz * kl * ds3)
    acc_ref[0:576] = dot2(first(h2cat), dpre3[:, :LANES], 1, 1) * (1.0 / loss_scale)
    acc_half[0:576] = acc_ref[0:576].astype(BF16)
    for to in range(12):
        scatter_start(to)
    dh2cat = dot(jnp.concatenate([w3[0], w3[1]], axis=1), jnp.concatenate([dpre3, dpre3], axis=0), 1, 0)
    dh2cat = dh2cat + dot(w3[0], dpre3_low, 1, 0)
    dpool2 = jnp.zeros((64, 2 * LANES), F32)
    for n, (du, dv) in enumerate(SHIFTS):
        dpool2 = dpool2 + block_shift(dh2cat[n * 64 : n * 64 + 64], -du, -dv)
    dpool2 = dpool2 * 0.25
    dpre2, dpre2_low = split2(jnp.concatenate([dpool2, dpool2, dpool2, dpool2], axis=0) * ds2)
    g2 = dot2(first(h1cat), dpre2[:, :LANES], 1, 1)
    for ti in range(3):
        for tj in range(3):
            total = jnp.zeros((32, 64), F32)
            for pi in range(2):
                for pj in range(2):
                    row = ((pi + ti) * 4 + pj + tj) * 32
                    col = (pi * 2 + pj) * 64
                    total = total + g2[row : row + 32, col : col + 64]
            total = total * (1.0 / loss_scale)
            for half in range(2):
                n = (ti * 3 + tj) * 2 + half
                at = ROW_TWO + (n % 9) * 16
                acc_ref[at : at + 16, (n // 9) * 64 : (n // 9) * 64 + 64] = total[half * 16 : half * 16 + 16]
    dh1cat = dot2(w2, dpre2, 1, 0) + dot(w2[0], dpre2_low, 1, 0)
    dpool1 = [jnp.zeros((32, 2 * LANES), F32) for _ in range(4)]
    n = 0
    for qi, du in EXT2:
        for qj, dv in EXT2:
            dpool1[qi * 2 + qj] = dpool1[qi * 2 + qj] + block_shift(dh1cat[n * 32 : n * 32 + 32], -du, -dv)
            n += 1
    dpool1 = [d * 0.25 for d in dpool1]
    dpre1, dpre1_low = split2(
        jnp.concatenate([dpool1[(pi // 2) * 2 + pj // 2] for pi in range(4) for pj in range(4)], axis=0) * ds1
    )
    g1 = dot(jnp.concatenate(first(xcat), axis=0), dpre1[:, :LANES], 1, 1)
    g1 = g1[:144] + g1[144:]
    at = iota((144, 512), 0)
    rows = []
    for ti in range(3):
        for tj in range(3):
            v = jnp.sum(jnp.where(at == tap_rows(ti, tj), g1, 0.0), axis=0, keepdims=True)
            v = v[:, 0:128] + v[:, 128:256] + v[:, 256:384] + v[:, 384:512]
            v = v + pltpu.roll(v, 64, 1)
            rows.append(v + pltpu.roll(v, 32, 1))
    rows.append(gl[0:1])
    rows.append(jnp.zeros((6, 128), F32))
    acc_ref[ROW_ONE : ROW_ONE + 16] = jnp.concatenate(rows, axis=0) * (1.0 / loss_scale)
    acc_half[576:720] = acc_ref[576:720].astype(BF16)
    for to in range(12, 16):
        scatter_start(to)
    dxcat = dot(jnp.concatenate([w1[0], w1[1]], axis=0), dpre1, 1, 0)
    dxcat = dxcat[:144] + dxcat[144:] + dot(w1[0], dpre1_low, 1, 0)
    dx0 = jnp.zeros((16, 2 * LANES), F32)
    for n, (du, dv) in enumerate(SHIFTS):
        dx0 = dx0 + block_shift(dxcat[n * 16 : n * 16 + 16], -du, -dv)
    x0_ref[...] = dx0
    for g in range(2):
        for p in range(OWN):
            for i4 in range(4):
                base = g * 32 + p * 16 + i4 * 4
                at = g * LANES + p * 256 + i4 * 64
                for pj in range(4):
                    if g == 0:
                        for pi in range(4):
                            fm_ref[base + pi : base + pi + 1, pj * 64 : pj * 64 + 64] = x0_ref[
                                pi * 4 + pj : pi * 4 + pj + 1, at : at + 64
                            ]
                    else:
                        fm_ref[base : base + 4, pj * 64 : pj * 64 + 64] = x0_ref[pj * 4 : pj * 4 + 4, at : at + 64]
    dfm = dot_exact(fm_ref[...], perm, 1)
    dfm1 = jnp.where(valid, dfm[:32], 0.0) * (1.0 / REGIONS)
    dfm2 = jnp.where(valid, dfm[32:], 0.0) * (1.0 / REGIONS)

    def scatter_sum(parts):
        total = acc_ref[pl.ds(pl.multiple_of(chip * 48, 48), 48)]
        for d in range(1, 16):
            source = (chip + 16 - d) % 16
            scatter_arrives(source, parts).wait_recv()
            total = total + parts[source].astype(F32)
        part_b[place] = total

    @pl.when(chip == 15)
    def _():
        scatter_sum(part_a)

    @pl.when(chip != 15)
    def _():
        scatter_sum(part_half)

    for d in range(1, 8):
        column_copy(d).start()

    sum1 = q1_ref[...].reshape(OWN, REGIONS, FRAMES, 256)
    q1 = dfm1.reshape(OWN, 1, FRAMES, 256) / sum1
    rowperm = ones_where(frame_rows((1, ROWS)) == iota((320, ROWS), 0))
    for s in range(REGIONS):
        q2 = (dfm2 / q2_ref[s]).reshape(OWN, 1, FRAMES, 256)
        grad = (e_ref[s].reshape(OWN, REGIONS, FRAMES, 256) * (q1 + q2)).reshape(ROWS, 256).astype(BF16)
        grad_ref[s] = dot(rowperm, grad, 1, 0).astype(BF16)

    def way(n):
        return 1 if n < 2 else -1

    def rep_copy(kind, n):
        d = -way(n) if kind == 2 else way(n)
        of = (rep + 2) % 4 if kind == 0 else (rep + d + 4) % 4
        return pltpu.make_async_remote_copy(
            src_ref=send_ref.at[of, :, pl.ds(n * CHUNK, CHUNK)],
            dst_ref=recv_ref.at[kind, :, pl.ds(n * CHUNK, CHUNK)],
            send_sem=rs.at[n * 3 + kind],
            recv_sem=rr.at[n * 3 + kind],
            device_id=(owner, (rep + d + 4) % 4),
            device_id_type=MESH,
        )

    order = (0, 2, 1, 3)
    for n in order:
        cols = slice(n * CHUNK, (n + 1) * CHUNK)
        product = jnp.zeros((320, CHUNK), F32)
        for s in range(REGIONS):
            pbs = pb_ref[:, s, :, cols].reshape(SEEN * FRAMES, CHUNK)
            product = product + dot(grad_ref[s], pbs, 1, 0)
        product = product.reshape(SIDE, 80, CHUNK)
        rg_ref[:, :, cols] = product
        send_ref[:, :, cols] = product.astype(BF16)
        rep_copy(0, n).start()
        rep_copy(2, n).start()
        if n == 2:
            for d in range(1, 8):
                pltpu.make_async_remote_copy(
                    src_ref=part_b.at[(place + 8 - d) % 8],
                    dst_ref=part_b.at[(place + 8 - d) % 8],
                    send_sem=sb.at[d - 1],
                    recv_sem=rb.at[d - 1],
                    device_id=in_column(d),
                    device_id_type=MESH,
                ).wait_recv()
            total = part_b[0]
            for q in range(1, 8):
                total = total + part_b[q]

            @pl.when(chip == 15)
            def _():
                all_ref[720:768] = total
                for d in range(1, 16):
                    gather_copy(d, chip, True).start()

            @pl.when(chip != 15)
            def _():
                all_half[pl.ds(pl.multiple_of(chip * 48, 48), 48)] = total.astype(BF16)
                for d in range(1, 16):
                    gather_copy(d, chip, False).start()

    for n in order:
        cols = slice(n * CHUNK, (n + 1) * CHUNK)
        of = (rep + way(n) + 4) % 4
        rep_copy(0, n).wait_recv()
        send_ref[of, :, cols] = (rg_ref[of, :, cols] + recv_ref[0, :, cols].astype(F32)).astype(BF16)
        rep_copy(1, n).start()
    for d in range(1, 16):
        source = (chip + 16 - d) % 16

        @pl.when(source == 15)
        def _(d=d, source=source):
            gather_copy(d, source, True).wait_recv()

        @pl.when(source != 15)
        def _(d=d, source=source):
            gather_copy(d, source, False).wait_recv()

    all_ref[0:720] = all_half[0:720].astype(F32)
    table = all_ref[ROW_PS:ROW_ALL]
    found = jnp.zeros((1, 512), F32)
    for p in range(OWN):
        left = dot(ones_where(iota((32, VIDEOS), 1) == 2 * iota((32, VIDEOS), 0) + p), hots_ref[0], 1, 0)
        value = dot_exact(table[:, p * 64 : p * 64 + 64], hots_ref[1])
        found = found + jnp.sum(left * value, axis=0, keepdims=True)
    ps_ref[...] = found
    own = own_ref[...]
    inverse = lax.rsqrt(jnp.sum(own * own, axis=1, keepdims=True) + norm_eps)
    along = jnp.zeros((80, 1), F32)
    for n in order:
        cols = slice(n * CHUNK, (n + 1) * CHUNK)
        rep_copy(2, n).wait_recv()
        rep_copy(1, n).wait_recv()
        total = rg_ref[rep, :, cols] + recv_ref[2, :, cols].astype(F32) + recv_ref[1, :, cols].astype(F32)
        rg_ref[rep, :, cols] = total
        along = along + jnp.sum(own_ref[:, cols] * total, axis=1, keepdims=True)
    back = along * inverse * inverse * inverse
    for n in range(CHUNKS):
        cols = slice(n * CHUNK, (n + 1) * CHUNK)
        result = rg_ref[rep, :, cols] * inverse - own_ref[:, cols] * back
        for q in range(18):
            fg_ref[q, :, cols] = result[q * 4 : q * 4 + 4]

    for copy, arriving in crossings:
        copy.wait_send()
    for m in range(2):
        for r in [ring1[m]] + [ring2[m][du] for du in offsets]:
            for name in ("send_plus", "send_minus", "fwd_plus", "fwd_minus"):
                r[name].wait_send()

    @pl.when(core == kc)
    def _():
        for copy in sent:
            copy.wait_send()

    for d in (1, 2, 3):
        c_copy(d, rep).wait_send()
        for n in range(CHUNKS):
            rep_copy(d - 1, n).wait_send()
    for to in range(16):

        @pl.when(chip != to)
        def _(to=to):
            scatter_copy(to).wait_send()

    @pl.when(chip == 15)
    def _():
        for d in range(1, 16):
            gather_copy(d, chip, True).wait_send()

    @pl.when(chip != 15)
    def _():
        for d in range(1, 16):
            gather_copy(d, chip, False).wait_send()

    for d in range(1, 8):
        column_copy(d).wait_send()


def whole(*args):
    return pl.pallas_call(
        whole_kernel,
        name="training_step",
        out_shape=(
            jax.ShapeDtypeStruct((OWN * REGIONS, 4, WIDTH), F32),
            jax.ShapeDtypeStruct((1, 512), F32),
            jax.ShapeDtypeStruct((ROW_ALL, 128), F32),
        ),
        in_specs=[ANY_SPEC] + [VMEM_SPEC] * 5 + [ANY_SPEC] * 2 + [VMEM_SPEC],
        out_specs=(VMEM_SPEC,) * 3,
        scratch_shapes=[
            pltpu.VMEM((OWN, REGIONS, FRAMES, WIDTH), F32),
            pltpu.VMEM((9, 32, 64), F32),
            pltpu.VMEM((576, C3), F32),
            pltpu.VMEM((OWN, REGIONS, FRAMES, WIDTH), BF16),
            pltpu.VMEM((SEEN, REGIONS, FRAMES, WIDTH), BF16),
            pltpu.VMEM((SIDE, VIDEOS, VIDEOS), F32),
            pltpu.VMEM((2, VIDEOS, 512), BF16),
            pltpu.VMEM((144, 512), F32),
            pltpu.VMEM((512, 256), F32),
            pltpu.VMEM((80, WIDTH), F32),
            pltpu.VMEM((REGIONS, ROWS, 256), F32),
            pltpu.VMEM((ROWS, 256), F32),
            pltpu.VMEM((REGIONS, 32, 256), F32),
            pltpu.VMEM((64, 256), F32),
            pltpu.VMEM((16, 2 * LANES), F32),
            pltpu.VMEM((REGIONS, 320, 256), BF16),
            pltpu.VMEM((ROW_ALL, 128), F32),
            pltpu.VMEM((SIDE, 80, WIDTH), F32),
            pltpu.VMEM((SIDE, 80, WIDTH), BF16),
            pltpu.VMEM((3, 80, WIDTH), BF16),
            pltpu.VMEM((16, 48, 128), F32),
            pltpu.VMEM((8, 48, 128), F32),
            pltpu.VMEM((720, 128), BF16),
            pltpu.VMEM((16, 48, 128), BF16),
            pltpu.VMEM((ROW_ALL, 128), BF16),
        ]
        + [
            pltpu.SemaphoreType.DMA((n,))
            for n in (40, 40, 30, 30, 3, 3, 1, 4, 3, 3, 3 * CHUNKS, 3 * CHUNKS, 16, 16, 7, 7, 15, 15)
        ],
        compiler_params=pltpu.CompilerParams(
            collective_id=0, has_side_effects=True, vmem_limit_bytes=58 * 2**20
        ),
    )(*args)


def outputs_kernel(fg_in, ps_in, all_in, ps_ref, fg_ref, g1_ref, g2_ref, g3_ref, gl_ref):
    fg_ref[...] = fg_in[...]
    ps_ref[...] = ps_in[...]
    g3_ref[...] = all_in[0:ROW_TWO]
    for n in range(18):
        at = ROW_TWO + (n % 9) * 16
        g2_ref[n // 2, (n % 2) * 16 : (n % 2) * 16 + 16, :] = all_in[at : at + 16, (n // 9) * 64 : (n // 9) * 64 + 64]
    for n in range(9):
        g1_ref[n // 3, n % 3] = all_in[ROW_ONE + n : ROW_ONE + n + 1, 0:32]
    gl_ref[...] = all_in[ROW_ONE + 9 : ROW_ONE + 10]


def outputs(fg, ps, summed):
    return pl.pallas_call(
        outputs_kernel,
        name="outputs",
        out_shape=(
            jax.ShapeDtypeStruct((1, 512), F32),
            jax.ShapeDtypeStruct((OWN * REGIONS, 4, WIDTH), F32),
            jax.ShapeDtypeStruct((3, 3, 1, 32), F32),
            jax.ShapeDtypeStruct((9, 32, 64), F32),
            jax.ShapeDtypeStruct((576, C3), F32),
            jax.ShapeDtypeStruct((1, C3), F32),
        ),
        in_specs=[VMEM_SPEC] * 3,
        out_specs=(VMEM_SPEC,) * 6,
    )(fg, ps, summed)


def local(
    features, frame_counts, video_rows, pair_list, pair_cotangent, kernel_one, kernel_two, kernel_three, kernel_last
):
    fg, ps, summed = whole(
        features.transpose(0, 2, 1, 3),
        frame_counts.reshape(1, VIDEOS),
        video_rows.reshape(1, VIDEOS),
        pair_list.T,
        pair_cotangent.reshape(1, 512),
        kernel_one,
        kernel_two.reshape(9, 32, 64),
        kernel_three.reshape(576, C3),
        kernel_last.reshape(1, C3),
    )
    ps, fg, g1, g2, g3, gl = outputs(fg, ps, summed)
    return (
        ps.reshape(512),
        fg.reshape(OWN, REGIONS, 4, WIDTH).transpose(0, 2, 1, 3),
        g1,
        g2.reshape(3, 3, 32, 64),
        g3.reshape(3, 3, 64, C3),
        gl.reshape(C3),
    )


def solution(mesh):
    placed = (P("owner", None, None, None), P(), P(), P("rep", None), P("rep"), P(), P(), P(), P())
    return jax.shard_map(
        local,
        mesh=mesh,
        in_specs=placed,
        out_specs=(P("rep"), P("owner", "rep", None, None), P(), P(), P(), P()),
        check_vma=False,
    )
```
